32 devices in a mesh: tp: 8 (over y, x, core), dp: 4 (over z).
Axes of the slice: x: 2, y: 2, z: 4, core: 2. Of those that a mesh axis runs over, the one named last changes fastest.
Arguments:
- block_input: bfloat16 [8192, 1024], P(('tp', 'dp')), may hold values from -6 to 6
- doc_starts: int32 [8192], P('tp'), may hold values from 0 to 1, as said below
- first_gain: bfloat16 [1024], replicated, may hold values from 0.099609375 to 1.8984375
- branch_weight: bfloat16 [1024, 1536], P(None, 'dp'), may hold values from -0.1875 to 0.1875
- lru_weight: bfloat16 [1024, 1536], P(None, 'dp'), may hold values from -0.1875 to 0.1875
- filter_taps: bfloat16 [4, 1536], P(None, 'dp'), may hold values from -3 to 3
- rate_gate: bfloat16 [6, 256, 256], replicated, may hold values from -0.375 to 0.375
- input_gate: bfloat16 [6, 256, 256], replicated, may hold values from -0.375 to 0.375
- rate_bias: bfloat16 [1536], replicated, may hold values from -3 to 3
- input_bias: bfloat16 [1536], replicated, may hold values from -3 to 3
- decay_logit: bfloat16 [1536], P('dp'), may hold values from 1.5 to 7.5
- out_weight: bfloat16 [1536, 1024], P('dp'), may hold values from -0.625 to 0.625
- second_gain: bfloat16 [1024], replicated, may hold values from 0.099609375 to 1.8984375
- feed_gate: bfloat16 [1024, 3072], P(None, 'dp'), may hold values from -0.1875 to 0.1875
- feed_up: bfloat16 [1024, 3072], P(None, 'dp'), may hold values from -0.1875 to 0.1875
- feed_down: bfloat16 [3072, 1024], P('dp'), may hold values from -0.21875 to 0.21875
- cotangent: bfloat16 [8192, 1024], P(('tp', 'dp')), may hold values from -12 to 12
Outputs:
- block_output: float32 [8192, 1024], P(('tp', 'dp'))
- input_grad: float32 [8192, 1024], P(('tp', 'dp'))
- first_gain_grad: float32 [1024], replicated
- branch_weight_grad: float32 [1024, 1536], P(None, 'dp')
- lru_weight_grad: float32 [1024, 1536], P(None, 'dp')
- filter_taps_grad: float32 [4, 1536], P(None, 'dp')
- rate_gate_grad: float32 [6, 256, 256], replicated
- input_gate_grad: float32 [6, 256, 256], replicated
- rate_bias_grad: float32 [1536], replicated
- input_bias_grad: float32 [1536], replicated
- decay_logit_grad: float32 [1536], P('dp')
- out_weight_grad: float32 [1536, 1024], P('dp')
- second_gain_grad: float32 [1024], replicated
- feed_gate_grad: float32 [1024, 3072], P(None, 'dp')
- feed_up_grad: float32 [1024, 3072], P(None, 'dp')
- feed_down_grad: float32 [3072, 1024], P('dp')
The draws below stay inside these ranges and needn't reach their ends.
Inputs may be any that keep to these rules, and one draw needn't show every extreme that they name: `doc_starts`: tokens form rows of 1024; the first token of every row is 1, and elsewhere a 1 marks a document's first token.
All inputs are finite; a program needn't handle non-finite values.
Results may differ from the reference program's by a relative error of at most 0.018.
Values may be sent and summed in bfloat16 or wider, within the bound.
A program may use at most 192 MiB of HBM per device.

```python
import jax
import jax.numpy as jnp
from jax import lax

D = 1024
LRU = 1536
FF = 3072
CONV = 4
BW = 256
ROW_LEN = 1024
HEADS = 6
TOKENS = 8192


def draw_doc_starts(key, part):
    key = jax.random.fold_in(key, 7)
    rate_key, pick_key = jax.random.split(key)
    row_count = TOKENS // ROW_LEN
    level = jax.random.randint(rate_key, (row_count, 1), 1, 8)
    bound = jnp.power(2, level)
    picks = jax.random.randint(pick_key, (row_count, ROW_LEN), 0, 2048)
    first = (jnp.arange(ROW_LEN) == 0)[None, :]
    return jnp.where(first | (picks < bound), 1, 0).astype(jnp.int32).reshape(TOKENS)


def draw_cotangent(key, part):
    key = jax.random.fold_in(key, 11)
    row_count = TOKENS // ROW_LEN
    place = jnp.arange(row_count, dtype=jnp.float32) / float(max(row_count - 1, 1))
    values = jnp.clip(jax.random.normal(key, (row_count, ROW_LEN, D), jnp.float32), -4.0, 4.0)
    factor = jnp.power(3.0, place)
    return (values * factor[:, None, None]).reshape(TOKENS, D).astype(jnp.bfloat16)


def block_levels(own_key, shape, cuts, smallest, largest):
    loudness = 1.0
    for position, blocks in cuts:
        heights = jax.random.uniform(jax.random.fold_in(jax.random.fold_in(own_key, 6), position), (blocks,), jnp.float32, smallest / len(cuts), largest / len(cuts))
        loudness = loudness * jnp.repeat(jnp.exp(heights), shape[position] // blocks).reshape((-1,) + (1,) * (len(shape) - 1 - position))
    return loudness


def scatter_about(rng, extent, spread, most, cuts=(), kind=jnp.bfloat16):
    drawn = spread * jax.random.normal(rng, extent, jnp.float32)
    if cuts:
        drawn = drawn * block_levels(rng, extent, cuts, -0.22, 0.18)
    return jnp.clip(drawn, -most, most).astype(kind)


def setup_inputs(seed: int = 0) -> dict:
    key_list = jax.random.split(jax.random.key(seed), 18)
    block_input = scatter_about(key_list[0], (TOKENS, D), 1.0, 6.0, ((0, 32),))
    doc_starts = draw_doc_starts(jax.random.fold_in(key_list[17], 71), 0)
    first_gain = jnp.clip(1.0 + 0.18 * jax.random.normal(key_list[2], (D,), jnp.float32), 0.099609375, 1.8984375).astype(jnp.bfloat16)
    branch_weight = scatter_about(key_list[3], (D, LRU), D ** -0.5, 0.1875, ((1, 4),))
    lru_weight = scatter_about(key_list[4], (D, LRU), D ** -0.5, 0.1875, ((1, 4),))
    filter_taps = scatter_about(key_list[5], (CONV, LRU), CONV ** -0.5, 3.0, ((1, 4),))
    rate_gate = scatter_about(key_list[6], (HEADS, BW, BW), BW ** -0.5, 0.375)
    input_gate = scatter_about(key_list[7], (HEADS, BW, BW), BW ** -0.5, 0.375)
    rate_bias = scatter_about(key_list[8], (LRU,), 1.0, 3.0)
    input_bias = scatter_about(key_list[9], (LRU,), 1.0, 3.0)
    decay_logit = jnp.clip(1.5 + 6.0 * jax.random.uniform(key_list[10], (LRU,), jnp.float32) ** block_levels(key_list[10], (LRU,), ((0, 4),), -0.2, 0.2), 1.5, 7.5).astype(jnp.bfloat16)
    out_weight = scatter_about(key_list[11], (LRU, D), (LRU // 16) ** -0.5, 0.625, ((0, 4),))
    second_gain = jnp.clip(1.0 + 0.18 * jax.random.normal(key_list[12], (D,), jnp.float32), 0.099609375, 1.8984375).astype(jnp.bfloat16)
    feed_gate = scatter_about(key_list[13], (D, FF), D ** -0.5, 0.1875, ((1, 4),))
    feed_up = scatter_about(key_list[14], (D, FF), D ** -0.5, 0.1875, ((1, 4),))
    feed_down = scatter_about(key_list[15], (FF, D), (FF // 4) ** -0.5, 0.21875, ((0, 4),))
    cotangent = draw_cotangent(jax.random.fold_in(key_list[17], 71), 0)
    return dict(block_input=block_input, doc_starts=doc_starts, first_gain=first_gain, branch_weight=branch_weight, lru_weight=lru_weight, filter_taps=filter_taps, rate_gate=rate_gate, input_gate=input_gate, rate_bias=rate_bias, input_bias=input_bias, decay_logit=decay_logit, out_weight=out_weight, second_gain=second_gain, feed_gate=feed_gate, feed_up=feed_up, feed_down=feed_down, cotangent=cotangent)


EPS = 1e-06
DECAY_SCALE = 8.0
HIGHEST = lax.Precision.HIGHEST

@jax.custom_vjp
def low(v):
    return lax.optimization_barrier(v.astype(jnp.bfloat16)).astype(jnp.float32)

@jax.custom_vjp
def low_back(v):
    return v

def low_keep(v):
    return (low(v), None)

def low_pass(kept, grad):
    return (grad,)

def back_keep(v):
    return (v, None)

def back_low(kept, grad):
    return (low(grad),)
low.defvjp(low_keep, low_pass)
low_back.defvjp(back_keep, back_low)

def matmul(left, right):
    return jnp.dot(left, right, precision=HIGHEST, preferred_element_type=jnp.float32)

def gelu_fn(value):
    return jax.nn.gelu(value, approximate=True)

def rms_norm(value, gain):
    return value * lax.rsqrt(lax.optimization_barrier(jnp.mean(value * value, axis=-1, keepdims=True)) + EPS) * gain

def delayed(signal, steps):
    if steps == 0:
        return signal
    return jnp.pad(signal, ((steps, 0), (0, 0)))[:signal.shape[0]]

def combine(earlier, later):
    return (earlier[0] * later[0], later[0] * earlier[1] + later[1])

def block_forward(block_input, starts, first_gain, branch_weight, lru_weight, filter_taps, rate_gate, input_gate, rate_bias, input_bias, decay_logit, out_weight, second_gain, feed_gate, feed_up, feed_down):
    first = low(rms_norm(block_input, first_gain))
    branch = low_back(matmul(first, branch_weight))
    lru_in = low_back(matmul(first, lru_weight))
    start_col = starts[:, None]
    keep = 1.0 - start_col
    valid = [jnp.ones_like(keep)]
    for steps in range(1, filter_taps.shape[0]):
        valid.append(valid[-1] * delayed(keep, steps - 1))
    mixed = filter_taps[0] * lru_in
    for steps in range(1, filter_taps.shape[0]):
        mixed = mixed + filter_taps[steps] * delayed(lru_in, steps) * valid[steps]
    convolved = low(mixed)
    length = convolved.shape[0]
    heads_in = low_back(convolved).reshape(length, HEADS, BW)
    rate_logit = jnp.einsum('thi,hio->tho', heads_in, rate_gate, precision=HIGHEST).reshape(length, LRU) + rate_bias
    input_logit = jnp.einsum('thi,hio->tho', heads_in, input_gate, precision=HIGHEST).reshape(length, LRU) + input_bias
    rate_logit = low(low_back(rate_logit))
    input_logit = low(low_back(input_logit))
    decay = jnp.exp(-DECAY_SCALE * jax.nn.sigmoid(rate_logit) * jax.nn.softplus(-decay_logit))
    carry = keep * decay
    scale = (start_col + keep * jnp.sqrt(1.0 - decay * decay)) * jax.nn.sigmoid(input_logit)
    state = lax.associative_scan(combine, (carry, scale * convolved), axis=0)[1]
    product = low(state * gelu_fn(branch))
    recurrent = low_back(matmul(product, out_weight))
    residual = block_input + recurrent
    second = low(rms_norm(residual, second_gain))
    feed_logit = low_back(matmul(second, feed_gate))
    up_branch = low_back(matmul(second, feed_up))
    hidden = low(gelu_fn(feed_logit) * up_branch)
    return residual + matmul(hidden, feed_down)

def reference(block_input, doc_starts, first_gain, branch_weight, lru_weight, filter_taps, rate_gate, input_gate, rate_bias, input_bias, decay_logit, out_weight, second_gain, feed_gate, feed_up, feed_down, cotangent):
    weights = tuple((weight.astype(jnp.float32) for weight in (first_gain, branch_weight, lru_weight, filter_taps, rate_gate, input_gate, rate_bias, input_bias, decay_logit, out_weight, second_gain, feed_gate, feed_up, feed_down)))
    pieces = TOKENS // ROW_LEN

    def one_piece(totals, index):
        begin = (index * ROW_LEN).astype(jnp.int32)
        piece_in = lax.dynamic_slice_in_dim(block_input, begin, ROW_LEN, 0).astype(jnp.float32)
        piece_starts = lax.dynamic_slice_in_dim(doc_starts, begin, ROW_LEN, 0).astype(jnp.float32)
        piece_cot = lax.dynamic_slice_in_dim(cotangent, begin, ROW_LEN, 0).astype(jnp.float32)

        def local_forward(value, *params):
            return block_forward(value, piece_starts, *params)
        result, pullback = jax.vjp(local_forward, piece_in, *weights)
        grads = pullback(piece_cot)
        totals = tuple((total + extra for total, extra in zip(totals, grads[1:])))
        return (totals, (result, grads[0]))
    zeros = tuple((jnp.zeros(weight.shape, jnp.float32) for weight in weights))
    totals, stacked = lax.scan(one_piece, zeros, jnp.arange(pieces, dtype=jnp.int32))
    outputs = stacked[0].reshape(TOKENS, D)
    input_grads = stacked[1].reshape(TOKENS, D)
    g_first, g_branch, g_lru, g_taps, g_rate, g_input, g_rbias, g_ibias, g_decay, g_out, g_second, g_gate, g_up, g_down = totals
    return (outputs, input_grads, g_first, g_branch, g_lru, g_taps, g_rate, g_input, g_rbias, g_ibias, g_decay, g_out, g_second, g_gate, g_up, g_down)
```

```python
import functools
import math

import jax
import jax.numpy as jnp
from jax import lax
from jax.experimental import pallas as pl
from jax.experimental.pallas import tpu as pltpu
from jax.sharding import PartitionSpec as P

EPS = 1e-06
DECAY_SCALE = 8.0
F32 = jnp.float32
BF16 = jnp.bfloat16
MESH = pl.DeviceIdType.MESH
VMEM = pltpu.VMEM
DMA = pltpu.SemaphoreType.DMA
NN = (((1,), (0,)), ((), ()))
NT = (((1,), (1,)), ((), ()))
TN = (((0,), (0,)), ((), ()))
HALO = 16
LANE = 128
GELU_A = math.sqrt(2.0 / math.pi)
GELU_B = 0.044715


def dot(left, right, form):
    return lax.dot_general(left, right, form, preferred_element_type=F32)


def sigmoid(v):
    return 1.0 / (1.0 + jnp.exp(-v))


def softplus(v):
    return jnp.maximum(v, 0.0) + jnp.log1p(jnp.exp(-jnp.abs(v)))


def gelu_both(v):
    square = v * v
    tanh = jnp.tanh(GELU_A * v * (1.0 + GELU_B * square))
    half = 0.5 * (1.0 + tanh)
    slope = half + 0.5 * v * (1.0 - tanh * tanh) * (GELU_A * (1.0 + 3.0 * GELU_B * square))
    return v * half, slope


def gelu_only(v):
    return v * (0.5 * (1.0 + jnp.tanh(GELU_A * v * (1.0 + GELU_B * v * v))))


class Place:
    def __init__(self, nz):
        self.nz = nz
        self.t = lax.axis_index("tp")
        self.z = lax.axis_index("dp")
        self.b = lax.rem(self.t, 8)
        self.core = lax.rem(self.t, 2)
        self.x = lax.rem(self.t // 2, 2)
        self.y = lax.rem(self.t // 4, 2)
        self.chip = self.b // 2

    def flip(self, r):
        t = self.t
        if r & 1:
            t = t + 2 - 4 * self.x
        if r & 2:
            t = t + 4 - 8 * self.y
        return t

    def chip_of(self, r):
        c = self.chip
        if r & 1:
            c = c + 1 - 2 * self.x
        if r & 2:
            c = c + 2 - 4 * self.y
        return c

    def plane(self, r):
        return (self.flip(r), self.z)

    def sibling(self):
        return (self.t + 1 - 2 * self.core, self.z)

    def along(self, d):
        return (self.t, lax.rem(self.z + d, self.nz))

    def z_from(self, d):
        return lax.rem(self.z + self.nz - d, self.nz)


def greet(peers):
    barrier = pltpu.get_barrier_semaphore()
    for peer in peers:
        pl.semaphore_signal(barrier, inc=1, device_id=peer, device_id_type=MESH)
    pl.semaphore_wait(barrier, len(peers))


def remote(src, dst, send, recv, peer):
    return pltpu.make_async_remote_copy(
        src_ref=src, dst_ref=dst, send_sem=send, recv_sem=recv, device_id=peer, device_id_type=MESH
    )


class Sends:
    def __init__(self):
        self.started = []

    def when(self, cond, action):
        if cond is None:
            action()
        else:
            pl.when(cond)(action)

    def go(self, make, cond=None):
        self.when(cond, lambda: make().start())
        self.started.append((cond, make))

    def arrived(self, make, cond=None):
        self.when(cond, lambda: make().wait_recv())

    def sent(self, make):
        make().wait_send()
        self.started = [(cond, other) for cond, other in self.started if other is not make]

    def finish(self):
        for cond, make in self.started:
            self.when(cond, lambda: make().wait_send())


class PlaneGather:
    def __init__(self, me, out, piece, send, recv, at, cond=None, first=None, siblings=True):
        self.me, self.out, self.piece, self.cond, self.siblings = me, out, piece, cond, siblings
        self.send, self.recv, self.at, self.first = send, recv, at, first

    def copy(self, i, src, dst, peer):
        return remote(src, dst, self.send.at[self.at + (i,)], self.recv.at[self.at + (i,)], peer)

    def whole(self, i, r, peer, first=False):
        def make():
            place = self.piece(self.me.chip_of(r), self.me.core, None)
            return self.copy(i, self.first() if first and self.first else place, place, peer)
        return make

    def half(self, i, r, part, peer):
        def make():
            place = self.piece(self.me.chip_of(r), self.me.core, part)
            return self.copy(i, place, place, peer)
        return make

    def begin(self):
        for i, r in ((0, 1), (1, 2)):
            self.out.go(self.whole(i, 0, self.me.plane(r), True), self.cond)
        if self.siblings:
            self.out.go(self.whole(4, 0, self.me.sibling(), True), self.cond)

    def relay(self):
        me = self.me
        for i, r, part in ((0, 1, 0), (1, 2, 1)):
            self.out.arrived(self.whole(i, r, me.plane(r)), self.cond)
            self.out.go(self.half(2 + i, r, part, me.plane(3 - r)), self.cond)
            if self.siblings:
                self.out.go(self.whole(4 + r, r, me.sibling()), self.cond)

    def far(self):
        for part in (0, 1):
            self.out.arrived(self.half(2 + part, 3, part, self.me.plane(2 - part)), self.cond)
        if self.siblings:
            self.out.go(self.whole(7, 3, self.me.sibling()), self.cond)

    def end(self):
        if not self.siblings:
            return
        me = self.me
        for r in range(4):
            def make(r=r):
                place = self.piece(me.chip_of(r), 1 - me.core, None)
                return self.copy(4 + r, place, place, me.sibling())
            self.out.arrived(make, self.cond)


class PlaneSum:
    def __init__(self, me, out, block, recv, send_sem, recv_sem, at, source=None):
        self.me, self.out, self.block, self.got = me, out, block, recv
        self.send_sem, self.recv_sem, self.at = send_sem, recv_sem, at
        self.source = source or block

    def copy(self, i, src, peer):
        def make():
            return remote(
                src(), self.got(i), self.send_sem.at[self.at + (i,)], self.recv_sem.at[self.at + (i,)], peer
            )
        return make

    def begin(self):
        for half, r in ((0, 1), (1, 2)):
            for i, to in ((1, 3), (0, r)):
                self.out.go(self.copy(2 * half + i, lambda to=to, half=half: self.source(to, half), self.me.plane(r)))

    def wait(self, i):
        self.out.arrived(self.copy(i, lambda: self.got(i), self.me.plane(1)))

    def relay(self):
        for half, r in ((0, 2), (1, 1)):
            self.wait(2 * half + 1)
            mine = self.block(r, half)
            mine[...] = (mine[...].astype(F32) + self.got(2 * half + 1)[...].astype(F32)).astype(BF16)
            self.out.go(self.copy(4 + half, lambda r=r, half=half: self.block(r, half), self.me.plane(r)))

    def total(self, half):
        self.wait(2 * half)
        self.wait(4 + half)
        return self.got(2 * half)[...].astype(F32) + self.got(4 + half)[...].astype(F32)


def rows(i, size):
    return pl.ds(pl.multiple_of(i * size, size), size)


def rms(v, gain):
    return v * lax.rsqrt(jnp.mean(v * v, axis=-1, keepdims=True) + EPS) * gain


def head_lanes(h, width):
    return pl.ds(pl.multiple_of(h * width, width), width)


def tile_scan(a, b, row, back):
    for step in (1, 2, 4):
        if back:
            seen = row < 8 - step
            shift = 8 - step
        else:
            seen = row >= step
            shift = step
        b_before = jnp.where(seen, pltpu.roll(b, shift, 0), 0.0)
        a_before = jnp.where(seen, pltpu.roll(a, shift, 0), 1.0)
        b = b + a * b_before
        a = a * a_before
    return a, b


def forward_kernel(nz, heads, x, vecs, rg, ig, cot, lw, bw, ow, fgate, fup, fdown,
                   o_wl, o_wb, o_wo, o_fb, o_lin, o_br, o_cv, o_rl, o_il, o_st, o_pr, o_y, o_wg,
                   sin, mk, vec, base, rgrad, g2g,
                   wl, wb, wo, f, cots, win, turned, fb, lin, br, cv, rl, il, st, pr, pst, ends, ms, hx,
                   res, s, h, lg, ug, ybuf, sbuf, srecv, sown,
                   lsem, osem, zs, zr, ps, pr_sem, fcs, fcr, qs, qr, vs, vr, es, er, hs, hr, ss, sr, gs, gr):
    me = Place(nz)
    out, feeds = Sends(), Sends()
    tokens, model = x.shape
    lru = wl.shape[1]
    width = lru // heads
    own = lru // nz
    cols = f.shape[1]
    part = cols // (2 * nz)
    piece_rows = model // 8
    chunk = 256
    z = me.z

    window = pl.ds(pl.multiple_of((me.chip // 2) * (4 * part) + lax.rem(me.chip, 2) * LANE, LANE), 256)
    shift = 64 * lax.rem(me.chip, 2)
    mine = rows(z, own)
    local = [
        (fgate.at[:, window], win.at[0]),
        (fup.at[:, window], win.at[1]),
        (lw, wl.at[:, mine]),
        (bw, wb.at[:, mine]),
        (ow, wo.at[mine]),
        (fdown.at[rows(me.chip, 2 * part)], f.at[2, rows(z, 2 * part)]),
        (cot, cots.at[0]),
    ]
    local = [pltpu.make_async_copy(a, b, lsem.at[i]) for i, (a, b) in enumerate(local)]
    for copy in local:
        copy.start()
    greet([me.along(d) for d in range(1, nz)] + [me.plane(r) for r in (1, 2, 3)] + [me.sibling()])

    def vector(d, origin):
        def make():
            place = vec.at[:, rows(origin(), own)]
            return remote(vecs.at[8:16, 0:own], place, vs.at[d - 1], vr.at[d - 1], me.along(d))
        return make

    def halo():
        return remote(x.at[tokens - HALO:tokens], hx, hs.at[0], hr.at[0], me.along(1))

    out.go(halo)
    for d in range(1, nz):
        out.go(vector(d, lambda: z))

    def slot(m, zz, b):
        if m < 2:
            return (wl, wb)[m].at[rows(b, piece_rows), rows(zz, own)]
        if m == 2:
            return wo.at[rows(zz, own), rows(b, LANE)]
        at = pl.ds(pl.multiple_of(zz * (2 * part) + me.core * part, part), part)
        return f.at[0:2, at] if m == 3 else f.at[2, at]

    def source(m):
        if m < 2:
            return (lw, bw)[m].at[rows(me.b, piece_rows)]
        if m == 2:
            return ow.at[:, rows(me.b, LANE)]
        if m == 3:
            return turned.at[:, pl.ds(pl.multiple_of(shift + me.core * part, 32), part)]
        return fdown.at[pl.ds(pl.multiple_of(me.chip * (2 * part) + me.core * part, part), part)]

    def origin(hop, right):
        return z - 1 - hop if right else z + 1 + hop

    def has(hop, right):
        return z - 1 - hop >= 0 if right else z + 1 + hop < nz

    def along(m, hop, right, from_me):
        def make():
            step = 1 if right else -1
            zz = z - step * hop if from_me else origin(hop, right)
            place = slot(m, zz, me.b)
            src = source(m) if from_me and hop == 0 else place
            at = (m, hop, int(right))
            peer = (me.t, z + step if from_me else z)
            return remote(src, place, zs.at[at], zr.at[at], peer)
        return make

    def z_begin(m, hop=0):
        for right in (True, False):
            there = z + 1 < nz if right else z >= 1
            if hop:
                there = jnp.logical_and(there, has(hop - 1, right))
            (out if m < 3 else feeds).go(along(m, hop, right, True), there)

    gathers = {}
    for m in range(3):
        for hop in range(nz - 1):
            for right in (True, False):
                def place(chip, core, half, m=m, hop=hop, right=right):
                    zz, b = origin(hop, right), 2 * chip + core
                    if half is None:
                        return slot(m, zz, b)
                    if m < 2:
                        at = pl.ds(pl.multiple_of(b * piece_rows + half * (piece_rows // 2), piece_rows // 2), piece_rows // 2)
                        return (wl, wb)[m].at[at, rows(zz, own)]
                    at = pl.ds(pl.multiple_of(zz * own + half * (own // 2), own // 2), own // 2)
                    return wo.at[at, rows(b, LANE)]
                gathers[m, hop, right] = PlaneGather(
                    me, out, place, ps, pr_sem, (m, 2 * hop + int(right)), has(hop, right)
                )

    def share(m, hop, right, from_me):
        def make():
            at = (m - 3, 2 * hop + int(right))
            place = slot(m, origin(hop, right), me.b)
            if not from_me:
                other = pl.ds(pl.multiple_of(origin(hop, right) * (2 * part) + (1 - me.core) * part, part), part)
                place = f.at[0:2, other] if m == 3 else f.at[2, other]
            return remote(place, place, fcs.at[at], fcr.at[at], me.sibling())
        return make

    def z_step(m, hop):
        for right in (True, False):
            out.arrived(along(m, hop, right, False), has(hop, right))
        if hop + 1 < nz - 1:
            z_begin(m, hop + 1)
        for right in (True, False):
            if m < 3:
                gathers[m, hop, right].begin()
            else:
                feeds.go(share(m, hop, right, True), has(hop, right))

    def relay(m, hop):
        for right in (True, False):
            gathers[m, hop, right].relay()

    def far(m, hop):
        for right in (True, False):
            gathers[m, hop, right].far()

    def all_of(m):
        for hop in range(nz - 1):
            for right in (True, False):
                gathers[m, hop, right].end()

    cot_half = tokens // 2

    def cot_whole(i, r):
        return lambda: remote(cot, cots.at[r], qs.at[i], qr.at[i], me.plane(r))

    def cot_part(half, r):
        at = pl.ds(half * cot_half, cot_half)
        return lambda: remote(cots.at[r, at], cots.at[3, at], qs.at[2 + half], qr.at[2 + half], me.plane(3 - r))

    z_begin(0)
    for i, r in ((0, 1), (1, 2)):
        out.go(cot_whole(i, r))

    length = nz * tokens
    lane = lax.broadcasted_iota(jnp.int32, (1, length), 1)
    start_row = vecs[4:5, 0:length]
    keep_row = 1.0 - start_row
    valid = keep_row
    lines, later_lines = [start_row, valid], []
    for k in range(1, 4):
        if k > 1:
            valid = valid * jnp.where(lane >= k - 1, pltpu.roll(keep_row, k - 1, 1), 0.0)
            lines.append(valid)
        later_lines.append(jnp.where(lane < length - k, pltpu.roll(valid, length - k, 1), 0.0))
    ms[...] = jnp.concatenate(lines + later_lines + [jnp.zeros_like(start_row)], axis=0)
    mk[...] = jnp.concatenate([ms[:, rows(z, tokens)], jnp.zeros((LANE - 8, tokens), F32)], axis=0).T
    g1, g2 = vecs[0:1, 0:model], vecs[1:2, 0:model]
    fb[HALO:] = rms(x[...].astype(F32), g1).astype(BF16)
    for i in range(2):
        local[i].wait()
        turned[i] = win[i].T
    own_turned = pltpu.make_async_copy(
        turned.at[:, pl.ds(pl.multiple_of(shift, 32), 2 * part)], f.at[0:2, rows(z, 2 * part)], lsem.at[7]
    )
    own_turned.start()
    out.arrived(halo)
    fb[0:HALO] = rms(hx[...].astype(F32), g1).astype(BF16)

    z_step(0, 0)
    z_begin(1)
    z_step(0, 1)
    z_step(1, 0)
    z_begin(2)
    relay(0, 0)
    z_step(0, 2)
    z_step(1, 1)
    z_step(2, 0)
    z_begin(3)
    relay(0, 1)
    relay(1, 0)
    z_step(1, 2)
    z_step(2, 1)
    z_begin(4)
    for i, r in ((0, 1), (1, 2)):
        out.arrived(cot_whole(i, r))
        out.go(cot_part(i, r))
    far(0, 0)
    relay(0, 2)
    relay(1, 1)
    relay(2, 0)
    z_step(2, 2)
    far(0, 1)
    far(0, 2)
    for d in range(1, nz):
        out.arrived(vector(d, lambda: me.z_from(d)))
    vec[:, mine] = vecs[8:16, 0:own]
    for i in range(2, 7):
        local[i].wait()
    all_of(0)

    def lanes(h):
        return head_lanes(h, width)

    def project(h, _):
        lin[h] = dot(fb[...], wl[:, lanes(h)], NN)
        taps = vec[0:4, lanes(h)]
        conv = taps[0:1] * lin[h, HALO:, :]
        for k in range(1, 4):
            conv = conv + taps[k:k + 1] * lin[h, HALO - k:HALO - k + tokens, :] * mk[:, k:k + 1]
        conv = conv.astype(BF16)
        cv[h] = conv
        rl[h] = (dot(conv, rg[h], NN) + vecs[2:3, lanes(h)]).astype(BF16)
        il[h] = (dot(conv, ig[h], NN) + vecs[3:4, lanes(h)]).astype(BF16)
        return 0

    lax.fori_loop(0, heads, project, 0)
    relay(1, 2)
    relay(2, 1)
    far(1, 0)
    far(1, 1)
    relay(2, 2)
    row = lax.broadcasted_iota(jnp.int32, (8, width), 0)

    def scan_head(h, _):
        rate = softplus(-vec[4:5, lanes(h)]) * -DECAY_SCALE

        def tile(i, carried):
            state, factor = carried
            at = rows(i, 16)
            start = mk[at, 0:1]
            keep = 1.0 - start
            decay = jnp.exp(sigmoid(rl[h, at, :].astype(F32)) * rate)
            a = keep * decay
            scale = (start + keep * jnp.sqrt(1.0 - decay * decay)) * sigmoid(il[h, at, :].astype(F32))
            b = scale * cv[h, at, :].astype(F32)
            for t in range(2):
                cum, run = tile_scan(a[8 * t:8 * t + 8], b[8 * t:8 * t + 8], row, False)
                run = run + cum * state
                cum = cum * factor
                here = pl.ds(pl.multiple_of(i * 16 + 8 * t, 8), 8)
                st[h, here, :] = run
                pst[h, here, :] = cum
                state, factor = run[7:8], cum[7:8]
            return state, factor

        state, factor = lax.fori_loop(
            0, tokens // 16, tile, (jnp.zeros((1, width), F32), jnp.ones((1, width), F32))
        )
        ends[0, 0:1, lanes(h)] = state
        ends[0, 1:2, lanes(h)] = factor
        return 0

    lax.fori_loop(0, heads, scan_head, 0)

    def end_copy(d):
        return lambda: remote(ends.at[0], ends.at[d], es.at[d - 1], er.at[d - 1], me.along(d))

    for d in range(1, nz):
        out.go(end_copy(d))
    far(1, 2)
    all_of(1)

    def branch(h, _):
        br[h] = dot(fb[HALO:], wb[:, lanes(h)], NN)
        return 0

    lax.fori_loop(0, heads, branch, 0)
    z_step(3, 0)
    for hop in range(nz - 1):
        far(2, hop)
    for d in range(1, nz):
        out.arrived(end_copy(d))
    incoming = jnp.zeros((1, lru), F32)
    for d in range(nz - 1, 0, -1):
        end = ends[d, 0:1, :] + ends[d, 1:2, :] * incoming
        incoming = jnp.where(d <= z, end, incoming)
    sin[...] = incoming

    def finish(h, _):
        state = st[h] + pst[h] * sin[:, lanes(h)]
        st[h] = state
        pr[:, lanes(h)] = (state * gelu_only(br[h])).astype(BF16)
        return 0

    lax.fori_loop(0, heads, finish, 0)
    z_step(3, 1)
    all_of(2)

    def project_out(j, _):
        at = rows(j, chunk)
        res[:, at] = x[:, at].astype(F32) + dot(pr[...], wo[:, at], NN)
        return 0

    lax.fori_loop(0, model // chunk, project_out, 0)
    s[0:tokens] = rms(res[...], g2).astype(BF16)

    def second_copy(r):
        return lambda: remote(s.at[0:tokens], s.at[r * tokens:(r + 1) * tokens], ss.at[r - 1], sr.at[r - 1], me.plane(r))

    for r in (1, 2, 3):
        out.go(second_copy(r))
    saved = [
        (wl, o_wl), (wb, o_wb), (wo, o_wo), (fb, o_fb), (lin, o_lin), (br, o_br), (cv, o_cv), (rl, o_rl), (il, o_il),
        (st, o_st), (pr, o_pr),
    ]
    saved = [pltpu.make_async_copy(a, b, osem.at[i]) for i, (a, b) in enumerate(saved)]
    for copy in saved:
        copy.start()
    z_step(3, 2)
    for hop in range(nz - 1):
        z_step(4, hop)
    for m in (3, 4):
        for hop in range(nz - 1):
            for right in (True, False):
                out.arrived(share(m, hop, right, False), has(hop, right))
    own_turned.wait()
    for half, r in ((0, 2), (1, 1)):
        out.arrived(cot_part(half, r))

    def sum_copy(r):
        return lambda: remote(sbuf.at[r - 1], srecv.at[r - 1], gs.at[r - 1], gr.at[r - 1], me.plane(r))

    for r in range(4):
        if r:
            out.arrived(second_copy(r))
        at = pl.ds(r * tokens, tokens)

        def hidden_of(j, _):
            here = rows(j, chunk)
            second = s[at]
            act, slope = gelu_both(dot(second, f[0, here, :], NT))
            up = dot(second, f[1, here, :], NT)
            h[at, here] = (act * up).astype(BF16)
            hg = dot(cots[r], f[2, here, :], NT)
            lg[at, here] = (hg * up * slope).astype(BF16)
            ug[at, here] = (hg * act).astype(BF16)
            return 0

        lax.fori_loop(0, cols // chunk, hidden_of, 0)

        def back_of(j, _):
            here = rows(j, chunk)
            value = dot(lg[at], f[0, :, here], NN) + dot(ug[at], f[1, :, here], NN)
            if r:
                sbuf[r - 1, :, here] = value.astype(BF16)
            else:
                sown[:, here] = value
            return 0

        lax.fori_loop(0, model // chunk, back_of, 0)
        if r:
            out.go(sum_copy(r))

    def out_of(j, _):
        here = rows(j, chunk)
        for r in range(4):
            value = dot(h[r * tokens:(r + 1) * tokens], f[2, :, here], NN)
            if r:
                ybuf[r - 1, :, here] = value.astype(BF16)
            else:
                base[:, here] = res[:, here] + value
        return 0

    lax.fori_loop(0, model // chunk, out_of, 0)
    last = [pltpu.make_async_copy(ybuf, o_y, osem.at[11])]
    last[0].start()

    def wgrads(i, _):
        here = rows(i, chunk)
        for j in range(cols // chunk):
            at = pl.ds(j * chunk, chunk)
            f[0, at, here] = dot(lg[:, j * chunk:(j + 1) * chunk], s[:, here], TN).astype(BF16)
            f[1, at, here] = dot(ug[:, j * chunk:(j + 1) * chunk], s[:, here], TN).astype(BF16)
            other = jnp.concatenate([cots[r, :, here] for r in range(4)], axis=0)
            f[2, at, here] = dot(h[:, j * chunk:(j + 1) * chunk], other, TN).astype(BF16)
        return 0

    feeds.finish()
    lax.fori_loop(0, model // chunk, wgrads, 0)
    last.append(pltpu.make_async_copy(f, o_wg, osem.at[12]))
    last[1].start()
    for r in (1, 2, 3):
        out.arrived(sum_copy(r))
    sg = sown[...]
    for r in range(3):
        sg = sg + srecv[r].astype(F32)
    value = res[...]
    q = sg * g2
    inv = lax.rsqrt(jnp.mean(value * value, axis=-1, keepdims=True) + EPS)
    pull = jnp.mean(q * value, axis=-1, keepdims=True)
    rgrad[...] = cots[0].astype(F32) + (inv * q - value * (inv * inv * inv * pull))
    g2g[...] = jnp.sum(sg * value * inv, axis=0, keepdims=True)
    for copy in saved + last:
        copy.wait()
    out.finish()


def forward(nz, x, vecs, rg, ig, cot, lw, bw, ow, fgate, fup, fdown):
    tokens, model = x.shape
    heads, width = rg.shape[0], rg.shape[1]
    lru = heads * width
    cols = fgate.shape[1]
    k = nz - 1
    vm = pl.BlockSpec(memory_space=VMEM)
    hbm = pl.BlockSpec(memory_space=pl.ANY)
    by_head = (heads, tokens, width)
    saved = [
        ((model, lru), BF16), ((model, lru), BF16), ((lru, model), BF16), ((HALO + tokens, model), BF16),
        ((heads, HALO + tokens, width), F32), (by_head, F32), (by_head, BF16), (by_head, BF16), (by_head, BF16),
        (by_head, F32), ((tokens, lru), BF16), ((3, tokens, model), BF16), ((3, cols, model), BF16),
    ]
    kept = [
        ((1, lru), F32), ((tokens, LANE), F32), ((8, lru), F32), ((tokens, model), F32), ((tokens, model), F32),
        ((1, model), F32),
    ]
    sems = []
    for shape in ((5, k, 2), (3, 2 * k, 8), (2, 2 * k), (4,), (k,), (k,), (1,), (3,), (3,)):
        sems += [DMA(shape)] * 2
    return pl.pallas_call(
        functools.partial(forward_kernel, nz, heads),
        out_shape=tuple(jax.ShapeDtypeStruct(*a) for a in saved + kept),
        in_specs=[vm] * 4 + [hbm] * 7,
        out_specs=[hbm] * len(saved) + [vm] * len(kept),
        scratch_shapes=[
            VMEM((model, lru), BF16), VMEM((model, lru), BF16), VMEM((lru, model), BF16), VMEM((3, cols, model), BF16),
            VMEM((4, tokens, model), BF16), VMEM((2, model, 256), BF16), VMEM((2, 256, model), BF16),
            VMEM((HALO + tokens, model), BF16), VMEM((heads, HALO + tokens, width), F32), VMEM(by_head, F32),
            VMEM(by_head, BF16), VMEM(by_head, BF16), VMEM(by_head, BF16), VMEM(by_head, F32), VMEM((tokens, lru), BF16),
            VMEM(by_head, F32), VMEM((nz, 8, lru), F32), VMEM((8, nz * tokens), F32), VMEM((HALO, model), BF16),
            VMEM((tokens, model), F32), VMEM((4 * tokens, model), BF16), VMEM((4 * tokens, cols), BF16),
            VMEM((4 * tokens, cols), BF16), VMEM((4 * tokens, cols), BF16), VMEM((3, tokens, model), BF16),
            VMEM((3, tokens, model), BF16), VMEM((3, tokens, model), BF16), VMEM((tokens, model), F32),
            DMA((8,)), DMA((len(saved),)),
        ] + sems,
        compiler_params=pltpu.CompilerParams(collective_id=0, has_side_effects=True, vmem_limit_bytes=62 * 2**20),
        name="forward_and_feed",
    )(x, vecs, rg, ig, cot, lw, bw, ow, fgate, fup, fdown)


def backward_kernel(nz, heads, rg, ig, sin, mk, vec, vecs, rgrad, g2g,
                    i_x, i_wl, i_wb, i_wo, i_fb, i_lin, i_br, i_cv, i_rl, i_il, i_st, i_pr, i_base, i_y, i_ffg,
                    wa, fa, ga, bout, igrad, osm, osmz,
                    x, wl, wb, wo, fb, lin, br, cv, rl, il, st, pr, yk, fown,
                    rgb, turned, fl, rlg, ilg, bg, lgr, ends, hal,
                    g, wc, wp, wz, fin, fc, fz, ffin, gt, gc, gp, gz, gfin, sm, smz, yp,
                    lsem, osem, wcs, wcr, wps, wpr, wzs, wzr, was, war, fcs, fcr, fzs, fzr, fas, far,
                    gcs, gcr, gps, gpr, gzs, gzr, gys, gyr, gas, gar, yps, ypr, s1s, s1r, s2s, s2r,
                    es, er, hs, hr):
    me = Place(nz)
    out = Sends()
    core, other, chip, z = me.core, 1 - me.core, me.chip, me.z
    tokens, model = x.shape
    lru = wl.shape[1]
    width = lru // heads
    own = lru // nz
    block = model // 8
    half_rows = block // 2
    part = fc.shape[2]
    k = nz - 1

    loads = dict(
        pr=(i_pr, pr), wo=(i_wo, wo), br=(i_br, br), st=(i_st, st), fown=(i_ffg.at[:, :, core], fown),
        y0=(i_y.at[1, 0:tokens // 2], yk.at[0]), y1=(i_y.at[0, tokens // 2:tokens], yk.at[1]),
        rl=(i_rl, rl), fb=(i_fb, fb), wb=(i_wb, wb), cv=(i_cv, cv), il=(i_il, il), lin=(i_lin, lin), wl=(i_wl, wl),
        x=(i_x, x), base=(i_base, bout),
    )
    loads = {name: pltpu.make_async_copy(a, b, lsem.at[i]) for i, (name, (a, b)) in enumerate(loads.items())}
    for copy in loads.values():
        copy.start()

    def need(*names):
        for name in names:
            loads[name].wait()

    greet([me.along(d) for d in range(1, nz)] + [me.plane(r) for r in (1, 2, 3)] + [me.sibling()])


    def lanes(h):
        return head_lanes(h, width)

    def feed_core():
        return remote(i_ffg.at[:, :, other], fc, fcs.at[0], fcr.at[0], me.sibling())

    def feed_along(d):
        return lambda: remote(fc.at[:, me.along(d)[1]], fz.at[d - 1], fzs.at[d - 1], fzr.at[d - 1], me.along(d))

    def feed_sum():
        out.arrived(feed_core)
        need("fown")

        def add(i, _):
            for m in range(3):
                fc[m, i] = (fc[m, i].astype(F32) + fown[m, i].astype(F32)).astype(BF16)
            return 0

        lax.fori_loop(0, nz, add, 0)
        for d in range(1, nz):
            out.go(feed_along(d))

    def feed_place(c, kk, half):
        at = pl.multiple_of((2 * c + kk) * part, part)
        if half is None:
            return fa.at[:, pl.ds(at, part)]
        return fa.at[:, pl.ds(pl.multiple_of(at + half * (part // 2), part // 2), part // 2)]

    feed_gather = PlaneGather(me, out, feed_place, fas, far, (), None, first=lambda: ffin)
    feed_own = pltpu.make_async_copy(ffin, feed_place(chip, core, None), osem.at[3])

    def feed_total():
        for d in range(1, nz):
            out.arrived(feed_along(d))
        for m in range(3):
            total = fc[m, z].astype(F32)
            for d in range(k):
                total = total + fz[d, m].astype(F32)
            ffin[m] = total.astype(BF16)
        feed_gather.begin()
        feed_own.start()

    def y_half(r, half):
        return i_y.at[r - 1, pl.ds(half * (tokens // 2), tokens // 2)]

    y_sum = PlaneSum(me, out, lambda r, half: yk.at[half], lambda i: yp.at[i], yps, ypr, (), source=y_half)

    slot_of = {2: 0, 1: 1, 0: 0}

    def core_of(m):
        at = pl.ds(pl.multiple_of(other * (model // 2), model // 2), model // 2)
        return lambda: remote(g.at[slot_of[m], at], wc.at[m], wcs.at[m], wcr.at[m], me.sibling())

    core_copies = [core_of(m) for m in range(3)]

    def block_of(m, r, half=None):
        start = me.chip_of(r) * block
        if half is None:
            return wc.at[m, pl.ds(pl.multiple_of(start, block), block)]
        return wc.at[m, pl.ds(pl.multiple_of(start + half * half_rows, half_rows), half_rows)]

    sums = [
        PlaneSum(me, out, lambda r, half, m=m: block_of(m, r, half), lambda i, m=m: wp.at[m, i], wps, wpr, (m,))
        for m in range(3)
    ]

    def core_sum(m):
        out.arrived(core_copies[m])

        def add(c, _):
            at = rows(c, block)
            mine = pl.ds(pl.multiple_of(core * (model // 2) + c * block, block), block)
            wc[m, at, :] = (wc[m, at, :].astype(F32) + g[slot_of[m], mine, :].astype(F32)).astype(BF16)
            return 0

        lax.fori_loop(0, 4, add, 0)
        sums[m].begin()

    def z_copy(m, d):
        return lambda: remote(
            wc.at[m, rows(chip, block), rows(me.along(d)[1], own)], wz.at[m, d - 1], wzs.at[m, d - 1], wzr.at[m, d - 1], me.along(d)
        )

    def plane_total(m):
        for half in range(2):
            at = pl.ds(pl.multiple_of(chip * block + half * half_rows, half_rows), half_rows)
            wc[m, at, :] = (wc[m, at, :].astype(F32) + sums[m].total(half)).astype(BF16)
        for d in range(1, nz):
            out.go(z_copy(m, d))

    def weight_place(m):
        def place(c, kk, half):
            start = (4 * kk + c) * block
            if half is None:
                return wa.at[m, pl.ds(pl.multiple_of(start, block), block)]
            return wa.at[m, pl.ds(pl.multiple_of(start + half * half_rows, half_rows), half_rows)]
        return place

    gathers = [PlaneGather(me, out, weight_place(m), was, war, (m,), None, first=lambda m=m: fin.at[m]) for m in range(3)]
    own_copies = [pltpu.make_async_copy(fin.at[m], weight_place(m)(chip, core, None), osem.at[m]) for m in range(3)]

    def z_total(m):
        for d in range(1, nz):
            out.arrived(z_copy(m, d))
        total = wc[m, rows(chip, block), rows(z, own)].astype(F32)
        for d in range(k):
            total = total + wz[m, d].astype(F32)
        fin[m] = total.astype(BF16)
        gathers[m].begin()
        own_copies[m].start()

    gate_half = gt.shape[0] // 2
    gate_block = gt.shape[0] // 8
    gate_part = gate_block // nz

    def gate_core():
        at = pl.ds(pl.multiple_of(other * gate_half, gate_half), gate_half)
        return remote(gt.at[at], gc, gcs.at[0], gcr.at[0], me.sibling())

    def gate_rows(r, half):
        return gc.at[pl.ds(pl.multiple_of(me.chip_of(r) * gate_block + half * (gate_block // 2), gate_block // 2), gate_block // 2)]

    gate_sum = PlaneSum(me, out, gate_rows, lambda i: gp.at[i], gps, gpr, ())

    def gate_core_sum():
        out.arrived(gate_core)
        mine = pl.ds(pl.multiple_of(core * gate_half, gate_half), gate_half)
        gc[...] = (gc[...].astype(F32) + gt[mine, :].astype(F32)).astype(BF16)
        gate_sum.begin()

    def gate_cut(i):
        return pl.ds(pl.multiple_of(chip * gate_block + i * gate_part, gate_part), gate_part)

    def gate_along(d):
        return lambda: remote(gc.at[gate_cut(me.along(d)[1])], gz.at[d - 1], gzs.at[d - 1], gzr.at[d - 1], me.along(d))

    def gate_back(d, origin):
        return lambda: remote(
            gfin.at[rows(origin(), gate_part)], gfin.at[rows(origin(), gate_part)], gys.at[d - 1], gyr.at[d - 1], me.along(d)
        )

    def gate_total():
        for half in range(2):
            at = pl.ds(pl.multiple_of(chip * gate_block + half * (gate_block // 2), gate_block // 2), gate_block // 2)
            gc[at, :] = (gc[at, :].astype(F32) + gate_sum.total(half)).astype(BF16)
        for d in range(1, nz):
            out.go(gate_along(d))

    def gate_z_total():
        for d in range(1, nz):
            out.arrived(gate_along(d))
        total = gc[gate_cut(z), :].astype(F32)
        for d in range(k):
            total = total + gz[d].astype(F32)
        gfin[rows(z, gate_part), :] = total.astype(BF16)
        for d in range(1, nz):
            out.go(gate_back(d, lambda: z))

    def gate_place(c, kk, half):
        start = (4 * kk + c) * gate_block
        if half is None:
            return ga.at[pl.ds(pl.multiple_of(start, gate_block), gate_block)]
        return ga.at[pl.ds(pl.multiple_of(start + half * (gate_block // 2), gate_block // 2), gate_block // 2)]

    gate_gather = PlaneGather(me, out, gate_place, gas, gar, (), None, first=lambda: gfin)
    gate_own = pltpu.make_async_copy(gfin, gate_place(chip, core, None), osem.at[4])

    def gate_spread():
        for d in range(1, nz):
            out.arrived(gate_back(d, lambda: me.z_from(d)))
        gate_gather.begin()
        gate_own.start()

    def small_copy(i):
        peer = (me.sibling(), me.plane(1), me.plane(2))[i]
        return lambda: remote(sm.at[2 * i], sm.at[2 * i + 1], s1s.at[i], s1r.at[i], peer)

    def small_step(i):
        out.arrived(small_copy(i))
        sm[2 * i + 2] = sm[2 * i] + sm[2 * i + 1]
        if i < 2:
            out.go(small_copy(i + 1))
        else:
            smz[z] = sm[6]
            for d in range(1, nz):
                out.go(small_along(d, lambda: z))

    def small_along(d, origin):
        return lambda: remote(sm.at[6], smz.at[origin()], s2s.at[d - 1], s2r.at[d - 1], me.along(d))


    out.go(feed_core)
    y_sum.begin()
    small = sm.at[0]
    small[...] = jnp.zeros(small.shape, F32)
    small[8:9, 0:model] = g2g[...]
    row = lax.broadcasted_iota(jnp.int32, (8, width), 0)
    rgb[...] = rgrad[...].astype(BF16)
    turned[...] = rgb[...].T
    need("pr")

    def wgrad(slot, right):
        def body(h, _):
            g[slot, :, lanes(h)] = dot(turned[...], right[:, lanes(h)], NN).astype(BF16)
            return 0

        lax.fori_loop(0, heads, body, 0)

    wgrad(0, pr)
    out.go(core_copies[2])
    need("wo", "br", "st")

    def branch_back(h, _):
        pg = dot(rgb[...], wo[lanes(h), :], NT)
        act, slope = gelu_both(br[h])
        bg[:, lanes(h)] = (pg * st[h] * slope).astype(BF16)
        fl[h, 0:tokens] = pg * act
        return 0

    lax.fori_loop(0, heads, branch_back, 0)
    need("fb")
    turned[...] = fb[HALO:, :].T
    wgrad(1, bg)
    out.go(core_copies[1])
    feed_sum()
    core_sum(2)
    need("rl")

    def scan_head(h, _):
        rate = softplus(-vec[4:5, lanes(h)]) * -DECAY_SCALE

        def tile(j, carried):
            later, factor = carried
            i = tokens // 16 - 1 - j
            at = rows(i, 16)
            keep = 1.0 - mk[at, 0:1]
            a = keep * jnp.exp(sigmoid(rl[h, at, :].astype(F32)) * rate)
            sgrad = fl[h, at, :]
            b = a * sgrad
            for t in (1, 0):
                cum, run = tile_scan(a[8 * t:8 * t + 8], b[8 * t:8 * t + 8], row, True)
                run = run + cum * later
                cum = cum * factor
                here = pl.ds(pl.multiple_of(i * 16 + 8 * t, 8), 8)
                last = row == 7
                fl[h, here, :] = sgrad[8 * t:8 * t + 8] + jnp.where(last, later, pltpu.roll(run, 7, 0))
                br[h, here, :] = jnp.where(last, factor, pltpu.roll(cum, 7, 0))
                later, factor = run[0:1], cum[0:1]
            return later, factor

        later, factor = lax.fori_loop(
            0, tokens // 16, tile, (jnp.zeros((1, width), F32), jnp.ones((1, width), F32))
        )
        ends[0, 0:1, lanes(h)] = later
        ends[0, 1:2, lanes(h)] = factor
        return 0

    lax.fori_loop(0, heads, scan_head, 0)

    def end_copy(d):
        return lambda: remote(ends.at[0], ends.at[d], es.at[d - 1], er.at[d - 1], me.along(nz - d))

    for d in range(1, nz):
        out.go(end_copy(d))
    core_sum(1)
    need("wb")
    igrad[...] = jnp.zeros(igrad.shape, F32)

    def first_back(left, right):
        def body(j, _):
            at = rows(j, 256)
            igrad[:, at] += dot(left[...], right[at, :], NT)
            return 0

        lax.fori_loop(0, model // 256, body, 0)

    first_back(bg, wb)
    need("y0", "y1")
    y_sum.relay()
    sums[2].relay()
    for d in range(1, nz):
        out.arrived(end_copy(d))
    incoming = jnp.zeros((1, lru), F32)
    for d in range(nz - 1, 0, -1):
        end = ends[d, 0:1, :] + ends[d, 1:2, :] * incoming
        incoming = jnp.where(d + z < nz, end, incoming)
    sm[1, 0:1, :] = incoming
    need("cv", "il")

    def terms(h, _):
        raw = vec[4:5, lanes(h)]
        soft = softplus(-raw)
        later = sm[1, 0:1, lanes(h)]

        def tile(i, carried):
            before, decays, rates, inputs = carried
            at = rows(i, 16)
            start = mk[at, 0:1]
            keep = 1.0 - start
            flow = fl[h, at, :] + br[h, at, :] * later
            state = st[h, at, :]
            first = lax.broadcasted_iota(jnp.int32, (16, width), 0) == 0
            earlier = jnp.where(first, before, pltpu.roll(state, 1, 0))
            sig = sigmoid(rl[h, at, :].astype(F32))
            gate = sigmoid(il[h, at, :].astype(F32))
            decay = jnp.exp(sig * (soft * -DECAY_SCALE))
            root = jnp.sqrt(1.0 - decay * decay)
            level = start + keep * root
            conv = cv[h, at, :].astype(F32)
            to_scale = flow * conv
            to_decay = keep * (flow * earlier - to_scale * gate * (decay / root))
            to_power = to_decay * decay * sig
            rate_grad = (to_power * (1.0 - sig) * (soft * -DECAY_SCALE)).astype(BF16)
            input_grad = (to_scale * level * gate * (1.0 - gate)).astype(BF16)
            rlg[h, at, :] = rate_grad
            ilg[h, at, :] = input_grad
            fl[h, at, :] = flow * level * gate
            rates = rates + rate_grad.astype(F32)
            inputs = inputs + input_grad.astype(F32)
            return state[15:16], decays + to_power, rates, inputs

        zero = jnp.zeros((16, width), F32)
        _, decays, rates, inputs = lax.fori_loop(0, tokens // 16, tile, (sin[:, lanes(h)], zero, zero, zero))
        small[4:5, lanes(h)] = jnp.sum(decays, axis=0, keepdims=True) * (DECAY_SCALE * sigmoid(-raw))
        small[5:6, lanes(h)] = jnp.sum(rates, axis=0, keepdims=True)
        small[6:7, lanes(h)] = jnp.sum(inputs, axis=0, keepdims=True)
        rate_out, input_out = rlg[h], ilg[h]
        gt[rows(h, width), :] = dot(cv[h], rate_out, TN).astype(BF16)
        gt[rows(heads + h, width), :] = dot(cv[h], input_out, TN).astype(BF16)
        path = (dot(rate_out, rg[h], NT) + dot(input_out, ig[h], NT)).astype(BF16)
        fl[h, 0:tokens] = fl[h, 0:tokens] + path.astype(F32)
        hal[0, h] = fl[h, 0:8]
        return 0

    lax.fori_loop(0, heads, terms, 0)

    def halo():
        return remote(hal.at[0], hal.at[1], hs.at[0], hr.at[0], me.along(nz - 1))

    out.go(halo)
    out.go(gate_core)
    sums[1].relay()
    plane_total(2)
    need("lin")
    out.sent(core_copies[2])
    out.arrived(halo)

    def filter_back(h, _):
        taps = vec[0:4, lanes(h)]
        fl[h, tokens:tokens + 8] = hal[1, h]
        value = taps[0:1] * fl[h, 0:tokens]
        small[0:1, lanes(h)] = jnp.sum(fl[h, 0:tokens] * lin[h, HALO:], axis=0, keepdims=True)
        for t in range(1, 4):
            value = value + taps[t:t + 1] * (fl[h, t:t + tokens] * mk[:, 3 + t:4 + t])
            small[t:t + 1, lanes(h)] = jnp.sum(
                fl[h, 0:tokens] * (lin[h, HALO - t:HALO - t + tokens] * mk[:, t:t + 1]), axis=0, keepdims=True
            )
        lgr[:, lanes(h)] = value.astype(BF16)
        return 0

    lax.fori_loop(0, heads, filter_back, 0)
    wgrad(0, lgr)
    out.go(core_copies[0])
    gate_core_sum()
    need("wl")
    first_back(lgr, wl)
    core_sum(0)
    need("x")
    value = x[...].astype(F32)
    fgrad = igrad[...]
    q = fgrad * vecs[0:1, 0:model]
    inv = lax.rsqrt(jnp.mean(value * value, axis=-1, keepdims=True) + EPS)
    pull = jnp.mean(q * value, axis=-1, keepdims=True)
    small[7:8, 0:model] = jnp.sum(fgrad * value * inv, axis=0, keepdims=True)
    igrad[...] = rgrad[...] + (inv * q - value * (inv * inv * inv * pull))
    out.go(small_copy(0))
    plane_total(1)
    z_total(2)
    feed_total()
    small_step(0)
    gate_sum.relay()
    need("base")
    for half in range(2):
        at = pl.ds(half * (tokens // 2), tokens // 2)
        bout[at, :] = bout[at, :] + y_sum.total(half)
    sums[0].relay()
    small_step(1)
    gathers[2].relay()
    gate_total()
    z_total(1)
    small_step(2)
    plane_total(0)
    gate_z_total()
    feed_gather.relay()
    gathers[2].far()
    gathers[1].relay()
    z_total(0)
    gate_spread()
    gathers[1].far()
    feed_gather.far()
    gathers[0].relay()
    gate_gather.relay()
    for d in range(1, nz):
        out.arrived(small_along(d, lambda: me.z_from(d)))
    total = smz[0]
    for i in range(1, nz):
        total = total + smz[i]
    osm[...] = total
    osmz[...] = osm[:, rows(z, own)]
    gathers[0].far()
    gate_gather.far()
    for gathered in gathers + [feed_gather, gate_gather]:
        gathered.end()
    for copy in own_copies + [feed_own, gate_own]:
        copy.wait()
    out.finish()


def backward(nz, rg, ig, sin, mk, vec, vecs, rgrad, g2g, x, wl, wb, wo, fb, lin, br, cv, rl, il, st, pr, base, y, ffg):
    tokens, model = x.shape
    heads, width = rg.shape[0], rg.shape[1]
    lru = heads * width
    own = lru // nz
    part = ffg.shape[3]
    k = nz - 1
    block = model // 8
    gate_rows = 2 * lru
    gate_block = gate_rows // 8
    vm = pl.BlockSpec(memory_space=VMEM)
    hbm = pl.BlockSpec(memory_space=pl.ANY)
    by_head = (heads, tokens, width)
    half = tokens // 2
    sems = []
    for shape in (
        (3,), (3, 6), (3, k), (3, 8), (1,), (k,), (8,),
        (1,), (6,), (k,), (k,), (8,), (6,), (3,), (k,), (k,), (1,),
    ):
        sems += [DMA(shape)] * 2
    return pl.pallas_call(
        functools.partial(backward_kernel, nz, heads),
        out_shape=(
            jax.ShapeDtypeStruct((3, model, own), BF16),
            jax.ShapeDtypeStruct((3, 8 * part, model), BF16),
            jax.ShapeDtypeStruct((gate_rows, width), BF16),
            jax.ShapeDtypeStruct((tokens, model), F32),
            jax.ShapeDtypeStruct((tokens, model), F32),
            jax.ShapeDtypeStruct((16, lru), F32),
            jax.ShapeDtypeStruct((16, own), F32),
        ),
        in_specs=[vm] * 8 + [hbm] * 15,
        out_specs=[hbm] * 3 + [vm] * 4,
        scratch_shapes=[
            VMEM((tokens, model), BF16), VMEM((model, lru), BF16), VMEM((model, lru), BF16), VMEM((lru, model), BF16),
            VMEM((HALO + tokens, model), BF16), VMEM((heads, HALO + tokens, width), F32), VMEM(by_head, F32),
            VMEM(by_head, BF16), VMEM(by_head, BF16), VMEM(by_head, BF16), VMEM(by_head, F32), VMEM((tokens, lru), BF16),
            VMEM((2, half, model), BF16), VMEM((3, nz, part, model), BF16),
            VMEM((tokens, model), BF16), VMEM((model, tokens), BF16), VMEM((heads, tokens + 8, width), F32),
            VMEM(by_head, BF16), VMEM(by_head, BF16), VMEM((tokens, lru), BF16), VMEM((tokens, lru), BF16),
            VMEM((nz, 8, lru), F32), VMEM((2, heads, 8, width), F32),
            VMEM((2, model, lru), BF16), VMEM((3, model // 2, lru), BF16), VMEM((3, 6, block // 2, lru), BF16),
            VMEM((3, k, block, own), BF16), VMEM((3, block, own), BF16),
            VMEM((3, nz, part, model), BF16), VMEM((k, 3, part, model), BF16), VMEM((3, part, model), BF16),
            VMEM((gate_rows, width), BF16), VMEM((gate_rows // 2, width), BF16), VMEM((6, gate_block // 2, width), BF16),
            VMEM((k, gate_block // nz, width), BF16), VMEM((gate_block, width), BF16),
            VMEM((7, 16, lru), F32), VMEM((nz, 16, lru), F32), VMEM((6, half, model), BF16),
            DMA((16,)), DMA((5,)),
        ] + sems,
        compiler_params=pltpu.CompilerParams(collective_id=1, has_side_effects=True, vmem_limit_bytes=62 * 2**20),
        name="backward_and_sums",
    )(rg, ig, sin, mk, vec, vecs, rgrad, g2g, x, wl, wb, wo, fb, lin, br, cv, rl, il, st, pr, base, y, ffg)


def results_kernel(wa, fa, ga, bout, igrad, osm, osmz,
                   o_out, o_in, o_g1, o_branch, o_lru, o_taps, o_gates, o_rb, o_ib, o_decay, o_ow, o_g2, o_gate, o_up, o_down):
    model = bout.shape[1]

    @pl.when(pl.program_id(0) == 0)
    def _():
        o_out[...] = bout[...]
        o_in[...] = igrad[...]
        o_taps[...] = osmz[0:4, :]
        o_decay[...] = osmz[4:5, :]
        o_rb[...] = osm[5:6, :]
        o_ib[...] = osm[6:7, :]
        o_g1[...] = osm[7:8, 0:model]
        o_g2[...] = osm[8:9, 0:model]

    o_lru[...] = wa[0].astype(F32)
    o_branch[...] = wa[1].astype(F32)
    o_ow[...] = wa[2].T.astype(F32)
    o_gates[...] = ga[...].astype(F32)
    o_gate[...] = fa[0].T.astype(F32)
    o_up[...] = fa[1].T.astype(F32)
    o_down[...] = fa[2].astype(F32)


def results(wa, fa, ga, bout, igrad, osm, osmz):
    steps = 3
    model, own = wa.shape[1:]
    cols = fa.shape[1]
    gate_rows, width = ga.shape
    lru = osm.shape[1]
    tokens = bout.shape[0]

    def whole(shape):
        return pl.BlockSpec(shape, lambda i: (0,) * len(shape))

    across = pl.BlockSpec((model, own // steps), lambda i: (0, i))
    feed_across = pl.BlockSpec((model, cols // steps), lambda i: (0, i))
    outs = [
        ((tokens, model), whole((tokens, model))), ((tokens, model), whole((tokens, model))), ((1, model), whole((1, model))),
        ((model, own), across), ((model, own), across), ((4, own), whole((4, own))),
        ((gate_rows, width), pl.BlockSpec((gate_rows // steps, width), lambda i: (i, 0))),
        ((1, lru), whole((1, lru))), ((1, lru), whole((1, lru))), ((1, own), whole((1, own))),
        ((own, model), pl.BlockSpec((own // steps, model), lambda i: (i, 0))), ((1, model), whole((1, model))),
        ((model, cols), feed_across), ((model, cols), feed_across),
        ((cols, model), pl.BlockSpec((cols // steps, model), lambda i: (i, 0))),
    ]
    return pl.pallas_call(
        results_kernel,
        grid=(steps,),
        out_shape=tuple(jax.ShapeDtypeStruct(shape, F32) for shape, _ in outs),
        in_specs=[
            pl.BlockSpec((3, model, own // steps), lambda i: (0, 0, i)),
            pl.BlockSpec((3, cols // steps, model), lambda i: (0, i, 0)),
            pl.BlockSpec((gate_rows // steps, width), lambda i: (i, 0)),
            whole((tokens, model)), whole((tokens, model)), whole((16, lru)), whole((16, own)),
        ],
        out_specs=tuple(spec for _, spec in outs),
        compiler_params=pltpu.CompilerParams(vmem_limit_bytes=48 * 2**20),
        name="results",
    )(wa, fa, ga, bout, igrad, osm, osmz)


def local(
    nz,
    groups,
    block_input,
    doc_starts,
    first_gain,
    branch_weight,
    lru_weight,
    filter_taps,
    rate_gate,
    input_gate,
    rate_bias,
    input_bias,
    decay_logit,
    out_weight,
    second_gain,
    feed_gate,
    feed_up,
    feed_down,
    cotangent,
):
    model = block_input.shape[1]
    heads, width = rate_gate.shape[:2]
    lru = heads * width

    def line(v):
        v = v.astype(F32)
        v = v[None] if v.ndim == 1 else v
        return jnp.pad(v, ((0, 0), (0, lru - v.shape[1])))

    blank = jnp.zeros((3, lru), F32)
    vecs = jnp.concatenate([
        line(first_gain), line(second_gain), line(rate_bias), line(input_bias), line(doc_starts), blank,
        line(filter_taps), line(decay_logit), blank,
    ])
    (wl, wb, wo, fb, lin, br, cv, rl, il, st, pr, y, ffg, sin, mk, vec, base, rgrad, g2g) = forward(
        nz, block_input, vecs, rate_gate, input_gate, cotangent, lru_weight, branch_weight, out_weight,
        feed_gate, feed_up, feed_down,
    )
    ffg = ffg.reshape(3, nz, 2, ffg.shape[1] // (2 * nz), model)
    sums = backward(
        nz, rate_gate, input_gate, sin, mk, vec, vecs, rgrad, g2g, block_input, wl, wb, wo, fb, lin, br, cv, rl, il, st, pr,
        base, y, ffg,
    )
    made = results(*sums)
    block_output, input_grad, *summed = made
    if groups > 1:
        same = [[8 * g + b for g in range(groups)] for b in range(8)]
        summed = lax.psum(tuple(summed), "tp", axis_index_groups=same)
    g1, branch, lru_grad, taps, gates, rb, ib, decay, ow, g2, gate, up, down = summed
    gates = gates.reshape(2, heads, width, width)
    return (
        block_output, input_grad, g1[0], branch, lru_grad, taps, gates[0], gates[1], rb[0], ib[0], decay[0], ow, g2[0],
        gate, up, down,
    )


def solution(mesh):
    by_rows = P(("tp", "dp"), None)
    by_cols = P(None, "dp")
    split = P("dp", None)
    return jax.shard_map(
        functools.partial(local, mesh.shape["dp"], mesh.shape["tp"] // 8),
        mesh=mesh,
        in_specs=(
            by_rows, P("tp"), P(), by_cols, by_cols, by_cols, P(), P(), P(), P(), P("dp"), split, P(), by_cols, by_cols,
            split, by_rows,
        ),
        out_specs=(
            by_rows, by_rows, P(), by_cols, by_cols, by_cols, P(), P(), P(), P(), P("dp"), split, P(), by_cols, by_cols,
            split,
        ),
        check_vma=False,
    )
```

```python
import functools
import math

import jax
import jax.numpy as jnp
from jax import lax
from jax.experimental import pallas as pl
from jax.experimental.pallas import tpu as pltpu
from jax.sharding import PartitionSpec as P

EPS = 1e-06
DECAY_SCALE = 8.0
F32 = jnp.float32
BF16 = jnp.bfloat16
MESH = pl.DeviceIdType.MESH
VMEM = pltpu.VMEM
DMA = pltpu.SemaphoreType.DMA
NN = (((1,), (0,)), ((), ()))
NT = (((1,), (1,)), ((), ()))
TN = (((0,), (0,)), ((), ()))
HALO = 16
LANE = 128
GELU_A = math.sqrt(2.0 / math.pi)
GELU_B = 0.044715


def dot(left, right, form):
    return lax.dot_general(left, right, form, preferred_element_type=F32)


def sigmoid(v):
    return 1.0 / (1.0 + jnp.exp(-v))


def softplus(v):
    return jnp.maximum(v, 0.0) + jnp.log1p(jnp.exp(-jnp.abs(v)))


def gelu_both(v):
    square = v * v
    tanh = jnp.tanh(GELU_A * v * (1.0 + GELU_B * square))
    half = 0.5 * (1.0 + tanh)
    slope = half + 0.5 * v * (1.0 - tanh * tanh) * (GELU_A * (1.0 + 3.0 * GELU_B * square))
    return v * half, slope


def gelu_only(v):
    return v * (0.5 * (1.0 + jnp.tanh(GELU_A * v * (1.0 + GELU_B * v * v))))


class Place:
    def __init__(self, nz):
        self.nz = nz
        self.t = lax.axis_index("tp")
        self.z = lax.axis_index("dp")
        self.b = lax.rem(self.t, 8)
        self.core = lax.rem(self.t, 2)
        self.x = lax.rem(self.t // 2, 2)
        self.y = lax.rem(self.t // 4, 2)
        self.chip = self.b // 2

    def flip(self, r):
        t = self.t
        if r & 1:
            t = t + 2 - 4 * self.x
        if r & 2:
            t = t + 4 - 8 * self.y
        return t

    def chip_of(self, r):
        c = self.chip
        if r & 1:
            c = c + 1 - 2 * self.x
        if r & 2:
            c = c + 2 - 4 * self.y
        return c

    def plane(self, r):
        return (self.flip(r), self.z)

    def sibling(self):
        return (self.t + 1 - 2 * self.core, self.z)

    def along(self, d):
        return (self.t, lax.rem(self.z + d, self.nz))

    def z_from(self, d):
        return lax.rem(self.z + self.nz - d, self.nz)


def greet(peers):
    barrier = pltpu.get_barrier_semaphore()
    for peer in peers:
        pl.semaphore_signal(barrier, inc=1, device_id=peer, device_id_type=MESH)
    pl.semaphore_wait(barrier, len(peers))


def remote(src, dst, send, recv, peer):
    return pltpu.make_async_remote_copy(
        src_ref=src, dst_ref=dst, send_sem=send, recv_sem=recv, device_id=peer, device_id_type=MESH
    )


class Sends:
    def __init__(self):
        self.started = []

    def when(self, cond, action):
        if cond is None:
            action()
        else:
            pl.when(cond)(action)

    def go(self, make, cond=None):
        self.when(cond, lambda: make().start())
        self.started.append((cond, make))

    def arrived(self, make, cond=None):
        self.when(cond, lambda: make().wait_recv())

    def sent(self, make):
        make().wait_send()
        self.started = [(cond, other) for cond, other in self.started if other is not make]

    def finish(self):
        for cond, make in self.started:
            self.when(cond, lambda: make().wait_send())


class PlaneGather:
    def __init__(self, me, out, piece, send, recv, at, cond=None, first=None, joined=None, ready=None):
        self.me, self.out, self.piece, self.cond, self.joined = me, out, piece, cond, joined
        self.send, self.recv, self.at, self.first, self.ready = send, recv, at, first, ready

    def copy(self, i, src, dst, peer):
        return remote(src, dst, self.send.at[self.at + (i,)], self.recv.at[self.at + (i,)], peer)

    def whole(self, i, r, peer, first=False):
        def make():
            place = self.piece(self.me.chip_of(r), self.me.core, None)
            return self.copy(i, self.first() if first and self.first else place, place, peer)
        return make

    def half(self, i, r, part, peer):
        def make():
            place = self.piece(self.me.chip_of(r), self.me.core, part)
            return self.copy(i, place, place, peer)
        return make

    def across(self, core):
        def make():
            place = self.joined(core)
            return self.copy(4, place, place, self.me.sibling())
        return make

    def begin(self):
        for i, r in ((0, 1), (1, 2)):
            self.out.go(self.whole(i, 0, self.me.plane(r), True), self.cond)
        if not self.joined:
            self.out.go(self.whole(4, 0, self.me.sibling(), True), self.cond)

    def relay(self):
        me = self.me
        for i, r, part in ((0, 1, 0), (1, 2, 1)):
            self.out.arrived(self.whole(i, r, me.plane(r)), self.cond)
            self.out.go(self.half(2 + i, r, part, me.plane(3 - r)), self.cond)
            if not self.joined:
                self.out.go(self.whole(4 + r, r, me.sibling()), self.cond)

    def far(self):
        for part in (0, 1):
            self.out.arrived(self.half(2 + part, 3, part, self.me.plane(2 - part)), self.cond)
        if self.joined:
            if self.ready:
                self.ready()
            self.out.go(self.across(self.me.core), self.cond)
        else:
            self.out.go(self.whole(7, 3, self.me.sibling()), self.cond)

    def end(self):
        me = self.me
        if self.joined:
            self.out.arrived(self.across(1 - me.core), self.cond)
            return
        for r in range(4):
            def make(r=r):
                place = self.piece(me.chip_of(r), 1 - me.core, None)
                return self.copy(4 + r, place, place, me.sibling())
            self.out.arrived(make, self.cond)


class PlaneSum:
    def __init__(self, me, out, block, recv, send_sem, recv_sem, at, source=None):
        self.me, self.out, self.block, self.got = me, out, block, recv
        self.send_sem, self.recv_sem, self.at = send_sem, recv_sem, at
        self.source = source or block

    def copy(self, i, src, peer):
        def make():
            return remote(
                src(), self.got(i), self.send_sem.at[self.at + (i,)], self.recv_sem.at[self.at + (i,)], peer
            )
        return make

    def put(self, i):
        half = i // 2
        to = 3 if i % 2 else half + 1
        self.out.go(self.copy(i, lambda: self.source(to, half), self.me.plane(half + 1)))

    def begin(self):
        for i in (1, 0, 3, 2):
            self.put(i)

    def wait(self, i):
        self.out.arrived(self.copy(i, lambda: self.got(i), self.me.plane(1)))

    def relay(self):
        for half, r in ((0, 2), (1, 1)):
            self.wait(2 * half + 1)
            mine = self.block(r, half)
            mine[...] = (mine[...].astype(F32) + self.got(2 * half + 1)[...].astype(F32)).astype(BF16)
            self.out.go(self.copy(4 + half, lambda r=r, half=half: self.block(r, half), self.me.plane(r)))

    def total(self, half):
        self.wait(2 * half)
        self.wait(4 + half)
        return self.got(2 * half)[...].astype(F32) + self.got(4 + half)[...].astype(F32)


def rows(i, size):
    return pl.ds(pl.multiple_of(i * size, size), size)


def rms(v, gain):
    return v * lax.rsqrt(jnp.mean(v * v, axis=-1, keepdims=True) + EPS) * gain


def head_lanes(h, width):
    return pl.ds(pl.multiple_of(h * width, width), width)


def tile_scan(a, b, row, back):
    for step in (1, 2, 4):
        if back:
            seen = row < 8 - step
            shift = 8 - step
        else:
            seen = row >= step
            shift = step
        b_before = jnp.where(seen, pltpu.roll(b, shift, 0), 0.0)
        a_before = jnp.where(seen, pltpu.roll(a, shift, 0), 1.0)
        b = b + a * b_before
        a = a * a_before
    return a, b


def forward_kernel(nz, heads, x, gain1, gain2, bias1, bias2, starts, taps_in, dlogit, rg, ig, cot, lw, bw, ow, fgate, fup, fdown,
                   o_wl, o_wb, o_wo, o_fb, o_lin, o_br, o_cv, o_rl, o_il, o_st, o_pr, o_y, o_wg,
                   sin, mk, vec, base, rgrad, g2g, vecs,
                   wl, wb, wo, f, cots, win, turned, fb, lin, br, cv, rl, il, st, pr, pst, ends, ms, hx,
                   res, s, h, lg, ug, ybuf, sbuf, srecv, sown, fc, acts, slopes,
                   lsem, osem, zs, zr, ps, pr_sem, fcs, fcr, qs, qr, vs, vr, es, er, hs, hr, ss, sr, gs, gr, ks, kr):
    me = Place(nz)
    out, feeds = Sends(), Sends()
    tokens, model = x.shape
    lru = wl.shape[1]
    width = lru // heads
    own = lru // nz
    cols = f.shape[1]
    part = cols // (2 * nz)
    piece_rows = model // 8
    chunk = 256
    z = me.z

    window = pl.ds(pl.multiple_of((me.chip // 2) * (4 * part) + lax.rem(me.chip, 2) * LANE, LANE), 256)
    shift = 64 * lax.rem(me.chip, 2)
    mine = rows(z, own)
    local = [
        (fgate.at[:, window], win.at[0]),
        (fup.at[:, window], win.at[1]),
        (lw, wl.at[:, mine]),
        (bw, wb.at[:, mine]),
        (ow, wo.at[mine]),
        (fdown.at[rows(me.chip, 2 * part)], f.at[2, rows(z, 2 * part)]),
        (cot, cots.at[0]),
    ]
    local = [pltpu.make_async_copy(a, b, lsem.at[i]) for i, (a, b) in enumerate(local)]
    for copy in local:
        copy.start()
    vecs[...] = jnp.zeros(vecs.shape, F32)
    for i, v in enumerate((gain1, gain2, bias1, bias2, starts)):
        vecs[i:i + 1, 0:v.shape[0]] = v[...].astype(F32).reshape(1, v.shape[0])
    vecs[8:12, 0:own] = taps_in[...].astype(F32)
    vecs[12:13, 0:own] = dlogit[...].astype(F32).reshape(1, own)
    greet([me.along(d) for d in range(1, nz)] + [me.plane(r) for r in (1, 2, 3)] + [me.sibling()])

    def vector(d, origin):
        def make():
            place = vec.at[:, rows(origin(), own)]
            return remote(vecs.at[8:16, 0:own], place, vs.at[d - 1], vr.at[d - 1], me.along(d))
        return make

    def halo():
        return remote(x.at[tokens - HALO:tokens], hx, hs.at[0], hr.at[0], me.along(1))

    out.go(halo)
    for d in range(1, nz):
        out.go(vector(d, lambda: z))

    mine_of = 4 * me.core + me.chip

    def slot(m, zz, b):
        if m < 2:
            return (wl, wb)[m].at[rows(b, piece_rows), rows(zz, own)]
        if m == 2:
            return wo.at[rows(zz, own), rows(b, LANE)]
        at = pl.ds(pl.multiple_of(zz * (2 * part) + me.core * part, part), part)
        return f.at[0:2, at] if m == 3 else f.at[2, at]

    def source(m):
        if m < 2:
            return (lw, bw)[m].at[rows(mine_of, piece_rows)]
        if m == 2:
            return ow.at[:, rows(mine_of, LANE)]
        if m == 3:
            return turned.at[:, pl.ds(pl.multiple_of(shift + me.core * part, 32), part)]
        return fdown.at[pl.ds(pl.multiple_of(me.chip * (2 * part) + me.core * part, part), part)]

    def origin(hop, right):
        return z - 1 - hop if right else z + 1 + hop

    def has(hop, right):
        return z - 1 - hop >= 0 if right else z + 1 + hop < nz

    def along(m, hop, right, from_me):
        def make():
            step = 1 if right else -1
            zz = z - step * hop if from_me else origin(hop, right)
            place = slot(m, zz, mine_of)
            src = source(m) if from_me and hop == 0 else place
            at = (m, hop, int(right))
            peer = (me.t, z + step if from_me else z)
            return remote(src, place, zs.at[at], zr.at[at], peer)
        return make

    def z_begin(m, hop=0):
        for right in (True, False):
            there = z + 1 < nz if right else z >= 1
            if hop:
                there = jnp.logical_and(there, has(hop - 1, right))
            (out if m < 3 else feeds).go(along(m, hop, right, True), there)

    gathers = {}
    for m in range(3):
        for hop in range(nz - 1):
            for right in (True, False):
                def place(chip, core, half, m=m, hop=hop, right=right):
                    zz, b = origin(hop, right), 4 * core + chip
                    if half is None:
                        return slot(m, zz, b)
                    if m < 2:
                        at = pl.ds(pl.multiple_of(b * piece_rows + half * (piece_rows // 2), piece_rows // 2), piece_rows // 2)
                        return (wl, wb)[m].at[at, rows(zz, own)]
                    at = pl.ds(pl.multiple_of(zz * own + half * (own // 2), own // 2), own // 2)
                    return wo.at[at, rows(b, LANE)]

                def joined(core, m=m, hop=hop, right=right):
                    zz = origin(hop, right)
                    if m < 2:
                        return (wl, wb)[m].at[rows(core, 4 * piece_rows), rows(zz, own)]
                    return wo.at[rows(zz, own), rows(core, 4 * LANE)]

                gathers[m, hop, right] = PlaneGather(
                    me, out, place, ps, pr_sem, (m, 2 * hop + int(right)), has(hop, right), joined=joined
                )

    def share(m, hop, right, from_me):
        def make():
            at = (m - 3, 2 * hop + int(right))
            place = slot(m, origin(hop, right), mine_of)
            if not from_me:
                other = pl.ds(pl.multiple_of(origin(hop, right) * (2 * part) + (1 - me.core) * part, part), part)
                place = f.at[0:2, other] if m == 3 else f.at[2, other]
            return remote(place, place, fcs.at[at], fcr.at[at], me.sibling())
        return make

    def z_step(m, hop):
        for right in (True, False):
            out.arrived(along(m, hop, right, False), has(hop, right))
        if hop + 1 < nz - 1:
            z_begin(m, hop + 1)
        for right in (True, False):
            if m < 3:
                gathers[m, hop, right].begin()
            else:
                feeds.go(share(m, hop, right, True), has(hop, right))

    def relay(m, hop):
        for right in (True, False):
            gathers[m, hop, right].relay()

    def far(m, hop):
        for right in (True, False):
            gathers[m, hop, right].far()

    def all_of(m):
        for hop in range(nz - 1):
            for right in (True, False):
                gathers[m, hop, right].end()

    half = tokens // 2

    def cot_whole(i, r, part_of):
        at = pl.ds(part_of * half, half)
        return lambda: remote(cot.at[at], cots.at[r, at], qs.at[2 * part_of + i], qr.at[2 * part_of + i], me.plane(r))

    def cot_part(part_of, r):
        at = pl.ds(part_of * half, half)
        return lambda: remote(cots.at[r, at], cots.at[3, at], qs.at[4 + part_of], qr.at[4 + part_of], me.plane(3 - r))

    def lanes(h):
        return head_lanes(h, width)

    def project(h, _):
        lin[h] = dot(fb[...], wl[:, lanes(h)], NN)
        taps = vec[0:4, lanes(h)]
        conv = taps[0:1] * lin[h, HALO:, :]
        for k in range(1, 4):
            conv = conv + taps[k:k + 1] * lin[h, HALO - k:HALO - k + tokens, :] * mk[:, k:k + 1]
        conv = conv.astype(BF16)
        cv[h] = conv
        rl[h] = (dot(conv, rg[h], NN) + vecs[2:3, lanes(h)]).astype(BF16)
        il[h] = (dot(conv, ig[h], NN) + vecs[3:4, lanes(h)]).astype(BF16)
        return 0

    row = lax.broadcasted_iota(jnp.int32, (8, width), 0)

    def scan_head(h, _):
        rate = softplus(-vec[4:5, lanes(h)]) * -DECAY_SCALE

        def tile(i, carried):
            state, factor = carried
            at = rows(i, 16)
            start = mk[at, 0:1]
            keep = 1.0 - start
            decay = jnp.exp(sigmoid(rl[h, at, :].astype(F32)) * rate)
            a = keep * decay
            scale = (start + keep * jnp.sqrt(1.0 - decay * decay)) * sigmoid(il[h, at, :].astype(F32))
            b = scale * cv[h, at, :].astype(F32)
            for t in range(2):
                cum, run = tile_scan(a[8 * t:8 * t + 8], b[8 * t:8 * t + 8], row, False)
                run = run + cum * state
                cum = cum * factor
                here = pl.ds(pl.multiple_of(i * 16 + 8 * t, 8), 8)
                st[h, here, :] = run
                pst[h, here, :] = cum
                state, factor = run[7:8], cum[7:8]
            return state, factor

        state, factor = lax.fori_loop(
            0, tokens // 16, tile, (jnp.zeros((1, width), F32), jnp.ones((1, width), F32)), unroll=8
        )
        ends[0, 0:1, lanes(h)] = state
        ends[0, 1:2, lanes(h)] = factor
        return 0

    def end_copy(d):
        return lambda: remote(ends.at[0], ends.at[d], es.at[d - 1], er.at[d - 1], me.along(d))

    def branch(h, _):
        br[h] = dot(fb[HALO:], wb[:, lanes(h)], NN)
        return 0

    def finish(h, _):
        state = st[h] + pst[h] * sin[:, lanes(h)]
        st[h] = state
        pr[:, lanes(h)] = (state * gelu_only(br[h])).astype(BF16)
        return 0

    def project_out(j, _):
        at = rows(j, chunk)
        res[:, at] = x[:, at].astype(F32) + dot(pr[...], wo[:, at], NN)
        return 0

    def second_copy(r):
        return lambda: remote(s.at[0:tokens], s.at[r * tokens:(r + 1) * tokens], ss.at[r - 1], sr.at[r - 1], me.plane(r))

    def second_part(part_of, r):
        at, to = (pl.ds(q * tokens + part_of * half, half) for q in (r, 3))
        return lambda: remote(s.at[at], s.at[to], ss.at[2 + part_of], sr.at[2 + part_of], me.plane(3 - r))

    saved = [
        (wl, o_wl), (wb, o_wb), (wo, o_wo), (fb, o_fb), (lin, o_lin), (br, o_br), (cv, o_cv), (rl, o_rl), (il, o_il),
        (st, o_st), (pr, o_pr),
    ]
    saved = [pltpu.make_async_copy(a, b, osem.at[i]) for i, (a, b) in enumerate(saved)]
    grad_sum = PlaneSum(
        me, out, lambda r, part: sbuf.at[r - 1, pl.ds(part * half, half)], lambda i: srecv.at[i], gs, gr, ()
    )
    def feed_ahead(r):
        at = pl.ds(r * tokens, tokens)

        def hidden_of(j, _):
            here = rows(j, chunk)
            second = s[at]
            act, slope = gelu_both(dot(second, f[0, here, :], NT))
            up = dot(second, f[1, here, :], NT)
            h[at, here] = (act * up).astype(BF16)
            acts[at, here] = act
            slopes[at, here] = up * slope
            return 0

        lax.fori_loop(0, cols // chunk, hidden_of, 0, unroll=3)

    def feed_back(r):
        at = pl.ds(r * tokens, tokens)

        def grads_of(j, _):
            here = rows(j, chunk)
            hg = dot(cots[r], f[2, here, :], NT)
            lg[at, here] = (hg * slopes[at, here]).astype(BF16)
            ug[at, here] = (hg * acts[at, here]).astype(BF16)
            return 0

        lax.fori_loop(0, cols // chunk, grads_of, 0, unroll=3)

        def back_of(j, _):
            here = rows(j, chunk)
            value = dot(lg[at], f[0, :, here], NN) + dot(ug[at], f[1, :, here], NN)
            if r:
                sbuf[r - 1, :, here] = value.astype(BF16)
            else:
                sown[:, here] = value
            return 0

        lax.fori_loop(0, model // chunk, back_of, 0, unroll=4)
        for i in {0: (), 1: (0,), 2: (2,), 3: (1, 3)}[r]:
            grad_sum.put(i)

    def out_of(j, _):
        here = rows(j, chunk)
        for r in range(4):
            value = dot(h[r * tokens:(r + 1) * tokens], f[2, :, here], NN)
            if r:
                ybuf[r - 1, :, here] = value.astype(BF16)
            else:
                base[:, here] = res[:, here] + value
        return 0

    def feed_half(zz, core):
        return pl.ds(pl.multiple_of(zz * (2 * part) + core * part, part), part)

    def core_copy(m, zz):
        at = (m, zz)
        return lambda: remote(f.at[m, feed_half(zz, 1 - me.core)], fc.at[m, zz], ks.at[at], kr.at[at], me.sibling())

    def feed_wgrad(m, left):
        def body(i, _):
            here = rows(i, chunk)
            right = jnp.concatenate([cots[r, :, here] for r in range(4)], axis=0) if m == 2 else s[:, here]
            for j in range(cols // chunk):
                f[m, pl.ds(j * chunk, chunk), here] = dot(left[:, j * chunk:(j + 1) * chunk], right, TN).astype(BF16)
            return 0

        lax.fori_loop(0, model // chunk, body, 0, unroll=4)
        for zz in range(nz):
            out.go(core_copy(m, zz))

    last = [pltpu.make_async_copy(ybuf, o_y, osem.at[11]), pltpu.make_async_copy(fc, o_wg, osem.at[12])]
    own_turned = pltpu.make_async_copy(
        turned.at[:, pl.ds(pl.multiple_of(shift, 32), 2 * part)], f.at[0:2, rows(z, 2 * part)], lsem.at[7]
    )
    g1, g2 = vecs[0:1, 0:model], vecs[1:2, 0:model]
    start_row = vecs[4:5, 0:nz * tokens]

    z_begin(0)
    for i, r in ((0, 1), (1, 2)):
        out.go(cot_whole(i, r, 0))
    for d in range(1, nz):
        out.arrived(vector(d, lambda: me.z_from(d)))
    vec[:, mine] = vecs[8:16, 0:own]
    for i in range(2, 7):
        local[i].wait()
    z_begin(1)
    out.arrived(halo)
    fb[0:HALO] = rms(hx[...].astype(F32), g1).astype(BF16)
    z_step(0, 0)
    z_begin(2)
    z_step(0, 1)
    z_step(1, 0)
    z_step(0, 2)
    z_step(1, 1)
    z_step(2, 0)
    relay(0, 2)
    length = nz * tokens
    lane = lax.broadcasted_iota(jnp.int32, (1, length), 1)
    keep_row = 1.0 - start_row
    valid = keep_row
    lines, later_lines = [start_row, valid], []
    for k in range(1, 4):
        if k > 1:
            valid = valid * jnp.where(lane >= k - 1, pltpu.roll(keep_row, k - 1, 1), 0.0)
            lines.append(valid)
        later_lines.append(jnp.where(lane < length - k, pltpu.roll(valid, length - k, 1), 0.0))
    ms[...] = jnp.concatenate(lines + later_lines + [jnp.zeros_like(start_row)], axis=0)
    mk[...] = jnp.concatenate([ms[:, rows(z, tokens)], jnp.zeros((LANE - 8, tokens), F32)], axis=0).T
    relay(0, 1)
    z_step(1, 2)
    relay(0, 0)
    for i in range(2):
        local[i].wait()
        turned[i] = win[i].T
    own_turned.start()
    fb[HALO:] = rms(x[...].astype(F32), g1).astype(BF16)
    z_begin(3)
    far(0, 1)
    z_step(2, 1)
    z_begin(4)
    relay(1, 0)
    relay(1, 1)
    relay(1, 2)
    far(0, 2)
    far(0, 0)
    z_step(3, 0)
    for i, r in ((0, 1), (1, 2)):
        out.go(cot_whole(i, r, 1))
    all_of(0)
    lax.fori_loop(0 * heads // 3, 1 * heads // 3, project, 0, unroll=2)
    z_step(2, 2)
    relay(2, 0)
    lax.fori_loop(1 * heads // 3, 2 * heads // 3, project, 0, unroll=2)
    relay(2, 1)
    far(1, 0)
    lax.fori_loop(2 * heads // 3, 3 * heads // 3, project, 0, unroll=2)
    far(1, 1)
    far(1, 2)
    lax.fori_loop(0 * heads // 3, 1 * heads // 3, scan_head, 0, unroll=2)
    lax.fori_loop(1 * heads // 3, 2 * heads // 3, scan_head, 0, unroll=2)
    all_of(1)
    lax.fori_loop(2 * heads // 3, 3 * heads // 3, scan_head, 0, unroll=2)
    for d in range(1, nz):
        out.go(end_copy(d), z + d < nz)
    relay(2, 2)
    for part_of in range(2):
        out.arrived(cot_whole(0, 1, part_of))
    out.go(cot_part(0, 1))
    for part_of in range(2):
        out.arrived(cot_whole(1, 2, part_of))
    out.go(cot_part(1, 2))
    z_step(4, 0)
    far(2, 0)
    lax.fori_loop(0, heads, branch, 0, unroll=3)
    far(2, 1)
    far(2, 2)
    for d in range(1, nz):
        out.arrived(end_copy(d), z >= d)
    incoming = jnp.zeros((1, lru), F32)
    for d in range(nz - 1, 0, -1):
        end = ends[d, 0:1, :] + ends[d, 1:2, :] * incoming
        incoming = jnp.where(d <= z, end, incoming)
    sin[...] = incoming

    all_of(2)
    lax.fori_loop(0, heads, finish, 0, unroll=3)
    lax.fori_loop(0, model // chunk, project_out, 0, unroll=4)
    s[0:tokens] = rms(res[...], g2).astype(BF16)
    for r in (1, 2):
        out.go(second_copy(r))
    for copy in saved:
        copy.start()
    z_step(3, 1)
    z_step(4, 1)
    z_step(3, 2)
    for part_of, r in ((0, 2), (1, 1)):
        out.arrived(cot_part(part_of, r))
    out.arrived(second_copy(2))
    out.go(second_part(1, 2))
    out.arrived(second_copy(1))
    out.go(second_part(0, 1))
    for hop in range(nz - 1):
        for right in (True, False):
            out.arrived(share(3, hop, right, False), has(hop, right))
    own_turned.wait()
    feed_ahead(1)
    z_step(4, 2)
    feed_ahead(2)
    for hop in range(nz - 1):
        for right in (True, False):
            out.arrived(share(4, hop, right, False), has(hop, right))
    feed_back(1)
    feed_back(2)
    for part_of, near in ((0, 2), (1, 1)):
        out.arrived(second_part(part_of, near))
    feed_ahead(3)
    feed_back(3)
    feed_ahead(0)
    feed_back(0)
    feeds.finish()
    feed_wgrad(0, lg)
    lax.fori_loop(0, model // chunk, out_of, 0, unroll=4)
    last[0].start()
    grad_sum.relay()
    feed_wgrad(1, ug)
    feed_wgrad(2, h)
    for zz in range(nz):
        out.arrived(core_copy(1, zz))
        fc[1, zz] = (fc[1, zz].astype(F32) + f[1, feed_half(zz, me.core), :].astype(F32)).astype(BF16)
    for zz in range(nz):
        out.arrived(core_copy(0, zz))
        fc[0, zz] = (fc[0, zz].astype(F32) + f[0, feed_half(zz, me.core), :].astype(F32)).astype(BF16)
    for zz in range(nz):
        out.arrived(core_copy(2, zz))
        fc[2, zz] = (fc[2, zz].astype(F32) + f[2, feed_half(zz, me.core), :].astype(F32)).astype(BF16)
    for part_of in range(2):
        at = pl.ds(part_of * half, half)
        sown[at, :] = sown[at, :] + grad_sum.total(part_of)
    sg = sown[...]
    value = res[...]
    q = sg * g2
    inv = lax.rsqrt(jnp.mean(value * value, axis=-1, keepdims=True) + EPS)
    pull = jnp.mean(q * value, axis=-1, keepdims=True)
    rgrad[...] = cots[0].astype(F32) + (inv * q - value * (inv * inv * inv * pull))
    g2g[...] = jnp.sum(sg * value * inv, axis=0, keepdims=True)
    last[1].start()
    for copy in saved + last:
        copy.wait()
    out.finish()


def forward(nz, x, gain1, gain2, bias1, bias2, starts, taps, dlogit, rg, ig, cot, lw, bw, ow, fgate, fup, fdown):
    tokens, model = x.shape
    heads, width = rg.shape[0], rg.shape[1]
    lru = heads * width
    cols = fgate.shape[1]
    k = nz - 1
    vm = pl.BlockSpec(memory_space=VMEM)
    hbm = pl.BlockSpec(memory_space=pl.ANY)
    by_head = (heads, tokens, width)
    saved = [
        ((model, lru), BF16), ((model, lru), BF16), ((lru, model), BF16), ((HALO + tokens, model), BF16),
        ((heads, HALO + tokens, width), F32), (by_head, F32), (by_head, BF16), (by_head, BF16), (by_head, BF16),
        (by_head, F32), ((tokens, lru), BF16), ((3, tokens, model), BF16), ((3, nz, cols // (2 * nz), model), BF16),
    ]
    kept = [
        ((1, lru), F32), ((tokens, LANE), F32), ((8, lru), F32), ((tokens, model), F32), ((tokens, model), F32),
        ((1, model), F32), ((16, lru), F32),
    ]
    sems = []
    for shape in ((5, k, 2), (3, 2 * k, 5), (2, 2 * k), (6,), (k,), (k,), (1,), (4,), (6,), (3, nz)):
        sems += [DMA(shape)] * 2
    return pl.pallas_call(
        functools.partial(forward_kernel, nz, heads),
        out_shape=tuple(jax.ShapeDtypeStruct(*a) for a in saved + kept),
        in_specs=[vm] * 10 + [hbm] * 7,
        out_specs=[hbm] * len(saved) + [vm] * len(kept),
        scratch_shapes=[
            VMEM((model, lru), BF16), VMEM((model, lru), BF16), VMEM((lru, model), BF16), VMEM((3, cols, model), BF16),
            VMEM((4, tokens, model), BF16), VMEM((2, model, 256), BF16), VMEM((2, 256, model), BF16),
            VMEM((HALO + tokens, model), BF16), VMEM((heads, HALO + tokens, width), F32), VMEM(by_head, F32),
            VMEM(by_head, BF16), VMEM(by_head, BF16), VMEM(by_head, BF16), VMEM(by_head, F32), VMEM((tokens, lru), BF16),
            VMEM(by_head, F32), VMEM((nz, 8, lru), F32), VMEM((8, nz * tokens), F32), VMEM((HALO, model), BF16),
            VMEM((tokens, model), F32), VMEM((4 * tokens, model), BF16), VMEM((4 * tokens, cols), BF16),
            VMEM((4 * tokens, cols), BF16), VMEM((4 * tokens, cols), BF16), VMEM((3, tokens, model), BF16),
            VMEM((3, tokens, model), BF16), VMEM((6, tokens // 2, model), BF16), VMEM((tokens, model), F32), VMEM((3, nz, cols // (2 * nz), model), BF16),
            VMEM((4 * tokens, cols), F32), VMEM((4 * tokens, cols), F32),
            DMA((8,)), DMA((len(saved),)),
        ] + sems,
        compiler_params=pltpu.CompilerParams(collective_id=0, has_side_effects=True, vmem_limit_bytes=62 * 2**20),
        name="forward_and_feed",
    )(x, gain1, gain2, bias1, bias2, starts, taps, dlogit, rg, ig, cot, lw, bw, ow, fgate, fup, fdown)


def backward_kernel(nz, heads, rg, ig, sin, mk, vec, vecs, rgrad, g2g,
                    i_x, i_wl, i_wb, i_wo, i_fb, i_lin, i_br, i_cv, i_rl, i_il, i_st, i_pr, i_base, i_y, i_ffg,
                    wa, fa, ga, bout, igrad, osm, osmz,
                    x, wl, wb, wo, fb, lin, br, cv, rl, il, st, pr, yk,
                    rgb, turned, fl, rlg, ilg, bg, lgr, ends, hal,
                    g, wc, wp, wz, fin, fc, fz, ffin, gt, gc, gp, gz, gfin, sm, smz, yp, inc,
                    lsem, osem, wcs, wcr, wps, wpr, wzs, wzr, was, war, fzs, fzr, fas, far,
                    gcs, gcr, gps, gpr, gzs, gzr, gys, gyr, gas, gar, yps, ypr, s1s, s1r, s2s, s2r,
                    es, er, hs, hr):
    me = Place(nz)
    out = Sends()
    core, other, chip, z = me.core, 1 - me.core, me.chip, me.z
    tokens, model = x.shape
    lru = wl.shape[1]
    width = lru // heads
    own = lru // nz
    block = model // 8
    half_rows = block // 2
    part = fc.shape[2]
    k = nz - 1

    loads = dict(
        fc=(i_ffg, fc), pr=(i_pr, pr), wo=(i_wo, wo), br=(i_br, br), st=(i_st, st),
        y0=(i_y.at[1, 0:tokens // 2], yk.at[0]), y1=(i_y.at[0, tokens // 2:tokens], yk.at[1]),
        rl=(i_rl, rl), fb=(i_fb, fb), wb=(i_wb, wb), cv=(i_cv, cv), il=(i_il, il), lin=(i_lin, lin), wl=(i_wl, wl),
        x=(i_x, x), base=(i_base, bout),
    )
    loads = {name: pltpu.make_async_copy(a, b, lsem.at[i]) for i, (name, (a, b)) in enumerate(loads.items())}
    for copy in loads.values():
        copy.start()

    def need(*names):
        for name in names:
            loads[name].wait()

    greet([me.along(d) for d in range(1, nz)] + [me.plane(r) for r in (1, 2, 3)] + [me.sibling()])


    def lanes(h):
        return head_lanes(h, width)

    def chain(i, right, from_me):
        def make():
            dest = nz - 1 - i if right else i
            peer = (me.t, z + (1 if right else -1) if from_me else z)
            at = (int(right), i)
            return remote(fc.at[:, dest], fz.at[at], fzs.at[at], fzr.at[at], peer)
        return make

    def chain_begin(i, right):
        out.go(chain(i, right, True), z == 0 if right else z == nz - 1)

    def chain_step(slot):
        for right in (True, False):
            i = slot - (z - 1 if right else nz - 2 - z)
            dest = nz - 1 - i if right else i
            here = jnp.logical_and(i >= 0, dest >= z if right else dest <= z)
            here = jnp.logical_and(here, z >= 1 if right else z <= nz - 2)
            onward = jnp.logical_and(here, dest != z)
            out.arrived(chain(i, right, False), here)

            @pl.when(here)
            def _(right=right, dest=dest, i=i):
                for m in range(3):
                    fc[m, dest] = (fc[m, dest].astype(F32) + fz[int(right), i, m].astype(F32)).astype(BF16)

            out.go(chain(i, right, True), onward)

    def feed_place(c, kk, half):
        at = pl.multiple_of((2 * c + kk) * part, part)
        if half is None:
            return fa.at[:, pl.ds(at, part)]
        return fa.at[:, pl.ds(pl.multiple_of(at + half * (part // 2), part // 2), part // 2)]

    feed_gather = PlaneGather(me, out, feed_place, fas, far, (), None, first=lambda: ffin)
    feed_own = pltpu.make_async_copy(ffin, feed_place(chip, core, None), osem.at[3])

    def feed_total():
        ffin[...] = fc[:, z]
        feed_gather.begin()
        feed_own.start()

    def y_half(r, half):
        return i_y.at[r - 1, pl.ds(half * (tokens // 2), tokens // 2)]

    y_sum = PlaneSum(me, out, lambda r, half: yk.at[half], lambda i: yp.at[i], yps, ypr, (), source=y_half)

    slot_of = {2: 0, 1: 1, 0: 0}

    def core_of(m):
        at = pl.ds(pl.multiple_of(other * (model // 2), model // 2), model // 2)
        return lambda: remote(g.at[slot_of[m], at], wc.at[m], wcs.at[m], wcr.at[m], me.sibling())

    core_copies = [core_of(m) for m in range(3)]

    def block_of(m, r, half=None):
        start = me.chip_of(r) * block
        if half is None:
            return wc.at[m, pl.ds(pl.multiple_of(start, block), block)]
        return wc.at[m, pl.ds(pl.multiple_of(start + half * half_rows, half_rows), half_rows)]

    sums = [
        PlaneSum(me, out, lambda r, half, m=m: block_of(m, r, half), lambda i, m=m: wp.at[m, i], wps, wpr, (m,))
        for m in range(3)
    ]

    def core_sum(m):
        out.arrived(core_copies[m])

        def add(c, _):
            at = rows(c, block)
            mine = pl.ds(pl.multiple_of(core * (model // 2) + c * block, block), block)
            wc[m, at, :] = (wc[m, at, :].astype(F32) + g[slot_of[m], mine, :].astype(F32)).astype(BF16)
            return 0

        lax.fori_loop(0, 4, add, 0)
        sums[m].begin()

    def z_copy(m, d):
        return lambda: remote(
            wc.at[m, rows(chip, block), rows(me.along(d)[1], own)], wz.at[m, d - 1], wzs.at[m, d - 1], wzr.at[m, d - 1], me.along(d)
        )

    def plane_total(m):
        for half in range(2):
            at = pl.ds(pl.multiple_of(chip * block + half * half_rows, half_rows), half_rows)
            wc[m, at, :] = (wc[m, at, :].astype(F32) + sums[m].total(half)).astype(BF16)
        for d in range(1, nz):
            out.go(z_copy(m, d))

    def weight_place(m):
        def place(c, kk, half):
            start = (4 * kk + c) * block
            if half is None:
                return wa.at[m, pl.ds(pl.multiple_of(start, block), block)]
            return wa.at[m, pl.ds(pl.multiple_of(start + half * half_rows, half_rows), half_rows)]
        return place

    own_copies = [pltpu.make_async_copy(fin.at[m], weight_place(m)(chip, core, None), osem.at[m]) for m in range(3)]
    gathers = [
        PlaneGather(
            me, out, weight_place(m), was, war, (m,), None, first=lambda m=m: fin.at[m],
            joined=lambda kk, m=m: wa.at[m, rows(kk, 4 * block)], ready=own_copies[m].wait,
        )
        for m in range(3)
    ]

    def z_total(m):
        for d in range(1, nz):
            out.arrived(z_copy(m, d))
        total = wc[m, rows(chip, block), rows(z, own)].astype(F32)
        for d in range(k):
            total = total + wz[m, d].astype(F32)
        fin[m] = total.astype(BF16)
        gathers[m].begin()
        own_copies[m].start()

    gate_half = gt.shape[0] // 2
    gate_block = gt.shape[0] // 8
    gate_part = gate_block // nz

    def gate_core():
        at = pl.ds(pl.multiple_of(other * gate_half, gate_half), gate_half)
        return remote(gt.at[at], gc, gcs.at[0], gcr.at[0], me.sibling())

    def gate_rows(r, half):
        return gc.at[pl.ds(pl.multiple_of(me.chip_of(r) * gate_block + half * (gate_block // 2), gate_block // 2), gate_block // 2)]

    gate_sum = PlaneSum(me, out, gate_rows, lambda i: gp.at[i], gps, gpr, ())

    def gate_core_sum():
        out.arrived(gate_core)
        mine = pl.ds(pl.multiple_of(core * gate_half, gate_half), gate_half)
        gc[...] = (gc[...].astype(F32) + gt[mine, :].astype(F32)).astype(BF16)
        gate_sum.begin()

    def gate_cut(i):
        return pl.ds(pl.multiple_of(chip * gate_block + i * gate_part, gate_part), gate_part)

    def gate_along(d):
        return lambda: remote(gc.at[gate_cut(me.along(d)[1])], gz.at[d - 1], gzs.at[d - 1], gzr.at[d - 1], me.along(d))

    def gate_back(d, origin):
        return lambda: remote(
            gfin.at[rows(origin(), gate_part)], gfin.at[rows(origin(), gate_part)], gys.at[d - 1], gyr.at[d - 1], me.along(d)
        )

    def gate_total():
        for half in range(2):
            at = pl.ds(pl.multiple_of(chip * gate_block + half * (gate_block // 2), gate_block // 2), gate_block // 2)
            gc[at, :] = (gc[at, :].astype(F32) + gate_sum.total(half)).astype(BF16)
        for d in range(1, nz):
            out.go(gate_along(d))

    def gate_z_total():
        for d in range(1, nz):
            out.arrived(gate_along(d))
        total = gc[gate_cut(z), :].astype(F32)
        for d in range(k):
            total = total + gz[d].astype(F32)
        gfin[rows(z, gate_part), :] = total.astype(BF16)
        for d in range(1, nz):
            out.go(gate_back(d, lambda: z))

    def gate_place(c, kk, half):
        start = (4 * kk + c) * gate_block
        if half is None:
            return ga.at[pl.ds(pl.multiple_of(start, gate_block), gate_block)]
        return ga.at[pl.ds(pl.multiple_of(start + half * (gate_block // 2), gate_block // 2), gate_block // 2)]

    gate_own = pltpu.make_async_copy(gfin, gate_place(chip, core, None), osem.at[4])
    gate_gather = PlaneGather(
        me, out, gate_place, gas, gar, (), None, first=lambda: gfin, joined=lambda kk: ga.at[rows(kk, 4 * gate_block)],
        ready=gate_own.wait,
    )

    def gate_spread():
        for d in range(1, nz):
            out.arrived(gate_back(d, lambda: me.z_from(d)))
        gate_gather.begin()
        gate_own.start()

    def small_copy(i):
        peer = (me.sibling(), me.plane(1), me.plane(2))[i]
        return lambda: remote(sm.at[2 * i], sm.at[2 * i + 1], s1s.at[i], s1r.at[i], peer)

    def small_step(i):
        out.arrived(small_copy(i))
        sm[2 * i + 2] = sm[2 * i] + sm[2 * i + 1]
        if i < 2:
            out.go(small_copy(i + 1))
        else:
            smz[z] = sm[6]
            for d in range(1, nz):
                out.go(small_along(d, lambda: z))

    def small_along(d, origin):
        return lambda: remote(sm.at[6], smz.at[origin()], s2s.at[d - 1], s2r.at[d - 1], me.along(d))


    small = sm.at[0]
    row = lax.broadcasted_iota(jnp.int32, (8, width), 0)

    def branch_back(h, _):
        pg = dot(rgb[...], wo[lanes(h), :], NT)
        act, slope = gelu_both(br[h])
        bg[:, lanes(h)] = (pg * st[h] * slope).astype(BF16)
        fl[h, 0:tokens] = pg * act
        return 0

    def scan_head(h, _):
        rate = softplus(-vec[4:5, lanes(h)]) * -DECAY_SCALE

        def tile(j, carried):
            later, factor = carried
            i = tokens // 16 - 1 - j
            at = rows(i, 16)
            keep = 1.0 - mk[at, 0:1]
            a = keep * jnp.exp(sigmoid(rl[h, at, :].astype(F32)) * rate)
            sgrad = fl[h, at, :]
            b = a * sgrad
            for t in (1, 0):
                cum, run = tile_scan(a[8 * t:8 * t + 8], b[8 * t:8 * t + 8], row, True)
                run = run + cum * later
                cum = cum * factor
                here = pl.ds(pl.multiple_of(i * 16 + 8 * t, 8), 8)
                last = row == 7
                fl[h, here, :] = sgrad[8 * t:8 * t + 8] + jnp.where(last, later, pltpu.roll(run, 7, 0))
                br[h, here, :] = jnp.where(last, factor, pltpu.roll(cum, 7, 0))
                later, factor = run[0:1], cum[0:1]
            return later, factor

        later, factor = lax.fori_loop(
            0, tokens // 16, tile, (jnp.zeros((1, width), F32), jnp.ones((1, width), F32)), unroll=16
        )
        ends[0, 0:1, lanes(h)] = later
        ends[0, 1:2, lanes(h)] = factor
        return 0

    def end_copy(d):
        return lambda: remote(ends.at[0], ends.at[d], es.at[d - 1], er.at[d - 1], me.along(nz - d))

    def wgrad(slot, right):
        def body(h, _):
            g[slot, :, lanes(h)] = dot(turned[...], right[:, lanes(h)], NN).astype(BF16)
            return 0

        lax.fori_loop(0, heads, body, 0, unroll=3)

    def terms(h, _):
        raw = vec[4:5, lanes(h)]
        soft = softplus(-raw)
        later = inc[:, lanes(h)]

        def tile(i, carried):
            before, decays, rates, inputs = carried
            at = rows(i, 16)
            start = mk[at, 0:1]
            keep = 1.0 - start
            flow = fl[h, at, :] + br[h, at, :] * later
            state = st[h, at, :]
            first = lax.broadcasted_iota(jnp.int32, (16, width), 0) == 0
            earlier = jnp.where(first, before, pltpu.roll(state, 1, 0))
            sig = sigmoid(rl[h, at, :].astype(F32))
            gate = sigmoid(il[h, at, :].astype(F32))
            decay = jnp.exp(sig * (soft * -DECAY_SCALE))
            root = jnp.sqrt(1.0 - decay * decay)
            level = start + keep * root
            conv = cv[h, at, :].astype(F32)
            to_scale = flow * conv
            to_decay = keep * (flow * earlier - to_scale * gate * (decay / root))
            to_power = to_decay * decay * sig
            rate_grad = (to_power * (1.0 - sig) * (soft * -DECAY_SCALE)).astype(BF16)
            input_grad = (to_scale * level * gate * (1.0 - gate)).astype(BF16)
            rlg[h, at, :] = rate_grad
            ilg[h, at, :] = input_grad
            fl[h, at, :] = flow * level * gate
            rates = rates + rate_grad.astype(F32)
            inputs = inputs + input_grad.astype(F32)
            return state[15:16], decays + to_power, rates, inputs

        zero = jnp.zeros((16, width), F32)
        _, decays, rates, inputs = lax.fori_loop(0, tokens // 16, tile, (sin[:, lanes(h)], zero, zero, zero), unroll=16)
        small[4:5, lanes(h)] = jnp.sum(decays, axis=0, keepdims=True) * (DECAY_SCALE * sigmoid(-raw))
        small[5:6, lanes(h)] = jnp.sum(rates, axis=0, keepdims=True)
        small[6:7, lanes(h)] = jnp.sum(inputs, axis=0, keepdims=True)
        rate_out, input_out = rlg[h], ilg[h]
        gt[rows(h, width), :] = dot(cv[h], rate_out, TN).astype(BF16)
        gt[rows(heads + h, width), :] = dot(cv[h], input_out, TN).astype(BF16)
        path = (dot(rate_out, rg[h], NT) + dot(input_out, ig[h], NT)).astype(BF16)
        fl[h, 0:tokens] = fl[h, 0:tokens] + path.astype(F32)
        hal[0, h] = fl[h, 0:8]
        return 0

    def halo():
        return remote(hal.at[0], hal.at[1], hs.at[0], hr.at[0], me.along(nz - 1))

    def first_back(left, right):
        def body(j, _):
            at = rows(j, 256)
            igrad[:, at] += dot(left[...], right[at, :], NT)
            return 0

        lax.fori_loop(0, model // 256, body, 0, unroll=4)

    def filter_back(h, _):
        taps = vec[0:4, lanes(h)]
        fl[h, tokens:tokens + 8] = hal[1, h]
        value = taps[0:1] * fl[h, 0:tokens]
        small[0:1, lanes(h)] = jnp.sum(fl[h, 0:tokens] * lin[h, HALO:], axis=0, keepdims=True)
        for t in range(1, 4):
            value = value + taps[t:t + 1] * (fl[h, t:t + tokens] * mk[:, 3 + t:4 + t])
            small[t:t + 1, lanes(h)] = jnp.sum(
                fl[h, 0:tokens] * (lin[h, HALO - t:HALO - t + tokens] * mk[:, t:t + 1]), axis=0, keepdims=True
            )
        lgr[:, lanes(h)] = value.astype(BF16)
        return 0

    need("fc")
    chain_begin(0, False)
    for i in range(k):
        chain_begin(i, True)
    y_sum.begin()
    small[...] = jnp.zeros(small.shape, F32)
    small[8:9, 0:model] = g2g[...]
    rgb[...] = rgrad[...].astype(BF16)
    need("pr")
    turned[...] = rgb[...].T
    wgrad(0, pr)
    out.go(core_copies[2])
    need("wo", "br", "st")
    lax.fori_loop(0, heads, branch_back, 0, unroll=3)
    need("rl")
    lax.fori_loop(0, heads // 2, scan_head, 0)
    need("y0", "y1")
    y_sum.relay()
    core_sum(2)
    lax.fori_loop(heads // 2, heads, scan_head, 0)
    need("fb")
    turned[...] = fb[HALO:, :].T
    wgrad(1, bg)
    out.go(core_copies[1])
    for d in range(1, nz):
        out.go(end_copy(d), z >= d)
    chain_step(0)
    chain_begin(1, False)
    for d in range(1, nz):
        out.arrived(end_copy(d), z + d < nz)
    incoming = jnp.zeros((1, lru), F32)
    for d in range(nz - 1, 0, -1):
        end = ends[d, 0:1, :] + ends[d, 1:2, :] * incoming
        incoming = jnp.where(d + z < nz, end, incoming)
    inc[...] = incoming
    chain_begin(2, False)
    need("base")
    for half in range(2):
        at = pl.ds(half * (tokens // 2), tokens // 2)
        bout[at, :] = bout[at, :] + y_sum.total(half)
    core_sum(1)
    need("cv", "il")
    lax.fori_loop(0, heads // 3, terms, 0)
    sums[2].relay()
    chain_step(1)
    lax.fori_loop(heads // 3, 2 * heads // 3, terms, 0)
    lax.fori_loop(2 * heads // 3, heads, terms, 0)
    out.go(gate_core)
    gate_core_sum()
    sums[1].relay()
    chain_step(2)
    need("wb")
    igrad[...] = jnp.zeros(igrad.shape, F32)
    first_back(bg, wb)
    feed_total()
    gate_sum.relay()
    out.go(halo)
    need("lin")
    out.arrived(halo)
    lax.fori_loop(0, heads, filter_back, 0, unroll=3)
    need("wl")
    first_back(lgr, wl)
    need("x")
    value = x[...].astype(F32)
    fgrad = igrad[...]
    q = fgrad * vecs[0:1, 0:model]
    inv = lax.rsqrt(jnp.mean(value * value, axis=-1, keepdims=True) + EPS)
    pull = jnp.mean(q * value, axis=-1, keepdims=True)
    small[7:8, 0:model] = jnp.sum(fgrad * value * inv, axis=0, keepdims=True)
    igrad[...] = rgrad[...] + (inv * q - value * (inv * inv * inv * pull))
    out.go(small_copy(0))
    out.sent(core_copies[2])
    wgrad(0, lgr)
    out.go(core_copies[0])
    plane_total(2)
    small_step(0)
    core_sum(0)
    plane_total(1)
    gate_total()
    sums[0].relay()
    feed_gather.relay()
    gate_z_total()
    plane_total(0)
    z_total(1)
    gate_spread()
    small_step(1)
    z_total(2)
    small_step(2)
    gate_gather.relay()
    feed_gather.far()
    z_total(0)
    gathers[2].relay()
    gathers[1].relay()
    gate_gather.far()
    gathers[0].relay()
    gathers[2].far()
    gathers[1].far()
    gathers[0].far()
    for d in range(1, nz):
        out.arrived(small_along(d, lambda: me.z_from(d)))
    total = smz[0]
    for i in range(1, nz):
        total = total + smz[i]
    osm[...] = total
    osmz[...] = osm[:, rows(z, own)]
    for gathered in [feed_gather, gathers[2], gathers[1], gate_gather, gathers[0]]:
        gathered.end()
    feed_own.wait()
    out.finish()


def backward(nz, rg, ig, sin, mk, vec, vecs, rgrad, g2g, x, wl, wb, wo, fb, lin, br, cv, rl, il, st, pr, base, y, ffg):
    tokens, model = x.shape
    heads, width = rg.shape[0], rg.shape[1]
    lru = heads * width
    own = lru // nz
    part = ffg.shape[2]
    k = nz - 1
    block = model // 8
    gate_rows = 2 * lru
    gate_block = gate_rows // 8
    vm = pl.BlockSpec(memory_space=VMEM)
    hbm = pl.BlockSpec(memory_space=pl.ANY)
    by_head = (heads, tokens, width)
    half = tokens // 2
    sems = []
    for shape in (
        (3,), (3, 6), (3, k), (3, 8), (2, k), (8,),
        (1,), (6,), (k,), (k,), (8,), (6,), (3,), (k,), (k,), (1,),
    ):
        sems += [DMA(shape)] * 2
    return pl.pallas_call(
        functools.partial(backward_kernel, nz, heads),
        out_shape=(
            jax.ShapeDtypeStruct((3, model, own), BF16),
            jax.ShapeDtypeStruct((3, 8 * part, model), BF16),
            jax.ShapeDtypeStruct((gate_rows, width), BF16),
            jax.ShapeDtypeStruct((tokens, model), F32),
            jax.ShapeDtypeStruct((tokens, model), F32),
            jax.ShapeDtypeStruct((16, lru), F32),
            jax.ShapeDtypeStruct((16, own), F32),
        ),
        in_specs=[vm] * 8 + [hbm] * 15,
        out_specs=[hbm] * 3 + [vm] * 4,
        scratch_shapes=[
            VMEM((tokens, model), BF16), VMEM((model, lru), BF16), VMEM((model, lru), BF16), VMEM((lru, model), BF16),
            VMEM((HALO + tokens, model), BF16), VMEM((heads, HALO + tokens, width), F32), VMEM(by_head, F32),
            VMEM(by_head, BF16), VMEM(by_head, BF16), VMEM(by_head, BF16), VMEM(by_head, F32), VMEM((tokens, lru), BF16),
            VMEM((2, half, model), BF16),
            VMEM((tokens, model), BF16), VMEM((model, tokens), BF16), VMEM((heads, tokens + 8, width), F32),
            VMEM(by_head, BF16), VMEM(by_head, BF16), VMEM((tokens, lru), BF16), VMEM((tokens, lru), BF16),
            VMEM((nz, 8, lru), F32), VMEM((2, heads, 8, width), F32),
            VMEM((2, model, lru), BF16), VMEM((3, model // 2, lru), BF16), VMEM((3, 6, block // 2, lru), BF16),
            VMEM((3, k, block, own), BF16), VMEM((3, block, own), BF16),
            VMEM((3, nz, part, model), BF16), VMEM((2, k, 3, part, model), BF16), VMEM((3, part, model), BF16),
            VMEM((gate_rows, width), BF16), VMEM((gate_rows // 2, width), BF16), VMEM((6, gate_block // 2, width), BF16),
            VMEM((k, gate_block // nz, width), BF16), VMEM((gate_block, width), BF16),
            VMEM((7, 16, lru), F32), VMEM((nz, 16, lru), F32), VMEM((6, half, model), BF16), VMEM((1, lru), F32),
            DMA((16,)), DMA((5,)),
        ] + sems,
        compiler_params=pltpu.CompilerParams(collective_id=1, has_side_effects=True, vmem_limit_bytes=62 * 2**20),
        name="backward_and_sums",
    )(rg, ig, sin, mk, vec, vecs, rgrad, g2g, x, wl, wb, wo, fb, lin, br, cv, rl, il, st, pr, base, y, ffg)


def results_kernel(wa, fa, ga, gb, bout, igrad, osm, osmz,
                   o_out, o_in, o_g1, o_branch, o_lru, o_taps, o_rate, o_input, o_rb, o_ib, o_decay, o_ow, o_g2, o_gate, o_up, o_down):
    model = bout.shape[1]

    @pl.when(pl.program_id(0) == 0)
    def _():
        o_out[...] = bout[...]
        o_in[...] = igrad[...]
        o_taps[...] = osmz[0:4, :]
        o_decay[...] = osmz[4, :]
        o_rb[...] = osm[5, :]
        o_ib[...] = osm[6, :]
        o_g1[...] = osm[7, 0:model]
        o_g2[...] = osm[8, 0:model]

    o_lru[...] = wa[0].astype(F32)
    o_branch[...] = wa[1].astype(F32)
    o_ow[...] = wa[2].T.astype(F32)
    o_rate[...] = ga[...].astype(F32)
    o_input[...] = gb[...].astype(F32)
    o_gate[...] = fa[0].T.astype(F32)
    o_up[...] = fa[1].T.astype(F32)
    o_down[...] = fa[2].astype(F32)


def results(wa, fa, ga, bout, igrad, osm, osmz):
    steps = 3
    model, own = wa.shape[1:]
    cols = fa.shape[1]
    gate_rows, width = ga.shape[0] // 2, ga.shape[1]
    lru = osm.shape[1]
    tokens = bout.shape[0]

    def whole(shape):
        return pl.BlockSpec(shape, lambda i: (0,) * len(shape))

    across = pl.BlockSpec((model, own // steps), lambda i: (0, i))
    feed_across = pl.BlockSpec((model, cols // steps), lambda i: (0, i))
    outs = [
        ((tokens, model), whole((tokens, model))), ((tokens, model), whole((tokens, model))), ((model,), whole((model,))),
        ((model, own), across), ((model, own), across), ((4, own), whole((4, own))),
        ((gate_rows, width), pl.BlockSpec((gate_rows // steps, width), lambda i: (i, 0))),
        ((gate_rows, width), pl.BlockSpec((gate_rows // steps, width), lambda i: (i, 0))),
        ((lru,), whole((lru,))), ((lru,), whole((lru,))), ((own,), whole((own,))),
        ((own, model), pl.BlockSpec((own // steps, model), lambda i: (i, 0))), ((model,), whole((model,))),
        ((model, cols), feed_across), ((model, cols), feed_across),
        ((cols, model), pl.BlockSpec((cols // steps, model), lambda i: (i, 0))),
    ]
    return pl.pallas_call(
        results_kernel,
        grid=(steps,),
        out_shape=tuple(jax.ShapeDtypeStruct(shape, F32) for shape, _ in outs),
        in_specs=[
            pl.BlockSpec((3, model, own // steps), lambda i: (0, 0, i)),
            pl.BlockSpec((3, cols // steps, model), lambda i: (0, i, 0)),
            pl.BlockSpec((gate_rows // steps, width), lambda i: (i, 0)),
            pl.BlockSpec((gate_rows // steps, width), lambda i: (i + steps, 0)),
            whole((tokens, model)), whole((tokens, model)), whole((16, lru)), whole((16, own)),
        ],
        out_specs=tuple(spec for _, spec in outs),
        compiler_params=pltpu.CompilerParams(vmem_limit_bytes=62 * 2**20),
        name="results",
    )(wa, fa, ga, ga, bout, igrad, osm, osmz)


def local(
    nz,
    groups,
    block_input,
    doc_starts,
    first_gain,
    branch_weight,
    lru_weight,
    filter_taps,
    rate_gate,
    input_gate,
    rate_bias,
    input_bias,
    decay_logit,
    out_weight,
    second_gain,
    feed_gate,
    feed_up,
    feed_down,
    cotangent,
):
    model = block_input.shape[1]
    heads, width = rate_gate.shape[:2]
    lru = heads * width

    (wl, wb, wo, fb, lin, br, cv, rl, il, st, pr, y, ffg, sin, mk, vec, base, rgrad, g2g, vecs) = forward(
        nz, block_input, first_gain, second_gain, rate_bias, input_bias, doc_starts, filter_taps, decay_logit, rate_gate,
        input_gate, cotangent, lru_weight, branch_weight, out_weight,
        feed_gate, feed_up, feed_down,
    )
    sums = backward(
        nz, rate_gate, input_gate, sin, mk, vec, vecs, rgrad, g2g, block_input, wl, wb, wo, fb, lin, br, cv, rl, il, st, pr,
        base, y, ffg,
    )
    made = results(*sums)
    block_output, input_grad, *summed = made
    if groups > 1:
        same = [[8 * g + b for g in range(groups)] for b in range(8)]
        summed = lax.psum(tuple(summed), "tp", axis_index_groups=same)
    g1, branch, lru_grad, taps, rate, inputs, rb, ib, decay, ow, g2, gate, up, down = summed
    rate, inputs = rate.reshape(heads, width, width), inputs.reshape(heads, width, width)
    return (
        block_output, input_grad, g1, branch, lru_grad, taps, rate, inputs, rb, ib, decay, ow, g2,
        gate, up, down,
    )


def solution(mesh):
    by_rows = P(("tp", "dp"), None)
    by_cols = P(None, "dp")
    split = P("dp", None)
    return jax.shard_map(
        functools.partial(local, mesh.shape["dp"], mesh.shape["tp"] // 8),
        mesh=mesh,
        in_specs=(
            by_rows, P("tp"), P(), by_cols, by_cols, by_cols, P(), P(), P(), P(), P("dp"), split, P(), by_cols, by_cols,
            split, by_rows,
        ),
        out_specs=(
            by_rows, by_rows, P(), by_cols, by_cols, by_cols, P(), P(), P(), P(), P("dp"), split, P(), by_cols, by_cols,
            split,
        ),
        check_vma=False,
    )
```

```python
import functools
import math

import jax
import jax.numpy as jnp
from jax import lax
from jax.experimental import pallas as pl
from jax.experimental.pallas import tpu as pltpu
from jax.sharding import PartitionSpec as P

EPS = 1e-06
DECAY_SCALE = 8.0
F32 = jnp.float32
BF16 = jnp.bfloat16
MESH = pl.DeviceIdType.MESH
VMEM = pltpu.VMEM
DMA = pltpu.SemaphoreType.DMA
NN = (((1,), (0,)), ((), ()))
NT = (((1,), (1,)), ((), ()))
TN = (((0,), (0,)), ((), ()))
HALO = 16
LANE = 128
GELU_A = math.sqrt(2.0 / math.pi)
GELU_B = 0.044715


def dot(left, right, form):
    return lax.dot_general(left, right, form, preferred_element_type=F32)


def sigmoid(v):
    return 1.0 / (1.0 + jnp.exp(-v))


def softplus(v):
    return jnp.maximum(v, 0.0) + jnp.log1p(jnp.exp(-jnp.abs(v)))


def gelu_both(v):
    square = v * v
    tanh = jnp.tanh(GELU_A * v * (1.0 + GELU_B * square))
    half = 0.5 * (1.0 + tanh)
    slope = half + 0.5 * v * (1.0 - tanh * tanh) * (GELU_A * (1.0 + 3.0 * GELU_B * square))
    return v * half, slope


def gelu_only(v):
    return v * (0.5 * (1.0 + jnp.tanh(GELU_A * v * (1.0 + GELU_B * v * v))))


class Place:
    def __init__(self, nz):
        self.nz = nz
        self.t = lax.axis_index("tp")
        self.z = lax.axis_index("dp")
        self.b = lax.rem(self.t, 8)
        self.core = lax.rem(self.t, 2)
        self.x = lax.rem(self.t // 2, 2)
        self.y = lax.rem(self.t // 4, 2)
        self.chip = self.b // 2

    def flip(self, r):
        t = self.t
        if r & 1:
            t = t + 2 - 4 * self.x
        if r & 2:
            t = t + 4 - 8 * self.y
        return t

    def chip_of(self, r):
        c = self.chip
        if r & 1:
            c = c + 1 - 2 * self.x
        if r & 2:
            c = c + 2 - 4 * self.y
        return c

    def plane(self, r):
        return (self.flip(r), self.z)

    def sibling(self):
        return (self.t + 1 - 2 * self.core, self.z)

    def along(self, d):
        return (self.t, lax.rem(self.z + d, self.nz))

    def z_from(self, d):
        return lax.rem(self.z + self.nz - d, self.nz)


def greet(peers):
    barrier = pltpu.get_barrier_semaphore()
    for peer in peers:
        pl.semaphore_signal(barrier, inc=1, device_id=peer, device_id_type=MESH)
    pl.semaphore_wait(barrier, len(peers))


def remote(src, dst, send, recv, peer):
    return pltpu.make_async_remote_copy(
        src_ref=src, dst_ref=dst, send_sem=send, recv_sem=recv, device_id=peer, device_id_type=MESH
    )


class Sends:
    def __init__(self):
        self.started = []

    def when(self, cond, action):
        if cond is None:
            action()
        else:
            pl.when(cond)(action)

    def go(self, make, cond=None):
        self.when(cond, lambda: make().start())
        self.started.append((cond, make))

    def start_if(self, cond, make):
        pl.when(cond)(lambda: make().start())
        self.started.append((None, make))

    def arrived(self, make, cond=None):
        self.when(cond, lambda: make().wait_recv())

    def sent(self, make):
        make().wait_send()
        self.started = [(cond, other) for cond, other in self.started if other is not make]

    def finish(self):
        for cond, make in self.started:
            self.when(cond, lambda: make().wait_send())


class PlaneGather:
    def __init__(self, me, out, piece, send, recv, at, cond=None, first=None, joined=None, ready=None):
        self.me, self.out, self.piece, self.cond, self.joined = me, out, piece, cond, joined
        self.send, self.recv, self.at, self.first, self.ready = send, recv, at, first, ready

    def copy(self, i, src, dst, peer):
        return remote(src, dst, self.send.at[self.at + (i,)], self.recv.at[self.at + (i,)], peer)

    def whole(self, i, r, peer, first=False):
        def make():
            place = self.piece(self.me.chip_of(r), self.me.core, None)
            return self.copy(i, self.first() if first and self.first else place, place, peer)
        return make

    def half(self, i, r, part, peer):
        def make():
            place = self.piece(self.me.chip_of(r), self.me.core, part)
            return self.copy(i, place, place, peer)
        return make

    def across(self, core):
        def make():
            place = self.joined(core)
            return self.copy(4, place, place, self.me.sibling())
        return make

    def begin(self):
        for i, r in ((0, 1), (1, 2)):
            self.out.go(self.whole(i, 0, self.me.plane(r), True), self.cond)
        if not self.joined:
            self.out.go(self.whole(4, 0, self.me.sibling(), True), self.cond)

    def relay(self):
        me = self.me
        for i, r, part in ((0, 1, 0), (1, 2, 1)):
            self.out.arrived(self.whole(i, r, me.plane(r)), self.cond)
            self.out.go(self.half(2 + i, r, part, me.plane(3 - r)), self.cond)
            if not self.joined:
                self.out.go(self.whole(4 + r, r, me.sibling()), self.cond)

    def far(self):
        for part in (0, 1):
            self.out.arrived(self.half(2 + part, 3, part, self.me.plane(2 - part)), self.cond)
        if self.joined:
            if self.ready:
                self.ready()
            self.out.go(self.across(self.me.core), self.cond)
        else:
            self.out.go(self.whole(7, 3, self.me.sibling()), self.cond)

    def end(self):
        me = self.me
        if self.joined:
            self.out.arrived(self.across(1 - me.core), self.cond)
            return
        for r in range(4):
            def make(r=r):
                place = self.piece(me.chip_of(r), 1 - me.core, None)
                return self.copy(4 + r, place, place, me.sibling())
            self.out.arrived(make, self.cond)


class PlaneSum:
    def __init__(self, me, out, block, recv, send_sem, recv_sem, at, source=None):
        self.me, self.out, self.block, self.got = me, out, block, recv
        self.send_sem, self.recv_sem, self.at = send_sem, recv_sem, at
        self.source = source or block
        self.near = {r: me.plane(r) for r in (1, 2)}

    def copy(self, i, src, peer):
        def make():
            return remote(
                src(), self.got(i), self.send_sem.at[self.at + (i,)], self.recv_sem.at[self.at + (i,)], peer
            )
        return make

    def put(self, i, cond=None):
        half = i // 2
        to = 3 if i % 2 else half + 1
        make = self.copy(i, lambda: self.source(to, half), self.near[half + 1])
        if cond is None:
            self.out.go(make)
        else:
            self.out.start_if(cond, make)

    def begin(self):
        for i in (1, 0, 3, 2):
            self.put(i)

    def wait(self, i):
        self.out.arrived(self.copy(i, lambda: self.got(i), self.me.plane(1)))

    def relay(self):
        for half, r in ((0, 2), (1, 1)):
            self.wait(2 * half + 1)
            mine = self.block(r, half)
            mine[...] = (mine[...].astype(F32) + self.got(2 * half + 1)[...].astype(F32)).astype(BF16)
            self.out.go(self.copy(4 + half, lambda r=r, half=half: self.block(r, half), self.me.plane(r)))

    def total(self, half):
        self.wait(2 * half)
        self.wait(4 + half)
        return self.got(2 * half)[...].astype(F32) + self.got(4 + half)[...].astype(F32)


def rows(i, size):
    return pl.ds(pl.multiple_of(i * size, size), size)


def rms(v, gain):
    return v * lax.rsqrt(jnp.mean(v * v, axis=-1, keepdims=True) + EPS) * gain


def head_lanes(h, width):
    return pl.ds(pl.multiple_of(h * width, width), width)


def tile_scan(a, b, row, back):
    for step in (1, 2, 4):
        if back:
            seen = row < 8 - step
            shift = 8 - step
        else:
            seen = row >= step
            shift = step
        b_before = jnp.where(seen, pltpu.roll(b, shift, 0), 0.0)
        a_before = jnp.where(seen, pltpu.roll(a, shift, 0), 1.0)
        b = b + a * b_before
        a = a * a_before
    return a, b


def forward_kernel(nz, heads, i_gain1, i_gain2, i_bias1, i_bias2, i_starts, i_taps, i_dlogit, i_x, i_rg, i_ig, cot, lw, bw, ow, fgate, fup, fdown,
                   o_wl, o_wb, o_wo, o_fb, o_lin, o_br, o_cv, o_rl, o_il, o_st, o_pr, o_y, o_wg, o_base, o_rgrad,
                   o_sin, o_mk, o_vec, o_g2g, o_vecs,
                   gain1, gain2, bias1, bias2, starts, taps_in, dlogit, sin, mk, vec, g2g, vecs,
                   x, rg, ig, base, rgrad, wl, wb, wo, f, cots, win, turned, fb, lin, br, cv, rl, il, st, pr, pst, ends, ms, hx,
                   res, s, h, lg, ug, ybuf, sbuf, srecv, sown, fc, acts, slopes, yp,
                   lsem, osem, zs, zr, ps, pr_sem, fcs, fcr, qs, qr, vs, vr, es, er, hs, hr, ss, sr, gs, gr, ks, kr, ys, yr):
    me = Place(nz)
    out, feeds = Sends(), Sends()
    tokens, model = x.shape
    lru = wl.shape[1]
    width = lru // heads
    own = lru // nz
    cols = f.shape[1]
    part = cols // (2 * nz)
    piece_rows = model // 8
    chunk = 256
    z = me.z

    window = pl.ds(pl.multiple_of((me.chip // 2) * (4 * part) + lax.rem(me.chip, 2) * LANE, LANE), 256)
    shift = 64 * lax.rem(me.chip, 2)
    mine = rows(z, own)
    local = [
        (fgate.at[:, window], win.at[0]),
        (fup.at[:, window], win.at[1]),
        (lw, wl.at[:, mine]),
        (bw, wb.at[:, mine]),
        (ow, wo.at[mine]),
        (fdown.at[rows(me.chip, 2 * part)], f.at[2, rows(z, 2 * part)]),
        (cot, cots.at[0]),
    ]
    local = [pltpu.make_async_copy(a, b, lsem.at[i]) for i, (a, b) in enumerate(local)]
    vectors = (
        (i_gain1, gain1), (i_gain2, gain2), (i_bias1, bias1), (i_bias2, bias2), (i_starts, starts), (i_taps, taps_in),
        (i_dlogit, dlogit),
    )
    vectors = [pltpu.make_async_copy(a, b, lsem.at[11 + i]) for i, (a, b) in enumerate(vectors)]
    more = [pltpu.make_async_copy(a, b, lsem.at[8 + i]) for i, (a, b) in enumerate(((i_x, x), (i_rg, rg), (i_ig, ig)))]
    for copy in vectors + more[:1] + local + more[1:]:
        copy.start()
    greet([me.along(d) for d in range(1, nz)] + [me.plane(r) for r in (1, 2, 3)] + [me.sibling()])
    for copy in vectors:
        copy.wait()
    vecs[...] = jnp.zeros(vecs.shape, F32)
    for i, v in enumerate((gain1, gain2, bias1, bias2, starts)):
        vecs[i:i + 1, 0:v.shape[0]] = v[...].astype(F32).reshape(1, v.shape[0])
    vecs[8:12, 0:own] = taps_in[...].astype(F32)
    vecs[12:13, 0:own] = dlogit[...].astype(F32).reshape(1, own)

    def vector(d, origin):
        def make():
            place = vec.at[:, rows(origin(), own)]
            return remote(vecs.at[8:16, 0:own], place, vs.at[d - 1], vr.at[d - 1], me.along(d))
        return make

    def halo():
        return remote(i_x.at[tokens - HALO:tokens], hx, hs.at[0], hr.at[0], me.along(1))

    out.go(halo)
    for d in range(1, nz):
        out.go(vector(d, lambda: z))

    mine_of = 4 * me.core + me.chip

    def slot(m, zz, b):
        if m < 2:
            return (wl, wb)[m].at[rows(b, piece_rows), rows(zz, own)]
        if m == 2:
            return wo.at[rows(zz, own), rows(b, LANE)]
        at = pl.ds(pl.multiple_of(zz * (2 * part) + me.core * part, part), part)
        return f.at[0:2, at] if m == 3 else f.at[2, at]

    def source(m):
        if m < 2:
            return (lw, bw)[m].at[rows(mine_of, piece_rows)]
        if m == 2:
            return ow.at[:, rows(mine_of, LANE)]
        if m == 3:
            return turned.at[:, pl.ds(pl.multiple_of(shift + me.core * part, 32), part)]
        return fdown.at[pl.ds(pl.multiple_of(me.chip * (2 * part) + me.core * part, part), part)]

    def origin(hop, right):
        return z - 1 - hop if right else z + 1 + hop

    def has(hop, right):
        return z - 1 - hop >= 0 if right else z + 1 + hop < nz

    def along(m, hop, right, from_me):
        def make():
            step = 1 if right else -1
            zz = z - step * hop if from_me else origin(hop, right)
            place = slot(m, zz, mine_of)
            src = source(m) if from_me and hop == 0 else place
            at = (m, hop, int(right))
            peer = (me.t, z + step if from_me else z)
            return remote(src, place, zs.at[at], zr.at[at], peer)
        return make

    def z_begin(m, hop=0):
        for right in (True, False):
            there = z + 1 < nz if right else z >= 1
            if hop:
                there = jnp.logical_and(there, has(hop - 1, right))
            (out if m < 3 else feeds).go(along(m, hop, right, True), there)

    gathers = {}
    for m in range(3):
        for hop in range(nz - 1):
            for right in (True, False):
                def place(chip, core, half, m=m, hop=hop, right=right):
                    zz, b = origin(hop, right), 4 * core + chip
                    if half is None:
                        return slot(m, zz, b)
                    if m < 2:
                        at = pl.ds(pl.multiple_of(b * piece_rows + half * (piece_rows // 2), piece_rows // 2), piece_rows // 2)
                        return (wl, wb)[m].at[at, rows(zz, own)]
                    at = pl.ds(pl.multiple_of(zz * own + half * (own // 2), own // 2), own // 2)
                    return wo.at[at, rows(b, LANE)]

                def joined(core, m=m, hop=hop, right=right):
                    zz = origin(hop, right)
                    if m < 2:
                        return (wl, wb)[m].at[rows(core, 4 * piece_rows), rows(zz, own)]
                    return wo.at[rows(zz, own), rows(core, 4 * LANE)]

                gathers[m, hop, right] = PlaneGather(
                    me, out, place, ps, pr_sem, (m, 2 * hop + int(right)), has(hop, right), joined=joined
                )

    def share(m, hop, right, from_me):
        def make():
            at = (m - 3, 2 * hop + int(right))
            place = slot(m, origin(hop, right), mine_of)
            if not from_me:
                other = pl.ds(pl.multiple_of(origin(hop, right) * (2 * part) + (1 - me.core) * part, part), part)
                place = f.at[0:2, other] if m == 3 else f.at[2, other]
            return remote(place, place, fcs.at[at], fcr.at[at], me.sibling())
        return make

    def z_step(m, hop):
        for right in (True, False):
            out.arrived(along(m, hop, right, False), has(hop, right))
        if hop + 1 < nz - 1:
            z_begin(m, hop + 1)
        for right in (True, False):
            if m < 3:
                gathers[m, hop, right].begin()
            else:
                feeds.go(share(m, hop, right, True), has(hop, right))

    def relay(m, hop):
        for right in (True, False):
            gathers[m, hop, right].relay()

    def far(m, hop):
        for right in (True, False):
            gathers[m, hop, right].far()

    def all_of(m):
        for hop in range(nz - 1):
            for right in (True, False):
                gathers[m, hop, right].end()

    half = tokens // 2

    def cot_whole(i, r, part_of):
        at = pl.ds(part_of * half, half)
        return lambda: remote(cot.at[at], cots.at[r, at], qs.at[2 * part_of + i], qr.at[2 * part_of + i], me.plane(r))

    def cot_part(part_of, r):
        at = pl.ds(part_of * half, half)
        return lambda: remote(cots.at[r, at], cots.at[3, at], qs.at[4 + part_of], qr.at[4 + part_of], me.plane(3 - r))

    def lanes(h):
        return head_lanes(h, width)

    def project(h, _):
        lin[h] = dot(fb[...], wl[:, lanes(h)], NN)
        taps = vec[0:4, lanes(h)]
        conv = taps[0:1] * lin[h, HALO:, :]
        for k in range(1, 4):
            conv = conv + taps[k:k + 1] * lin[h, HALO - k:HALO - k + tokens, :] * mk[:, k:k + 1]
        conv = conv.astype(BF16)
        cv[h] = conv
        rl[h] = (dot(conv, rg[h], NN) + vecs[2:3, lanes(h)]).astype(BF16)
        il[h] = (dot(conv, ig[h], NN) + vecs[3:4, lanes(h)]).astype(BF16)
        return 0

    row = lax.broadcasted_iota(jnp.int32, (8, width), 0)

    def scan_head(h, _):
        rate = softplus(-vec[4:5, lanes(h)]) * -DECAY_SCALE

        def tile(i, carried):
            state, factor = carried
            at = rows(i, 16)
            start = mk[at, 0:1]
            keep = 1.0 - start
            decay = jnp.exp(sigmoid(rl[h, at, :].astype(F32)) * rate)
            a = keep * decay
            scale = (start + keep * jnp.sqrt(1.0 - decay * decay)) * sigmoid(il[h, at, :].astype(F32))
            b = scale * cv[h, at, :].astype(F32)
            for t in range(2):
                cum, run = tile_scan(a[8 * t:8 * t + 8], b[8 * t:8 * t + 8], row, False)
                run = run + cum * state
                cum = cum * factor
                here = pl.ds(pl.multiple_of(i * 16 + 8 * t, 8), 8)
                st[h, here, :] = run
                pst[h, here, :] = cum
                state, factor = run[7:8], cum[7:8]
            return state, factor

        state, factor = lax.fori_loop(
            0, tokens // 16, tile, (jnp.zeros((1, width), F32), jnp.ones((1, width), F32)), unroll=4
        )
        ends[0, 0:1, lanes(h)] = state
        ends[0, 1:2, lanes(h)] = factor
        return 0

    def end_copy(d):
        return lambda: remote(ends.at[0], ends.at[d], es.at[d - 1], er.at[d - 1], me.along(d))

    def branch(h, _):
        br[h] = dot(fb[HALO:], wb[:, lanes(h)], NN)
        return 0

    def finish(h, _):
        state = st[h] + pst[h] * sin[:, lanes(h)]
        st[h] = state
        pr[:, lanes(h)] = (state * gelu_only(br[h])).astype(BF16)
        return 0

    def project_out(j, _):
        at = rows(j, chunk)
        res[:, at] = x[:, at].astype(F32) + dot(pr[...], wo[:, at], NN)
        return 0

    def second_copy(r):
        return lambda: remote(s.at[0:tokens], s.at[r * tokens:(r + 1) * tokens], ss.at[r - 1], sr.at[r - 1], me.plane(r))

    def second_part(part_of, r):
        at, to = (pl.ds(q * tokens + part_of * half, half) for q in (r, 3))
        return lambda: remote(s.at[at], s.at[to], ss.at[2 + part_of], sr.at[2 + part_of], me.plane(3 - r))

    saved = [
        (wl, o_wl), (wb, o_wb), (wo, o_wo), (fb, o_fb), (lin, o_lin), (br, o_br), (cv, o_cv), (rl, o_rl), (il, o_il),
        (st, o_st), (pr, o_pr), (sin, o_sin), (mk, o_mk), (vec, o_vec), (vecs, o_vecs),
    ]
    saved = [pltpu.make_async_copy(a, b, osem.at[i]) for i, (a, b) in enumerate(saved)]
    grad_sum = PlaneSum(
        me, out, lambda r, part: sbuf.at[r, pl.ds(part * half, half)], lambda i: srecv.at[i], gs, gr, ()
    )
    def feed_ahead(r):
        at = rows(r, tokens)

        def hidden_of(j, _):
            here = rows(j, chunk)
            second = s[at]
            act, slope = gelu_both(dot(second, f[0, here, :], NT))
            up = dot(second, f[1, here, :], NT)
            h[at, here] = (act * up).astype(BF16)
            acts[at, here] = act
            slopes[at, here] = up * slope
            return 0

        lax.fori_loop(0, cols // chunk, hidden_of, 0, unroll=3)

    def feed_back(r):
        at = rows(r, tokens)

        def grads_of(j, _):
            here = rows(j, chunk)
            hg = dot(cots[r], f[2, here, :], NT)
            lg[at, here] = (hg * slopes[at, here]).astype(BF16)
            ug[at, here] = (hg * acts[at, here]).astype(BF16)
            return 0

        lax.fori_loop(0, cols // chunk, grads_of, 0, unroll=3)

        def back_of(j, _):
            here = rows(j, chunk)
            value = dot(lg[at], f[0, :, here], NN) + dot(ug[at], f[1, :, here], NN)
            sbuf[r, :, here] = value.astype(BF16)
            return 0

        lax.fori_loop(0, model // chunk, back_of, 0, unroll=4)

    def near_ahead(r, _):
        feed_ahead(r)
        return 0

    def near_back(r, _):
        feed_back(r)
        grad_sum.put(0, r == 1)
        grad_sum.put(2, r == 2)
        return 0

    def far_ahead(i, _):
        feed_ahead(3 - 3 * i)
        return 0

    def far_back(i, _):
        feed_back(3 - 3 * i)
        for piece in (1, 3):
            grad_sum.put(piece, i == 0)
        return 0

    def out_of(j, _):
        here = rows(j, chunk)
        for r in range(4):
            value = dot(h[r * tokens:(r + 1) * tokens], f[2, :, here], NN)
            if r:
                ybuf[r - 1, :, here] = value.astype(BF16)
            else:
                base[:, here] = res[:, here] + value
        return 0

    def feed_half(zz, core):
        return pl.ds(pl.multiple_of(zz * (2 * part) + core * part, part), part)

    def core_copy(m, zz):
        at = (m, zz)
        return lambda: remote(f.at[m, feed_half(zz, 1 - me.core)], fc.at[m, zz], ks.at[at], kr.at[at], me.sibling())

    def feed_wgrad(m, left):
        def body(i, _):
            here = rows(i, chunk)
            right = jnp.concatenate([cots[r, :, here] for r in range(4)], axis=0) if m == 2 else s[:, here]
            for j in range(cols // chunk):
                f[m, pl.ds(j * chunk, chunk), here] = dot(left[:, j * chunk:(j + 1) * chunk], right, TN).astype(BF16)
            return 0

        lax.fori_loop(0, model // chunk, body, 0)
        for zz in range(nz):
            out.go(core_copy(m, zz))

    last = [
        pltpu.make_async_copy(a, b, osem.at[15 + i])
        for i, (a, b) in enumerate((
            (ybuf, o_y), (base, o_base), (fc, o_wg), (rgrad, o_rgrad), (g2g, o_g2g),
        ))
    ]
    y_sum = PlaneSum(
        me, out, lambda r, part_of: ybuf.at[r - 1, pl.ds(part_of * half, half)], lambda i: yp.at[i // 2], ys, yr, ()
    )
    own_turned = pltpu.make_async_copy(
        turned.at[:, pl.ds(pl.multiple_of(shift, 32), 2 * part)], f.at[0:2, rows(z, 2 * part)], lsem.at[7]
    )
    g1, g2 = vecs[0:1, 0:model], vecs[1:2, 0:model]
    start_row = vecs[4:5, 0:nz * tokens]

    z_begin(0)
    for i, r in ((0, 1), (1, 2)):
        out.go(cot_whole(i, r, 0))
    for d in range(1, nz):
        out.arrived(vector(d, lambda: me.z_from(d)))
    vec[:, mine] = vecs[8:16, 0:own]
    for copy in local[2:] + more[1:]:
        copy.wait()
    z_begin(1)
    out.arrived(halo)
    fb[0:HALO] = rms(hx[...].astype(F32), g1).astype(BF16)
    z_step(0, 0)
    z_begin(2)
    z_step(0, 1)
    z_step(1, 0)
    z_step(0, 2)
    z_step(1, 1)
    z_step(1, 2)
    length = nz * tokens
    lane = lax.broadcasted_iota(jnp.int32, (1, length), 1)
    keep_row = 1.0 - start_row
    valid = keep_row
    lines, later_lines = [start_row, valid], []
    for k in range(1, 4):
        if k > 1:
            valid = valid * jnp.where(lane >= k - 1, pltpu.roll(keep_row, k - 1, 1), 0.0)
            lines.append(valid)
        later_lines.append(jnp.where(lane < length - k, pltpu.roll(valid, length - k, 1), 0.0))
    ms[...] = jnp.concatenate(lines + later_lines + [jnp.zeros_like(start_row)], axis=0)
    mk[...] = jnp.concatenate([ms[:, rows(z, tokens)], jnp.zeros((LANE - 8, tokens), F32)], axis=0).T
    relay(0, 1)
    relay(0, 0)
    z_step(2, 0)
    relay(0, 2)
    for i in range(2):
        local[i].wait()
        turned[i] = win[i].T
    own_turned.start()
    more[0].wait()
    fb[HALO:] = rms(x[...].astype(F32), g1).astype(BF16)
    z_begin(3)
    far(0, 1)
    relay(1, 1)
    z_step(2, 1)
    z_begin(4)
    relay(1, 0)
    far(0, 2)
    relay(1, 2)
    far(0, 0)
    z_step(3, 0)
    for i, r in ((0, 1), (1, 2)):
        out.go(cot_whole(i, r, 1))
    all_of(0)
    lax.fori_loop(0, heads // 3, project, 0, unroll=2)
    z_step(2, 2)
    relay(2, 0)
    lax.fori_loop(heads // 3, heads, project, 0, unroll=2)
    far(1, 1)
    far(1, 0)
    relay(2, 1)
    far(1, 2)
    lax.fori_loop(0, 2 * heads // 3, scan_head, 0)
    lax.fori_loop(2 * heads // 3, heads, scan_head, 0)
    all_of(1)
    for d in range(1, nz):
        out.go(end_copy(d), z + d < nz)
    relay(2, 2)
    far(2, 0)
    for part_of in range(2):
        out.arrived(cot_whole(0, 1, part_of))
    out.go(cot_part(0, 1))
    z_step(4, 0)
    lax.fori_loop(0, heads, branch, 0, unroll=2)
    for part_of in range(2):
        out.arrived(cot_whole(1, 2, part_of))
    out.go(cot_part(1, 2))
    far(2, 1)
    far(2, 2)
    for d in range(1, nz):
        out.arrived(end_copy(d), z >= d)
    incoming = jnp.zeros((1, lru), F32)
    for d in range(nz - 1, 0, -1):
        end = ends[d, 0:1, :] + ends[d, 1:2, :] * incoming
        incoming = jnp.where(d <= z, end, incoming)
    sin[...] = incoming

    all_of(2)
    lax.fori_loop(0, heads, finish, 0, unroll=2)
    lax.fori_loop(0, model // chunk, project_out, 0)
    s[0:tokens] = rms(res[...], g2).astype(BF16)
    for r in (1, 2):
        out.go(second_copy(r))
    for copy in saved:
        copy.start()
    z_step(3, 1)
    z_step(4, 1)
    z_step(3, 2)
    for part_of, r in ((0, 2), (1, 1)):
        out.arrived(cot_part(part_of, r))
    out.arrived(second_copy(2))
    out.go(second_part(1, 2))
    out.arrived(second_copy(1))
    out.go(second_part(0, 1))
    for hop in range(nz - 1):
        for right in (True, False):
            out.arrived(share(3, hop, right, False), has(hop, right))
    own_turned.wait()
    lax.fori_loop(1, 3, near_ahead, 0)
    z_step(4, 2)
    for hop in range(nz - 1):
        for right in (True, False):
            out.arrived(share(4, hop, right, False), has(hop, right))
    lax.fori_loop(1, 3, near_back, 0)
    for part_of, near in ((0, 2), (1, 1)):
        out.arrived(second_part(part_of, near))
    lax.fori_loop(0, 2, far_ahead, 0)
    lax.fori_loop(0, 2, far_back, 0)
    feeds.finish()
    feed_wgrad(0, lg)
    lax.fori_loop(0, model // chunk, out_of, 0)
    last[0].start()
    y_sum.put(0)
    y_sum.put(2)
    grad_sum.relay()
    feed_wgrad(1, ug)
    feed_wgrad(2, h)
    for zz in range(nz):
        out.arrived(core_copy(1, zz))
        fc[1, zz] = (fc[1, zz].astype(F32) + f[1, feed_half(zz, me.core), :].astype(F32)).astype(BF16)
    for part_of in range(2):
        at = pl.ds(part_of * half, half)
        y_sum.wait(2 * part_of)
        base[at, :] = base[at, :] + yp[part_of].astype(F32)
    last[1].start()
    for part_of in range(2):
        at = pl.ds(part_of * half, half)
        sown[at, :] = sbuf[0, at, :].astype(F32) + grad_sum.total(part_of)
    sg = sown[...]
    value = res[...]
    q = sg * g2
    inv = lax.rsqrt(jnp.mean(value * value, axis=-1, keepdims=True) + EPS)
    pull = jnp.mean(q * value, axis=-1, keepdims=True)
    rgrad[...] = cots[0].astype(F32) + (inv * q - value * (inv * inv * inv * pull))
    g2g[...] = jnp.sum(sg * value * inv, axis=0, keepdims=True)
    last[3].start()
    last[4].start()
    for zz in range(nz):
        out.arrived(core_copy(2, zz))
        fc[2, zz] = (fc[2, zz].astype(F32) + f[2, feed_half(zz, me.core), :].astype(F32)).astype(BF16)
    for zz in range(nz):
        out.arrived(core_copy(0, zz))
        fc[0, zz] = (fc[0, zz].astype(F32) + f[0, feed_half(zz, me.core), :].astype(F32)).astype(BF16)
    last[2].start()
    for copy in saved + last:
        copy.wait()
    out.finish()


def forward(nz, gain1, gain2, bias1, bias2, starts, taps, dlogit, x, rg, ig, cot, lw, bw, ow, fgate, fup, fdown):
    tokens, model = x.shape
    heads, width = rg.shape[0], rg.shape[1]
    lru = heads * width
    cols = fgate.shape[1]
    k = nz - 1
    hbm = pl.BlockSpec(memory_space=pl.ANY)
    by_head = (heads, tokens, width)
    saved = [
        ((model, lru), BF16), ((model, lru), BF16), ((lru, model), BF16), ((HALO + tokens, model), BF16),
        ((heads, HALO + tokens, width), F32), (by_head, F32), (by_head, BF16), (by_head, BF16), (by_head, BF16),
        (by_head, F32), ((tokens, lru), BF16), ((3, tokens, model), BF16), ((3, nz, cols // (2 * nz), model), BF16),
        ((tokens, model), F32), ((tokens, model), F32),
    ]
    kept = [((1, lru), F32), ((tokens, LANE), F32), ((8, lru), F32), ((1, model), F32), ((16, lru), F32)]
    sems = []
    for shape in ((5, k, 2), (3, 2 * k, 5), (2, 2 * k), (6,), (k,), (k,), (1,), (4,), (6,), (3, nz), (3,)):
        sems += [DMA(shape)] * 2
    return pl.pallas_call(
        functools.partial(forward_kernel, nz, heads),
        out_shape=tuple(jax.ShapeDtypeStruct(*a) for a in saved + kept),
        in_specs=[hbm] * 17,
        out_specs=[hbm] * (len(saved) + len(kept)),
        scratch_shapes=[VMEM(v.shape, v.dtype) for v in (gain1, gain2, bias1, bias2, starts, taps, dlogit)]
        + [VMEM(*a) for a in kept]
        + [
            VMEM((tokens, model), BF16), VMEM((heads, width, width), BF16), VMEM((heads, width, width), BF16),
            VMEM((tokens, model), F32), VMEM((tokens, model), F32), VMEM((model, lru), BF16), VMEM((model, lru), BF16), VMEM((lru, model), BF16), VMEM((3, cols, model), BF16),
            VMEM((4, tokens, model), BF16), VMEM((2, model, 256), BF16), VMEM((2, 256, model), BF16),
            VMEM((HALO + tokens, model), BF16), VMEM((heads, HALO + tokens, width), F32), VMEM(by_head, F32),
            VMEM(by_head, BF16), VMEM(by_head, BF16), VMEM(by_head, BF16), VMEM(by_head, F32), VMEM((tokens, lru), BF16),
            VMEM(by_head, F32), VMEM((nz, 8, lru), F32), VMEM((8, nz * tokens), F32), VMEM((HALO, model), BF16),
            VMEM((tokens, model), F32), VMEM((4 * tokens, model), BF16), VMEM((4 * tokens, cols), BF16),
            VMEM((4 * tokens, cols), BF16), VMEM((4 * tokens, cols), BF16), VMEM((3, tokens, model), BF16),
            VMEM((4, tokens, model), BF16), VMEM((6, tokens // 2, model), BF16), VMEM((tokens, model), F32), VMEM((3, nz, cols // (2 * nz), model), BF16),
            VMEM((4 * tokens, cols), F32), VMEM((4 * tokens, cols), F32),
            VMEM((2, tokens // 2, model), BF16),
            DMA((18,)), DMA((len(saved) + len(kept),)),
        ] + sems,
        compiler_params=pltpu.CompilerParams(collective_id=0, has_side_effects=True, vmem_limit_bytes=62 * 2**20),
        name="forward_and_feed",
    )(gain1, gain2, bias1, bias2, starts, taps, dlogit, x, rg, ig, cot, lw, bw, ow, fgate, fup, fdown)


def backward_kernel(nz, heads, i_sin, i_mk, i_vec, i_vecs, i_g2g,
                    i_rg, i_ig, i_rgrad, i_x, i_wl, i_wb, i_wo, i_fb, i_lin, i_br, i_cv, i_rl, i_il, i_st, i_pr, i_base, i_y, i_ffg,
                    wa, fa, ga, o_bout, o_igrad, o_osm, o_osmz,
                    sin, mk, vec, vecs, g2g, osm, osmz, rg, ig, rgrad, bout, igrad, x, wl, wb, wo, fb, lin, br, cv, rl, il, st, pr, yk,
                    rgb, turned, fl, rlg, ilg, bg, lgr, ends, hal,
                    g, wc, wp, wz, fin, fc, fz, ffin, gt, gc, gp, gz, gfin, sm, smz, yp, inc,
                    lsem, osem, wcs, wcr, wps, wpr, wzs, wzr, was, war, fzs, fzr, fas, far,
                    gcs, gcr, gps, gpr, gzs, gzr, gys, gyr, gas, gar, yps, ypr, s1s, s1r, s2s, s2r,
                    es, er, hs, hr):
    me = Place(nz)
    out = Sends()
    core, other, chip, z = me.core, 1 - me.core, me.chip, me.z
    tokens, model = x.shape
    lru = wl.shape[1]
    width = lru // heads
    own = lru // nz
    block = model // 8
    half_rows = block // 2
    part = fc.shape[2]
    k = nz - 1

    loads = dict(
        rgrad=(i_rgrad, rgrad), g2g=(i_g2g, g2g), vec=(i_vec, vec), mk=(i_mk, mk), sin=(i_sin, sin), vecs=(i_vecs, vecs),
        fc=(i_ffg, fc), pr=(i_pr, pr), wo=(i_wo, wo), br=(i_br, br), st=(i_st, st),
        rl=(i_rl, rl), fb=(i_fb, fb), wb=(i_wb, wb), cv=(i_cv, cv), il=(i_il, il), lin=(i_lin, lin), wl=(i_wl, wl),
        y0=(i_y.at[1, 0:tokens // 2], yk.at[0]), y1=(i_y.at[0, tokens // 2:tokens], yk.at[1]),
        x=(i_x, x), base=(i_base, bout), rg=(i_rg, rg), ig=(i_ig, ig),
    )
    loads = {name: pltpu.make_async_copy(a, b, lsem.at[i]) for i, (name, (a, b)) in enumerate(loads.items())}
    for copy in loads.values():
        copy.start()

    def need(*names):
        for name in names:
            loads[name].wait()

    greet([me.along(d) for d in range(1, nz)] + [me.plane(r) for r in (1, 2, 3)] + [me.sibling()])


    def lanes(h):
        return head_lanes(h, width)

    def chain(i, right, from_me):
        def make():
            dest = nz - 1 - i if right else i
            peer = (me.t, z + (1 if right else -1) if from_me else z)
            at = (int(right), i)
            return remote(fc.at[:, dest], fz.at[at], fzs.at[at], fzr.at[at], peer)
        return make

    def chain_begin(i, right):
        out.go(chain(i, right, True), z == 0 if right else z == nz - 1)

    def chain_step(slot):
        for right in (True, False):
            i = slot - (z - 1 if right else nz - 2 - z)
            dest = nz - 1 - i if right else i
            here = jnp.logical_and(i >= 0, dest >= z if right else dest <= z)
            here = jnp.logical_and(here, z >= 1 if right else z <= nz - 2)
            onward = jnp.logical_and(here, dest != z)
            out.arrived(chain(i, right, False), here)

            @pl.when(here)
            def _(right=right, dest=dest, i=i):
                for m in range(3):
                    fc[m, dest] = (fc[m, dest].astype(F32) + fz[int(right), i, m].astype(F32)).astype(BF16)

            out.go(chain(i, right, True), onward)

    def feed_place(c, kk, half):
        at = pl.multiple_of((2 * c + kk) * part, part)
        if half is None:
            return fa.at[:, pl.ds(at, part)]
        return fa.at[:, pl.ds(pl.multiple_of(at + half * (part // 2), part // 2), part // 2)]

    feed_gather = PlaneGather(me, out, feed_place, fas, far, (), None, first=lambda: ffin)
    feed_own = pltpu.make_async_copy(ffin, feed_place(chip, core, None), osem.at[3])

    def feed_total():
        ffin[...] = fc[:, z]
        feed_gather.begin()
        feed_own.start()

    def y_half(r, half):
        return i_y.at[r - 1, pl.ds(half * (tokens // 2), tokens // 2)]

    y_sum = PlaneSum(me, out, lambda r, half: yk.at[half], lambda i: yp.at[{1: 0, 3: 1, 4: 2, 5: 3}[i]], yps, ypr, (), source=y_half)
    made = [pltpu.make_async_copy(a, b, osem.at[5 + i]) for i, (a, b) in enumerate(((bout, o_bout), (igrad, o_igrad), (osm, o_osm), (osmz, o_osmz)))]

    slot_of = {2: 0, 1: 1, 0: 0}

    def core_of(m):
        at = pl.ds(pl.multiple_of(other * (model // 2), model // 2), model // 2)
        return lambda: remote(g.at[slot_of[m], at], wc.at[m], wcs.at[m], wcr.at[m], me.sibling())

    core_copies = [core_of(m) for m in range(3)]

    def block_of(m, r, half=None):
        start = me.chip_of(r) * block
        if half is None:
            return wc.at[m, pl.ds(pl.multiple_of(start, block), block)]
        return wc.at[m, pl.ds(pl.multiple_of(start + half * half_rows, half_rows), half_rows)]

    sums = [
        PlaneSum(me, out, lambda r, half, m=m: block_of(m, r, half), lambda i, m=m: wp.at[m, i], wps, wpr, (m,))
        for m in range(3)
    ]

    def core_sum(m):
        out.arrived(core_copies[m])

        def add(c, _):
            at = rows(c, block)
            mine = pl.ds(pl.multiple_of(core * (model // 2) + c * block, block), block)
            wc[m, at, :] = (wc[m, at, :].astype(F32) + g[slot_of[m], mine, :].astype(F32)).astype(BF16)
            return 0

        lax.fori_loop(0, 4, add, 0)
        sums[m].begin()

    def z_copy(m, d):
        return lambda: remote(
            wc.at[m, rows(chip, block), rows(me.along(d)[1], own)], wz.at[m, d - 1], wzs.at[m, d - 1], wzr.at[m, d - 1], me.along(d)
        )

    def plane_total(m):
        for half in range(2):
            at = pl.ds(pl.multiple_of(chip * block + half * half_rows, half_rows), half_rows)
            wc[m, at, :] = (wc[m, at, :].astype(F32) + sums[m].total(half)).astype(BF16)
        for d in range(1, nz):
            out.go(z_copy(m, d))

    def weight_place(m):
        def place(c, kk, half):
            start = (4 * kk + c) * block
            if half is None:
                return wa.at[m, pl.ds(pl.multiple_of(start, block), block)]
            return wa.at[m, pl.ds(pl.multiple_of(start + half * half_rows, half_rows), half_rows)]
        return place

    own_copies = [pltpu.make_async_copy(fin.at[m], weight_place(m)(chip, core, None), osem.at[m]) for m in range(3)]
    gathers = [
        PlaneGather(
            me, out, weight_place(m), was, war, (m,), None, first=lambda m=m: fin.at[m],
            joined=lambda kk, m=m: wa.at[m, rows(kk, 4 * block)], ready=own_copies[m].wait,
        )
        for m in range(3)
    ]

    def z_total(m):
        for d in range(1, nz):
            out.arrived(z_copy(m, d))
        total = wc[m, rows(chip, block), rows(z, own)].astype(F32)
        for d in range(k):
            total = total + wz[m, d].astype(F32)
        fin[m] = total.astype(BF16)
        gathers[m].begin()
        own_copies[m].start()

    gate_half = gt.shape[0] // 2
    gate_block = gt.shape[0] // 8
    gate_part = gate_block // nz

    def gate_core():
        at = pl.ds(pl.multiple_of(other * gate_half, gate_half), gate_half)
        return remote(gt.at[at], gc, gcs.at[0], gcr.at[0], me.sibling())

    def gate_rows(r, half):
        return gc.at[pl.ds(pl.multiple_of(me.chip_of(r) * gate_block + half * (gate_block // 2), gate_block // 2), gate_block // 2)]

    gate_sum = PlaneSum(me, out, gate_rows, lambda i: gp.at[i], gps, gpr, ())

    def gate_core_sum():
        out.arrived(gate_core)
        mine = pl.ds(pl.multiple_of(core * gate_half, gate_half), gate_half)
        gc[...] = (gc[...].astype(F32) + gt[mine, :].astype(F32)).astype(BF16)
        gate_sum.begin()

    def gate_cut(i):
        return pl.ds(pl.multiple_of(chip * gate_block + i * gate_part, gate_part), gate_part)

    def gate_along(d):
        return lambda: remote(gc.at[gate_cut(me.along(d)[1])], gz.at[d - 1], gzs.at[d - 1], gzr.at[d - 1], me.along(d))

    def gate_back(d, origin):
        return lambda: remote(
            gfin.at[rows(origin(), gate_part)], gfin.at[rows(origin(), gate_part)], gys.at[d - 1], gyr.at[d - 1], me.along(d)
        )

    def gate_total():
        for half in range(2):
            at = pl.ds(pl.multiple_of(chip * gate_block + half * (gate_block // 2), gate_block // 2), gate_block // 2)
            gc[at, :] = (gc[at, :].astype(F32) + gate_sum.total(half)).astype(BF16)
        for d in range(1, nz):
            out.go(gate_along(d))

    def gate_z_total():
        for d in range(1, nz):
            out.arrived(gate_along(d))
        total = gc[gate_cut(z), :].astype(F32)
        for d in range(k):
            total = total + gz[d].astype(F32)
        gfin[rows(z, gate_part), :] = total.astype(BF16)
        for d in range(1, nz):
            out.go(gate_back(d, lambda: z))

    def gate_place(c, kk, half):
        start = (4 * kk + c) * gate_block
        if half is None:
            return ga.at[pl.ds(pl.multiple_of(start, gate_block), gate_block)]
        return ga.at[pl.ds(pl.multiple_of(start + half * (gate_block // 2), gate_block // 2), gate_block // 2)]

    gate_own = pltpu.make_async_copy(gfin, gate_place(chip, core, None), osem.at[4])
    gate_gather = PlaneGather(
        me, out, gate_place, gas, gar, (), None, first=lambda: gfin, joined=lambda kk: ga.at[rows(kk, 4 * gate_block)],
        ready=gate_own.wait,
    )

    def gate_spread():
        for d in range(1, nz):
            out.arrived(gate_back(d, lambda: me.z_from(d)))
        gate_gather.begin()
        gate_own.start()

    def small_copy(i):
        peer = (me.sibling(), me.plane(1), me.plane(2))[i]
        return lambda: remote(sm.at[2 * i], sm.at[2 * i + 1], s1s.at[i], s1r.at[i], peer)

    def small_step(i):
        out.arrived(small_copy(i))
        sm[2 * i + 2] = sm[2 * i] + sm[2 * i + 1]
        if i < 2:
            out.go(small_copy(i + 1))
        else:
            smz[z] = sm[6]
            for d in range(1, nz):
                out.go(small_along(d, lambda: z))

    def small_along(d, origin):
        return lambda: remote(sm.at[6], smz.at[origin()], s2s.at[d - 1], s2r.at[d - 1], me.along(d))


    small = sm.at[0]
    row = lax.broadcasted_iota(jnp.int32, (8, width), 0)

    def branch_back(h, _):
        pg = dot(rgb[...], wo[lanes(h), :], NT)
        act, slope = gelu_both(br[h])
        bg[:, lanes(h)] = (pg * st[h] * slope).astype(BF16)
        fl[h, 0:tokens] = pg * act
        return 0

    def scan_head(h, _):
        rate = softplus(-vec[4:5, lanes(h)]) * -DECAY_SCALE

        def tile(j, carried):
            later, factor = carried
            i = tokens // 16 - 1 - j
            at = rows(i, 16)
            keep = 1.0 - mk[at, 0:1]
            a = keep * jnp.exp(sigmoid(rl[h, at, :].astype(F32)) * rate)
            sgrad = fl[h, at, :]
            b = a * sgrad
            for t in (1, 0):
                cum, run = tile_scan(a[8 * t:8 * t + 8], b[8 * t:8 * t + 8], row, True)
                run = run + cum * later
                cum = cum * factor
                here = pl.ds(pl.multiple_of(i * 16 + 8 * t, 8), 8)
                last = row == 7
                fl[h, here, :] = sgrad[8 * t:8 * t + 8] + jnp.where(last, later, pltpu.roll(run, 7, 0))
                br[h, here, :] = jnp.where(last, factor, pltpu.roll(cum, 7, 0))
                later, factor = run[0:1], cum[0:1]
            return later, factor

        later, factor = lax.fori_loop(
            0, tokens // 16, tile, (jnp.zeros((1, width), F32), jnp.ones((1, width), F32)), unroll=4
        )
        ends[0, 0:1, lanes(h)] = later
        ends[0, 1:2, lanes(h)] = factor
        return 0

    def end_copy(d):
        return lambda: remote(ends.at[0], ends.at[d], es.at[d - 1], er.at[d - 1], me.along(nz - d))

    def wgrad(slot, right):
        def body(h, _):
            g[slot, :, lanes(h)] = dot(turned[...], right[:, lanes(h)], NN).astype(BF16)
            return 0

        lax.fori_loop(0, heads, body, 0)

    def terms(h, _):
        raw = vec[4:5, lanes(h)]
        soft = softplus(-raw)
        later = inc[:, lanes(h)]

        def tile(i, carried):
            before, decays, rates, inputs = carried
            at = rows(i, 16)
            start = mk[at, 0:1]
            keep = 1.0 - start
            flow = fl[h, at, :] + br[h, at, :] * later
            state = st[h, at, :]
            first = lax.broadcasted_iota(jnp.int32, (16, width), 0) == 0
            earlier = jnp.where(first, before, pltpu.roll(state, 1, 0))
            sig = sigmoid(rl[h, at, :].astype(F32))
            gate = sigmoid(il[h, at, :].astype(F32))
            decay = jnp.exp(sig * (soft * -DECAY_SCALE))
            root = jnp.sqrt(1.0 - decay * decay)
            level = start + keep * root
            conv = cv[h, at, :].astype(F32)
            to_scale = flow * conv
            to_decay = keep * (flow * earlier - to_scale * gate * (decay / root))
            to_power = to_decay * decay * sig
            rate_grad = (to_power * (1.0 - sig) * (soft * -DECAY_SCALE)).astype(BF16)
            input_grad = (to_scale * level * gate * (1.0 - gate)).astype(BF16)
            rlg[h, at, :] = rate_grad
            ilg[h, at, :] = input_grad
            fl[h, at, :] = flow * level * gate
            rates = rates + rate_grad.astype(F32)
            inputs = inputs + input_grad.astype(F32)
            return state[15:16], decays + to_power, rates, inputs

        zero = jnp.zeros((16, width), F32)
        _, decays, rates, inputs = lax.fori_loop(0, tokens // 16, tile, (sin[:, lanes(h)], zero, zero, zero), unroll=4)
        small[4:5, lanes(h)] = jnp.sum(decays, axis=0, keepdims=True) * (DECAY_SCALE * sigmoid(-raw))
        small[5:6, lanes(h)] = jnp.sum(rates, axis=0, keepdims=True)
        small[6:7, lanes(h)] = jnp.sum(inputs, axis=0, keepdims=True)
        rate_out, input_out = rlg[h], ilg[h]
        gt[rows(h, width), :] = dot(cv[h], rate_out, TN).astype(BF16)
        gt[rows(heads + h, width), :] = dot(cv[h], input_out, TN).astype(BF16)
        path = (dot(rate_out, rg[h], NT) + dot(input_out, ig[h], NT)).astype(BF16)
        fl[h, 0:tokens] = fl[h, 0:tokens] + path.astype(F32)
        hal[0, h] = fl[h, 0:8]
        return 0

    def halo():
        return remote(hal.at[0], hal.at[1], hs.at[0], hr.at[0], me.along(nz - 1))

    def first_back(left, right):
        def body(j, _):
            at = rows(j, 256)
            igrad[:, at] += dot(left[...], right[at, :], NT)
            return 0

        lax.fori_loop(0, model // 256, body, 0)

    def filter_back(h, _):
        taps = vec[0:4, lanes(h)]
        fl[h, tokens:tokens + 8] = hal[1, h]
        value = taps[0:1] * fl[h, 0:tokens]
        small[0:1, lanes(h)] = jnp.sum(fl[h, 0:tokens] * lin[h, HALO:], axis=0, keepdims=True)
        for t in range(1, 4):
            value = value + taps[t:t + 1] * (fl[h, t:t + tokens] * mk[:, 3 + t:4 + t])
            small[t:t + 1, lanes(h)] = jnp.sum(
                fl[h, 0:tokens] * (lin[h, HALO - t:HALO - t + tokens] * mk[:, t:t + 1]), axis=0, keepdims=True
            )
        lgr[:, lanes(h)] = value.astype(BF16)
        return 0

    y_sum.put(1)
    y_sum.put(3)
    need("g2g", "vec", "mk", "sin", "vecs", "fc")
    chain_begin(0, False)
    for i in range(k):
        chain_begin(i, True)
    small[...] = jnp.zeros(small.shape, F32)
    small[8:9, 0:model] = g2g[...]
    need("rgrad")
    rgb[...] = rgrad[...].astype(BF16)
    need("pr")
    turned[...] = rgb[...].T
    wgrad(0, pr)
    out.go(core_copies[2])
    need("wo", "br", "st")
    lax.fori_loop(0, heads, branch_back, 0)
    core_sum(2)
    need("rl")
    lax.fori_loop(0, heads // 2, scan_head, 0)
    need("y0", "y1")
    y_sum.relay()
    lax.fori_loop(heads // 2, heads, scan_head, 0)
    for d in range(1, nz):
        out.go(end_copy(d), z >= d)
    chain_begin(1, False)
    need("fb")
    turned[...] = fb[HALO:, :].T
    wgrad(1, bg)
    out.go(core_copies[1])
    chain_step(0)
    for d in range(1, nz):
        out.arrived(end_copy(d), z + d < nz)
    incoming = jnp.zeros((1, lru), F32)
    for d in range(nz - 1, 0, -1):
        end = ends[d, 0:1, :] + ends[d, 1:2, :] * incoming
        incoming = jnp.where(d + z < nz, end, incoming)
    inc[...] = incoming
    core_sum(1)
    sums[2].relay()
    need("cv", "il", "rg", "ig")
    lax.fori_loop(0, heads // 3, terms, 0)
    chain_begin(2, False)
    lax.fori_loop(heads // 3, heads, terms, 0)
    chain_step(1)
    out.go(gate_core)
    sums[1].relay()
    gate_core_sum()
    need("wb")
    igrad[...] = jnp.zeros(igrad.shape, F32)
    first_back(bg, wb)
    gate_sum.relay()
    out.go(halo)
    chain_step(2)
    feed_total()
    need("base")
    for half in range(2):
        at = pl.ds(half * (tokens // 2), tokens // 2)
        y_sum.wait(4 + half)
        bout[at, :] = bout[at, :] + yp[2 + half].astype(F32)
    made[0].start()
    plane_total(2)
    need("lin")
    out.arrived(halo)
    lax.fori_loop(0, heads, filter_back, 0)
    out.sent(core_copies[2])
    wgrad(0, lgr)
    out.go(core_copies[0])
    core_sum(0)
    gate_total()
    need("wl")
    first_back(lgr, wl)
    need("x")
    value = x[...].astype(F32)
    fgrad = igrad[...]
    q = fgrad * vecs[0:1, 0:model]
    inv = lax.rsqrt(jnp.mean(value * value, axis=-1, keepdims=True) + EPS)
    pull = jnp.mean(q * value, axis=-1, keepdims=True)
    small[7:8, 0:model] = jnp.sum(fgrad * value * inv, axis=0, keepdims=True)
    igrad[...] = rgrad[...] + (inv * q - value * (inv * inv * inv * pull))
    made[1].start()
    out.go(small_copy(0))
    gate_z_total()
    sums[0].relay()
    small_step(0)
    feed_gather.relay()
    plane_total(1)
    small_step(1)
    plane_total(0)
    gate_spread()
    z_total(1)
    z_total(2)
    small_step(2)
    gate_gather.relay()
    z_total(0)
    gathers[2].relay()
    feed_gather.far()
    gathers[1].relay()
    gate_gather.far()
    gathers[0].relay()
    gathers[2].far()
    for d in range(1, nz):
        out.arrived(small_along(d, lambda: me.z_from(d)))
    total = smz[0]
    for i in range(1, nz):
        total = total + smz[i]
    osm[...] = total
    osmz[...] = osm[:, rows(z, own)]
    made[2].start()
    made[3].start()
    gathers[1].far()
    gathers[0].far()
    for gathered in [feed_gather, gathers[2], gathers[1], gate_gather, gathers[0]]:
        gathered.end()
    for copy in [feed_own] + made:
        copy.wait()
    out.finish()


def backward(nz, sin, mk, vec, vecs, g2g, rg, ig, rgrad, x, wl, wb, wo, fb, lin, br, cv, rl, il, st, pr, base, y, ffg):
    tokens, model = x.shape
    heads, width = rg.shape[0], rg.shape[1]
    lru = heads * width
    own = lru // nz
    part = ffg.shape[2]
    k = nz - 1
    block = model // 8
    gate_rows = 2 * lru
    gate_block = gate_rows // 8
    hbm = pl.BlockSpec(memory_space=pl.ANY)
    by_head = (heads, tokens, width)
    half = tokens // 2
    sems = []
    for shape in (
        (3,), (3, 6), (3, k), (3, 8), (2, k), (8,),
        (1,), (6,), (k,), (k,), (8,), (6,), (3,), (k,), (k,), (1,),
    ):
        sems += [DMA(shape)] * 2
    return pl.pallas_call(
        functools.partial(backward_kernel, nz, heads),
        out_shape=(
            jax.ShapeDtypeStruct((3, model, own), BF16),
            jax.ShapeDtypeStruct((3, 8 * part, model), BF16),
            jax.ShapeDtypeStruct((gate_rows, width), BF16),
            jax.ShapeDtypeStruct((tokens, model), F32),
            jax.ShapeDtypeStruct((tokens, model), F32),
            jax.ShapeDtypeStruct((16, lru), F32),
            jax.ShapeDtypeStruct((16, own), F32),
        ),
        in_specs=[hbm] * 23,
        out_specs=[hbm] * 7,
        scratch_shapes=[
            VMEM(sin.shape, F32), VMEM(mk.shape, F32), VMEM(vec.shape, F32), VMEM(vecs.shape, F32), VMEM(g2g.shape, F32),
            VMEM((16, lru), F32), VMEM((16, own), F32),
            VMEM((heads, width, width), BF16), VMEM((heads, width, width), BF16), VMEM((tokens, model), F32),
            VMEM((tokens, model), F32), VMEM((tokens, model), F32),
            VMEM((tokens, model), BF16), VMEM((model, lru), BF16), VMEM((model, lru), BF16), VMEM((lru, model), BF16),
            VMEM((HALO + tokens, model), BF16), VMEM((heads, HALO + tokens, width), F32), VMEM(by_head, F32),
            VMEM(by_head, BF16), VMEM(by_head, BF16), VMEM(by_head, BF16), VMEM(by_head, F32), VMEM((tokens, lru), BF16),
            VMEM((2, half, model), BF16),
            VMEM((tokens, model), BF16), VMEM((model, tokens), BF16), VMEM((heads, tokens + 8, width), F32),
            VMEM(by_head, BF16), VMEM(by_head, BF16), VMEM((tokens, lru), BF16), VMEM((tokens, lru), BF16),
            VMEM((nz, 8, lru), F32), VMEM((2, heads, 8, width), F32),
            VMEM((2, model, lru), BF16), VMEM((3, model // 2, lru), BF16), VMEM((3, 6, block // 2, lru), BF16),
            VMEM((3, k, block, own), BF16), VMEM((3, block, own), BF16),
            VMEM((3, nz, part, model), BF16), VMEM((2, k, 3, part, model), BF16), VMEM((3, part, model), BF16),
            VMEM((gate_rows, width), BF16), VMEM((gate_rows // 2, width), BF16), VMEM((6, gate_block // 2, width), BF16),
            VMEM((k, gate_block // nz, width), BF16), VMEM((gate_block, width), BF16),
            VMEM((7, 16, lru), F32), VMEM((nz, 16, lru), F32), VMEM((4, half, model), BF16), VMEM((1, lru), F32),
            DMA((25,)), DMA((9,)),
        ] + sems,
        compiler_params=pltpu.CompilerParams(collective_id=1, has_side_effects=True, vmem_limit_bytes=62 * 2**20),
        name="backward_and_sums",
    )(sin, mk, vec, vecs, g2g, rg, ig, rgrad, x, wl, wb, wo, fb, lin, br, cv, rl, il, st, pr, base, y, ffg)


def results_kernel(wa, fa, ga, gb, bout, igrad, osm, osmz,
                   o_out, o_in, o_g1, o_branch, o_lru, o_taps, o_rate, o_input, o_rb, o_ib, o_decay, o_ow, o_g2, o_gate, o_up, o_down):
    model = bout.shape[1]

    @pl.when(pl.program_id(0) == 0)
    def _():
        o_out[...] = bout[...]
        o_in[...] = igrad[...]
        o_taps[...] = osmz[0:4, :]
        o_decay[...] = osmz[4, :]
        o_rb[...] = osm[5, :]
        o_ib[...] = osm[6, :]
        o_g1[...] = osm[7, 0:model]
        o_g2[...] = osm[8, 0:model]

    o_lru[...] = wa[0].astype(F32)
    o_branch[...] = wa[1].astype(F32)
    o_ow[...] = wa[2].T.astype(F32)
    o_rate[...] = ga[...].astype(F32)
    o_input[...] = gb[...].astype(F32)
    o_gate[...] = fa[0].T.astype(F32)
    o_up[...] = fa[1].T.astype(F32)
    o_down[...] = fa[2].astype(F32)


def results(wa, fa, ga, bout, igrad, osm, osmz):
    steps = 3
    model, own = wa.shape[1:]
    cols = fa.shape[1]
    gate_rows, width = ga.shape[0] // 2, ga.shape[1]
    lru = osm.shape[1]
    tokens = bout.shape[0]

    def whole(shape):
        return pl.BlockSpec(shape, lambda i: (0,) * len(shape))

    across = pl.BlockSpec((model, own // steps), lambda i: (0, i))
    feed_across = pl.BlockSpec((model, cols // steps), lambda i: (0, i))
    outs = [
        ((tokens, model), whole((tokens, model))), ((tokens, model), whole((tokens, model))), ((model,), whole((model,))),
        ((model, own), across), ((model, own), across), ((4, own), whole((4, own))),
        ((gate_rows, width), pl.BlockSpec((gate_rows // steps, width), lambda i: (i, 0))),
        ((gate_rows, width), pl.BlockSpec((gate_rows // steps, width), lambda i: (i, 0))),
        ((lru,), whole((lru,))), ((lru,), whole((lru,))), ((own,), whole((own,))),
        ((own, model), pl.BlockSpec((own // steps, model), lambda i: (i, 0))), ((model,), whole((model,))),
        ((model, cols), feed_across), ((model, cols), feed_across),
        ((cols, model), pl.BlockSpec((cols // steps, model), lambda i: (i, 0))),
    ]
    return pl.pallas_call(
        results_kernel,
        grid=(steps,),
        out_shape=tuple(jax.ShapeDtypeStruct(shape, F32) for shape, _ in outs),
        in_specs=[
            pl.BlockSpec((3, model, own // steps), lambda i: (0, 0, i)),
            pl.BlockSpec((3, cols // steps, model), lambda i: (0, i, 0)),
            pl.BlockSpec((gate_rows // steps, width), lambda i: (i, 0)),
            pl.BlockSpec((gate_rows // steps, width), lambda i: (i + steps, 0)),
            whole((tokens, model)), whole((tokens, model)), whole((16, lru)), whole((16, own)),
        ],
        out_specs=tuple(spec for _, spec in outs),
        compiler_params=pltpu.CompilerParams(vmem_limit_bytes=62 * 2**20),
        name="results",
    )(wa, fa, ga, ga, bout, igrad, osm, osmz)


def local(
    nz,
    groups,
    block_input,
    doc_starts,
    first_gain,
    branch_weight,
    lru_weight,
    filter_taps,
    rate_gate,
    input_gate,
    rate_bias,
    input_bias,
    decay_logit,
    out_weight,
    second_gain,
    feed_gate,
    feed_up,
    feed_down,
    cotangent,
):
    model = block_input.shape[1]
    heads, width = rate_gate.shape[:2]
    lru = heads * width

    (wl, wb, wo, fb, lin, br, cv, rl, il, st, pr, y, ffg, base, rgrad, sin, mk, vec, g2g, vecs) = forward(
        nz, first_gain, second_gain, rate_bias, input_bias, doc_starts, filter_taps, decay_logit, block_input, rate_gate,
        input_gate, cotangent, lru_weight, branch_weight, out_weight,
        feed_gate, feed_up, feed_down,
    )
    sums = backward(
        nz, sin, mk, vec, vecs, g2g, rate_gate, input_gate, rgrad, block_input, wl, wb, wo, fb, lin, br, cv, rl, il, st, pr,
        base, y, ffg,
    )
    made = results(*sums)
    block_output, input_grad, *summed = made
    if groups > 1:
        same = [[8 * g + b for g in range(groups)] for b in range(8)]
        summed = lax.psum(tuple(summed), "tp", axis_index_groups=same)
    g1, branch, lru_grad, taps, rate, inputs, rb, ib, decay, ow, g2, gate, up, down = summed
    rate, inputs = rate.reshape(heads, width, width), inputs.reshape(heads, width, width)
    return (
        block_output, input_grad, g1, branch, lru_grad, taps, rate, inputs, rb, ib, decay, ow, g2,
        gate, up, down,
    )


def solution(mesh):
    by_rows = P(("tp", "dp"), None)
    by_cols = P(None, "dp")
    split = P("dp", None)
    return jax.shard_map(
        functools.partial(local, mesh.shape["dp"], mesh.shape["tp"] // 8),
        mesh=mesh,
        in_specs=(
            by_rows, P("tp"), P(), by_cols, by_cols, by_cols, P(), P(), P(), P(), P("dp"), split, P(), by_cols, by_cols,
            split, by_rows,
        ),
        out_specs=(
            by_rows, by_rows, P(), by_cols, by_cols, by_cols, P(), P(), P(), P(), P("dp"), split, P(), by_cols, by_cols,
            split,
        ),
        check_vma=False,
    )
```

```python
import functools
import math

import jax
import jax.numpy as jnp
from jax import lax
from jax.experimental import pallas as pl
from jax.experimental.pallas import tpu as pltpu
from jax.sharding import PartitionSpec as P

EPS = 1e-06
DECAY_SCALE = 8.0
F32 = jnp.float32
BF16 = jnp.bfloat16
MESH = pl.DeviceIdType.MESH
VMEM = pltpu.VMEM
DMA = pltpu.SemaphoreType.DMA
NN = (((1,), (0,)), ((), ()))
NT = (((1,), (1,)), ((), ()))
TN = (((0,), (0,)), ((), ()))
HALO = 16
LANE = 128
GELU_A = math.sqrt(2.0 / math.pi)
GELU_B = 0.044715


def dot(left, right, form):
    return lax.dot_general(left, right, form, preferred_element_type=F32)


def sigmoid(v):
    return 1.0 / (1.0 + jnp.exp(-v))


def softplus(v):
    return jnp.maximum(v, 0.0) + jnp.log1p(jnp.exp(-jnp.abs(v)))


def gelu_both(v):
    square = v * v
    tanh = jnp.tanh(GELU_A * v * (1.0 + GELU_B * square))
    half = 0.5 * (1.0 + tanh)
    slope = half + 0.5 * v * (1.0 - tanh * tanh) * (GELU_A * (1.0 + 3.0 * GELU_B * square))
    return v * half, slope


def gelu_only(v):
    return v * (0.5 * (1.0 + jnp.tanh(GELU_A * v * (1.0 + GELU_B * v * v))))


class Place:
    def __init__(self, nz):
        self.nz = nz
        self.t = lax.axis_index("tp")
        self.z = lax.axis_index("dp")
        self.b = lax.rem(self.t, 8)
        self.core = lax.rem(self.t, 2)
        self.x = lax.rem(self.t // 2, 2)
        self.y = lax.rem(self.t // 4, 2)
        self.chip = self.b // 2

    def flip(self, r):
        t = self.t
        if r & 1:
            t = t + 2 - 4 * self.x
        if r & 2:
            t = t + 4 - 8 * self.y
        return t

    def chip_of(self, r):
        c = self.chip
        if r & 1:
            c = c + 1 - 2 * self.x
        if r & 2:
            c = c + 2 - 4 * self.y
        return c

    def plane(self, r):
        return (self.flip(r), self.z)

    def sibling(self):
        return (self.t + 1 - 2 * self.core, self.z)

    def along(self, d):
        return (self.t, lax.rem(self.z + d, self.nz))

    def z_from(self, d):
        return lax.rem(self.z + self.nz - d, self.nz)


def greet(peers):
    barrier = pltpu.get_barrier_semaphore()
    for peer in peers:
        pl.semaphore_signal(barrier, inc=1, device_id=peer, device_id_type=MESH)
    pl.semaphore_wait(barrier, len(peers))


def remote(src, dst, send, recv, peer):
    return pltpu.make_async_remote_copy(
        src_ref=src, dst_ref=dst, send_sem=send, recv_sem=recv, device_id=peer, device_id_type=MESH
    )


class Sends:
    def __init__(self):
        self.started = []

    def when(self, cond, action):
        if cond is None:
            action()
        else:
            pl.when(cond)(action)

    def go(self, make, cond=None):
        self.when(cond, lambda: make().start())
        self.started.append((cond, make))

    def start_if(self, cond, make):
        pl.when(cond)(lambda: make().start())
        self.started.append((None, make))

    def arrived(self, make, cond=None):
        self.when(cond, lambda: make().wait_recv())

    def sent(self, make):
        make().wait_send()
        self.started = [(cond, other) for cond, other in self.started if other is not make]

    def finish(self):
        for cond, make in self.started:
            self.when(cond, lambda: make().wait_send())


class PlaneGather:
    def __init__(self, me, out, piece, send, recv, at, cond=None, first=None, joined=None, ready=None):
        self.me, self.out, self.piece, self.cond, self.joined = me, out, piece, cond, joined
        self.send, self.recv, self.at, self.first, self.ready = send, recv, at, first, ready

    def copy(self, i, src, dst, peer):
        return remote(src, dst, self.send.at[self.at + (i,)], self.recv.at[self.at + (i,)], peer)

    def whole(self, i, r, peer, first=False):
        def make():
            place = self.piece(self.me.chip_of(r), self.me.core, None)
            return self.copy(i, self.first() if first and self.first else place, place, peer)
        return make

    def half(self, i, r, part, peer):
        def make():
            place = self.piece(self.me.chip_of(r), self.me.core, part)
            return self.copy(i, place, place, peer)
        return make

    def across(self, core):
        def make():
            place = self.joined(core)
            return self.copy(4, place, place, self.me.sibling())
        return make

    def begin(self):
        for i, r in ((0, 1), (1, 2)):
            self.out.go(self.whole(i, 0, self.me.plane(r), True), self.cond)
        if not self.joined:
            self.out.go(self.whole(4, 0, self.me.sibling(), True), self.cond)

    def relay(self):
        me = self.me
        for i, r, part in ((0, 1, 0), (1, 2, 1)):
            self.out.arrived(self.whole(i, r, me.plane(r)), self.cond)
            self.out.go(self.half(2 + i, r, part, me.plane(3 - r)), self.cond)
            if not self.joined:
                self.out.go(self.whole(4 + r, r, me.sibling()), self.cond)

    def far(self):
        for part in (0, 1):
            self.out.arrived(self.half(2 + part, 3, part, self.me.plane(2 - part)), self.cond)
        if self.joined:
            if self.ready:
                self.ready()
            self.out.go(self.across(self.me.core), self.cond)
        else:
            self.out.go(self.whole(7, 3, self.me.sibling()), self.cond)

    def end(self):
        me = self.me
        if self.joined:
            self.out.arrived(self.across(1 - me.core), self.cond)
            return
        for r in range(4):
            def make(r=r):
                place = self.piece(me.chip_of(r), 1 - me.core, None)
                return self.copy(4 + r, place, place, me.sibling())
            self.out.arrived(make, self.cond)


class PlaneSum:
    def __init__(self, me, out, block, recv, send_sem, recv_sem, at, source=None):
        self.me, self.out, self.block, self.got = me, out, block, recv
        self.send_sem, self.recv_sem, self.at = send_sem, recv_sem, at
        self.source = source or block
        self.near = {r: me.plane(r) for r in (1, 2)}

    def copy(self, i, src, peer):
        def make():
            return remote(
                src(), self.got(i), self.send_sem.at[self.at + (i,)], self.recv_sem.at[self.at + (i,)], peer
            )
        return make

    def put(self, i, cond=None):
        half = i // 2
        to = 3 if i % 2 else half + 1
        make = self.copy(i, lambda: self.source(to, half), self.near[half + 1])
        if cond is None:
            self.out.go(make)
        else:
            self.out.start_if(cond, make)

    def begin(self):
        for i in (1, 0, 3, 2):
            self.put(i)

    def wait(self, i):
        self.out.arrived(self.copy(i, lambda: self.got(i), self.me.plane(1)))

    def relay(self):
        for half, r in ((0, 2), (1, 1)):
            self.wait(2 * half + 1)
            mine = self.block(r, half)
            mine[...] = (mine[...].astype(F32) + self.got(2 * half + 1)[...].astype(F32)).astype(BF16)
            self.out.go(self.copy(4 + half, lambda r=r, half=half: self.block(r, half), self.me.plane(r)))

    def total(self, half):
        self.wait(2 * half)
        self.wait(4 + half)
        return self.got(2 * half)[...].astype(F32) + self.got(4 + half)[...].astype(F32)


def rows(i, size):
    return pl.ds(pl.multiple_of(i * size, size), size)


def rms(v, gain):
    return v * lax.rsqrt(jnp.mean(v * v, axis=-1, keepdims=True) + EPS) * gain


def head_lanes(h, width):
    return pl.ds(pl.multiple_of(h * width, width), width)


def tile_scan(a, b, row, back):
    for step in (1, 2, 4):
        if back:
            seen = row < 8 - step
            shift = 8 - step
        else:
            seen = row >= step
            shift = step
        b_before = jnp.where(seen, pltpu.roll(b, shift, 0), 0.0)
        a_before = jnp.where(seen, pltpu.roll(a, shift, 0), 1.0)
        b = b + a * b_before
        a = a * a_before
    return a, b


def forward_kernel(nz, heads, i_gain1, i_gain2, i_bias1, i_bias2, i_starts, i_taps, i_dlogit, i_x, i_rg, i_ig, cot, lw, bw, ow, fgate, fup, fdown,
                   o_wl, o_wb, o_wo, o_fb, o_lin, o_br, o_cv, o_rl, o_il, o_st, o_pr, o_y, o_wg, o_base, o_rgrad,
                   o_sin, o_mk, o_vec, o_g2g, o_vecs,
                   gain1, gain2, bias1, bias2, starts, taps_in, dlogit, sin, mk, vec, g2g, vecs,
                   x, rg, ig, base, rgrad, wl, wb, wo, f, cots, win, turned, fb, lin, br, cv, rl, il, st, pr, pst, ends, ms, hx,
                   res, s, h, lg, ug, ybuf, sbuf, srecv, sown, fc, acts, slopes, yp,
                   lsem, osem, zs, zr, ps, pr_sem, fcs, fcr, qs, qr, vs, vr, es, er, hs, hr, ss, sr, gs, gr, ks, kr, ys, yr):
    me = Place(nz)
    out, feeds = Sends(), Sends()
    tokens, model = x.shape
    lru = wl.shape[1]
    width = lru // heads
    own = lru // nz
    cols = f.shape[1]
    part = cols // (2 * nz)
    piece_rows = model // 8
    chunk = 256
    z = me.z

    window = pl.ds(pl.multiple_of((me.chip // 2) * (4 * part) + lax.rem(me.chip, 2) * LANE, LANE), 256)
    shift = 64 * lax.rem(me.chip, 2)
    mine = rows(z, own)
    local = [
        (fgate.at[:, window], win.at[0]),
        (fup.at[:, window], win.at[1]),
        (lw, wl.at[:, mine]),
        (bw, wb.at[:, mine]),
        (ow, wo.at[mine]),
        (fdown.at[rows(me.chip, 2 * part)], f.at[2, rows(z, 2 * part)]),
        (cot, cots.at[0]),
    ]
    local = [pltpu.make_async_copy(a, b, lsem.at[i]) for i, (a, b) in enumerate(local)]
    vectors = (
        (i_gain1, gain1), (i_gain2, gain2), (i_bias1, bias1), (i_bias2, bias2), (i_starts, starts), (i_taps, taps_in),
        (i_dlogit, dlogit),
    )
    vectors = [pltpu.make_async_copy(a, b, lsem.at[11 + i]) for i, (a, b) in enumerate(vectors)]
    more = [pltpu.make_async_copy(a, b, lsem.at[8 + i]) for i, (a, b) in enumerate(((i_x, x), (i_rg, rg), (i_ig, ig)))]
    for copy in vectors + more[:1] + local + more[1:]:
        copy.start()
    greet([me.along(d) for d in range(1, nz)] + [me.plane(r) for r in (1, 2, 3)] + [me.sibling()])
    for copy in vectors:
        copy.wait()
    vecs[...] = jnp.zeros(vecs.shape, F32)
    for i, v in enumerate((gain1, gain2, bias1, bias2, starts)):
        vecs[i:i + 1, 0:v.shape[0]] = v[...].astype(F32).reshape(1, v.shape[0])
    vecs[8:12, 0:own] = taps_in[...].astype(F32)
    vecs[12:13, 0:own] = dlogit[...].astype(F32).reshape(1, own)

    def vector(d, origin):
        def make():
            place = vec.at[:, rows(origin(), own)]
            return remote(vecs.at[8:16, 0:own], place, vs.at[d - 1], vr.at[d - 1], me.along(d))
        return make

    def halo():
        return remote(i_x.at[tokens - HALO:tokens], hx, hs.at[0], hr.at[0], me.along(1))

    out.go(halo)
    for d in range(1, nz):
        out.go(vector(d, lambda: z))

    mine_of = 4 * me.core + me.chip

    def slot(m, zz, b):
        if m < 2:
            return (wl, wb)[m].at[rows(b, piece_rows), rows(zz, own)]
        if m == 2:
            return wo.at[rows(zz, own), rows(b, LANE)]
        at = pl.ds(pl.multiple_of(zz * (2 * part) + me.core * part, part), part)
        return f.at[0:2, at] if m == 3 else f.at[2, at]

    def source(m):
        if m < 2:
            return (lw, bw)[m].at[rows(mine_of, piece_rows)]
        if m == 2:
            return ow.at[:, rows(mine_of, LANE)]
        if m == 3:
            return turned.at[:, pl.ds(pl.multiple_of(shift + me.core * part, 32), part)]
        return fdown.at[pl.ds(pl.multiple_of(me.chip * (2 * part) + me.core * part, part), part)]

    def origin(hop, right):
        return z - 1 - hop if right else z + 1 + hop

    def has(hop, right):
        return z - 1 - hop >= 0 if right else z + 1 + hop < nz

    def along(m, hop, right, from_me):
        def make():
            step = 1 if right else -1
            zz = z - step * hop if from_me else origin(hop, right)
            place = slot(m, zz, mine_of)
            src = source(m) if from_me and hop == 0 else place
            at = (m, hop, int(right))
            peer = (me.t, z + step if from_me else z)
            return remote(src, place, zs.at[at], zr.at[at], peer)
        return make

    def z_begin(m, hop=0):
        for right in (True, False):
            there = z + 1 < nz if right else z >= 1
            if hop:
                there = jnp.logical_and(there, has(hop - 1, right))
            (out if m < 3 else feeds).go(along(m, hop, right, True), there)

    gathers = {}
    for m in range(3):
        for hop in range(nz - 1):
            for right in (True, False):
                def place(chip, core, half, m=m, hop=hop, right=right):
                    zz, b = origin(hop, right), 4 * core + chip
                    if half is None:
                        return slot(m, zz, b)
                    if m < 2:
                        at = pl.ds(pl.multiple_of(b * piece_rows + half * (piece_rows // 2), piece_rows // 2), piece_rows // 2)
                        return (wl, wb)[m].at[at, rows(zz, own)]
                    at = pl.ds(pl.multiple_of(zz * own + half * (own // 2), own // 2), own // 2)
                    return wo.at[at, rows(b, LANE)]

                def joined(core, m=m, hop=hop, right=right):
                    zz = origin(hop, right)
                    if m < 2:
                        return (wl, wb)[m].at[rows(core, 4 * piece_rows), rows(zz, own)]
                    return wo.at[rows(zz, own), rows(core, 4 * LANE)]

                gathers[m, hop, right] = PlaneGather(
                    me, out, place, ps, pr_sem, (m, 2 * hop + int(right)), has(hop, right), joined=joined
                )

    def share(m, hop, right, from_me):
        def make():
            at = (m - 3, 2 * hop + int(right))
            place = slot(m, origin(hop, right), mine_of)
            if not from_me:
                other = pl.ds(pl.multiple_of(origin(hop, right) * (2 * part) + (1 - me.core) * part, part), part)
                place = f.at[0:2, other] if m == 3 else f.at[2, other]
            return remote(place, place, fcs.at[at], fcr.at[at], me.sibling())
        return make

    def z_step(m, hop):
        for right in (True, False):
            out.arrived(along(m, hop, right, False), has(hop, right))
        if hop + 1 < nz - 1:
            z_begin(m, hop + 1)
        for right in (True, False):
            if m < 3:
                gathers[m, hop, right].begin()
            else:
                feeds.go(share(m, hop, right, True), has(hop, right))

    def relay(m, hop):
        for right in (True, False):
            gathers[m, hop, right].relay()

    def far(m, hop):
        for right in (True, False):
            gathers[m, hop, right].far()

    def all_of(m):
        for hop in range(nz - 1):
            for right in (True, False):
                gathers[m, hop, right].end()

    half = tokens // 2

    def cot_whole(i, r, part_of):
        at = pl.ds(part_of * half, half)
        return lambda: remote(cot.at[at], cots.at[r, at], qs.at[2 * part_of + i], qr.at[2 * part_of + i], me.plane(r))

    def cot_part(part_of, r):
        at = pl.ds(part_of * half, half)
        return lambda: remote(cots.at[r, at], cots.at[3, at], qs.at[4 + part_of], qr.at[4 + part_of], me.plane(3 - r))

    def lanes(h):
        return head_lanes(h, width)

    def project(h, _):
        lin[h] = dot(fb[...], wl[:, lanes(h)], NN)
        taps = vec[0:4, lanes(h)]
        conv = taps[0:1] * lin[h, HALO:, :]
        for k in range(1, 4):
            conv = conv + taps[k:k + 1] * lin[h, HALO - k:HALO - k + tokens, :] * mk[:, k:k + 1]
        conv = conv.astype(BF16)
        cv[h] = conv
        rl[h] = (dot(conv, rg[h], NN) + vecs[2:3, lanes(h)]).astype(BF16)
        il[h] = (dot(conv, ig[h], NN) + vecs[3:4, lanes(h)]).astype(BF16)
        return 0

    row = lax.broadcasted_iota(jnp.int32, (8, width), 0)

    def scan_head(h, _):
        rate = softplus(-vec[4:5, lanes(h)]) * -DECAY_SCALE

        def tile(i, carried):
            state, factor = carried
            at = rows(i, 16)
            start = mk[at, 0:1]
            keep = 1.0 - start
            decay = jnp.exp(sigmoid(rl[h, at, :].astype(F32)) * rate)
            a = keep * decay
            scale = (start + keep * jnp.sqrt(1.0 - decay * decay)) * sigmoid(il[h, at, :].astype(F32))
            b = scale * cv[h, at, :].astype(F32)
            for t in range(2):
                cum, run = tile_scan(a[8 * t:8 * t + 8], b[8 * t:8 * t + 8], row, False)
                run = run + cum * state
                cum = cum * factor
                here = pl.ds(pl.multiple_of(i * 16 + 8 * t, 8), 8)
                st[h, here, :] = run
                pst[h, here, :] = cum
                state, factor = run[7:8], cum[7:8]
            return state, factor

        state, factor = lax.fori_loop(
            0, tokens // 16, tile, (jnp.zeros((1, width), F32), jnp.ones((1, width), F32)), unroll=4
        )
        ends[0, 0:1, lanes(h)] = state
        ends[0, 1:2, lanes(h)] = factor
        return 0

    def end_copy(d):
        return lambda: remote(ends.at[0], ends.at[d], es.at[d - 1], er.at[d - 1], me.along(d))

    def branch(h, _):
        br[h] = dot(fb[HALO:], wb[:, lanes(h)], NN)
        return 0

    def finish(h, _):
        state = st[h] + pst[h] * sin[:, lanes(h)]
        st[h] = state
        pr[:, lanes(h)] = (state * gelu_only(br[h])).astype(BF16)
        return 0

    def project_out(j, _):
        at = rows(j, chunk)
        res[:, at] = x[:, at].astype(F32) + dot(pr[...], wo[:, at], NN)
        return 0

    def second_copy(r):
        return lambda: remote(s.at[0:tokens], s.at[r * tokens:(r + 1) * tokens], ss.at[r - 1], sr.at[r - 1], me.plane(r))

    def second_part(part_of, r):
        at, to = (pl.ds(q * tokens + part_of * half, half) for q in (r, 3))
        return lambda: remote(s.at[at], s.at[to], ss.at[2 + part_of], sr.at[2 + part_of], me.plane(3 - r))

    saved = [
        (wl, o_wl), (wb, o_wb), (wo, o_wo), (fb, o_fb), (lin, o_lin), (br, o_br), (cv, o_cv), (rl, o_rl), (il, o_il),
        (st, o_st), (pr, o_pr), (sin, o_sin), (mk, o_mk), (vec, o_vec), (vecs, o_vecs),
    ]
    saved = [pltpu.make_async_copy(a, b, osem.at[i]) for i, (a, b) in enumerate(saved)]
    grad_sum = PlaneSum(
        me, out, lambda r, part: sbuf.at[r, pl.ds(part * half, half)], lambda i: srecv.at[i], gs, gr, ()
    )
    def feed_ahead(r):
        at = rows(r, tokens)

        def hidden_of(j, _):
            here = rows(j, chunk)
            second = s[at]
            act, slope = gelu_both(dot(second, f[0, here, :], NT))
            up = dot(second, f[1, here, :], NT)
            h[at, here] = (act * up).astype(BF16)
            acts[at, here] = act
            slopes[at, here] = up * slope
            return 0

        lax.fori_loop(0, cols // chunk, hidden_of, 0, unroll=3)

    def feed_back(r):
        at = rows(r, tokens)

        def grads_of(j, _):
            here = rows(j, chunk)
            hg = dot(cots[r], f[2, here, :], NT)
            lg[at, here] = (hg * slopes[at, here]).astype(BF16)
            ug[at, here] = (hg * acts[at, here]).astype(BF16)
            return 0

        lax.fori_loop(0, cols // chunk, grads_of, 0, unroll=3)

        def back_of(j, _):
            here = rows(j, chunk)
            value = dot(lg[at], f[0, :, here], NN) + dot(ug[at], f[1, :, here], NN)
            sbuf[r, :, here] = value.astype(BF16)
            return 0

        lax.fori_loop(0, model // chunk, back_of, 0, unroll=4)

    def near_ahead(r, _):
        feed_ahead(r)
        return 0

    def near_back(r, _):
        feed_back(r)
        grad_sum.put(0, r == 1)
        grad_sum.put(2, r == 2)
        return 0

    def far_ahead(i, _):
        feed_ahead(3 - 3 * i)
        return 0

    def far_back(i, _):
        feed_back(3 - 3 * i)
        for piece in (1, 3):
            grad_sum.put(piece, i == 0)
        return 0

    def out_of(j, _):
        here = rows(j, chunk)
        for r in range(4):
            value = dot(h[r * tokens:(r + 1) * tokens], f[2, :, here], NN)
            if r:
                ybuf[r - 1, :, here] = value.astype(BF16)
            else:
                base[:, here] = res[:, here] + value
        return 0

    def feed_half(zz, core):
        return pl.ds(pl.multiple_of(zz * (2 * part) + core * part, part), part)

    def core_copy(m, zz):
        at = (m, zz)
        return lambda: remote(f.at[m, feed_half(zz, 1 - me.core)], fc.at[m, zz], ks.at[at], kr.at[at], me.sibling())

    def feed_wgrad(m, left):
        def body(i, _):
            here = rows(i, chunk)
            right = jnp.concatenate([cots[r, :, here] for r in range(4)], axis=0) if m == 2 else s[:, here]
            for j in range(cols // chunk):
                f[m, pl.ds(j * chunk, chunk), here] = dot(left[:, j * chunk:(j + 1) * chunk], right, TN).astype(BF16)
            return 0

        lax.fori_loop(0, model // chunk, body, 0)
        for zz in range(nz):
            out.go(core_copy(m, zz))

    last = [
        pltpu.make_async_copy(a, b, osem.at[15 + i])
        for i, (a, b) in enumerate((
            (ybuf, o_y), (base, o_base), (fc, o_wg), (rgrad, o_rgrad), (g2g, o_g2g),
        ))
    ]
    y_sum = PlaneSum(
        me, out, lambda r, part_of: ybuf.at[r - 1, pl.ds(part_of * half, half)], lambda i: yp.at[i // 2], ys, yr, ()
    )
    own_turned = pltpu.make_async_copy(
        turned.at[:, pl.ds(pl.multiple_of(shift, 32), 2 * part)], f.at[0:2, rows(z, 2 * part)], lsem.at[7]
    )
    g1, g2 = vecs[0:1, 0:model], vecs[1:2, 0:model]
    start_row = vecs[4:5, 0:nz * tokens]

    z_begin(0)
    for i, r in ((0, 1), (1, 2)):
        out.go(cot_whole(i, r, 0))
    for d in range(1, nz):
        out.arrived(vector(d, lambda: me.z_from(d)))
    vec[:, mine] = vecs[8:16, 0:own]
    for copy in local[2:] + more[1:]:
        copy.wait()
    z_begin(1)
    out.arrived(halo)
    fb[0:HALO] = rms(hx[...].astype(F32), g1).astype(BF16)
    z_step(0, 0)
    z_begin(2)
    z_step(0, 1)
    z_step(1, 0)
    z_step(0, 2)
    z_step(1, 1)
    z_step(1, 2)
    length = nz * tokens
    lane = lax.broadcasted_iota(jnp.int32, (1, length), 1)
    keep_row = 1.0 - start_row
    valid = keep_row
    lines, later_lines = [start_row, valid], []
    for k in range(1, 4):
        if k > 1:
            valid = valid * jnp.where(lane >= k - 1, pltpu.roll(keep_row, k - 1, 1), 0.0)
            lines.append(valid)
        later_lines.append(jnp.where(lane < length - k, pltpu.roll(valid, length - k, 1), 0.0))
    ms[...] = jnp.concatenate(lines + later_lines + [jnp.zeros_like(start_row)], axis=0)
    mk[...] = jnp.concatenate([ms[:, rows(z, tokens)], jnp.zeros((LANE - 8, tokens), F32)], axis=0).T
    relay(0, 1)
    relay(0, 0)
    z_step(2, 0)
    relay(0, 2)
    for i in range(2):
        local[i].wait()
        turned[i] = win[i].T
    own_turned.start()
    more[0].wait()
    fb[HALO:] = rms(x[...].astype(F32), g1).astype(BF16)
    z_begin(3)
    far(0, 1)
    relay(1, 1)
    z_step(2, 1)
    z_begin(4)
    relay(1, 0)
    far(0, 2)
    relay(1, 2)
    far(0, 0)
    z_step(3, 0)
    for i, r in ((0, 1), (1, 2)):
        out.go(cot_whole(i, r, 1))
    all_of(0)
    lax.fori_loop(0, heads // 3, project, 0, unroll=2)
    z_step(2, 2)
    relay(2, 0)
    lax.fori_loop(heads // 3, heads, project, 0, unroll=2)
    far(1, 1)
    far(1, 0)
    relay(2, 1)
    far(1, 2)
    lax.fori_loop(0, 2 * heads // 3, scan_head, 0)
    lax.fori_loop(2 * heads // 3, heads, scan_head, 0)
    all_of(1)
    for d in range(1, nz):
        out.go(end_copy(d), z + d < nz)
    relay(2, 2)
    far(2, 0)
    for part_of in range(2):
        out.arrived(cot_whole(0, 1, part_of))
    out.go(cot_part(0, 1))
    z_step(4, 0)
    lax.fori_loop(0, heads, branch, 0, unroll=2)
    for part_of in range(2):
        out.arrived(cot_whole(1, 2, part_of))
    out.go(cot_part(1, 2))
    far(2, 1)
    far(2, 2)
    for d in range(1, nz):
        out.arrived(end_copy(d), z >= d)
    incoming = jnp.zeros((1, lru), F32)
    for d in range(nz - 1, 0, -1):
        end = ends[d, 0:1, :] + ends[d, 1:2, :] * incoming
        incoming = jnp.where(d <= z, end, incoming)
    sin[...] = incoming

    all_of(2)
    lax.fori_loop(0, heads, finish, 0, unroll=2)
    lax.fori_loop(0, model // chunk, project_out, 0, unroll=4)
    s[0:tokens] = rms(res[...], g2).astype(BF16)
    for r in (1, 2):
        out.go(second_copy(r))
    for copy in saved:
        copy.start()
    z_step(3, 1)
    z_step(4, 1)
    z_step(3, 2)
    for part_of, r in ((0, 2), (1, 1)):
        out.arrived(cot_part(part_of, r))
    out.arrived(second_copy(2))
    out.go(second_part(1, 2))
    out.arrived(second_copy(1))
    out.go(second_part(0, 1))
    for hop in range(nz - 1):
        for right in (True, False):
            out.arrived(share(3, hop, right, False), has(hop, right))
    own_turned.wait()
    lax.fori_loop(1, 3, near_ahead, 0)
    z_step(4, 2)
    for hop in range(nz - 1):
        for right in (True, False):
            out.arrived(share(4, hop, right, False), has(hop, right))
    lax.fori_loop(1, 3, near_back, 0)
    for part_of, near in ((0, 2), (1, 1)):
        out.arrived(second_part(part_of, near))
    lax.fori_loop(0, 2, far_ahead, 0)
    lax.fori_loop(0, 2, far_back, 0)
    feeds.finish()
    feed_wgrad(0, lg)
    lax.fori_loop(0, model // chunk, out_of, 0, unroll=2)
    last[0].start()
    y_sum.put(0)
    y_sum.put(2)
    grad_sum.relay()
    feed_wgrad(1, ug)
    feed_wgrad(2, h)
    for zz in range(nz):
        out.arrived(core_copy(1, zz))
        fc[1, zz] = (fc[1, zz].astype(F32) + f[1, feed_half(zz, me.core), :].astype(F32)).astype(BF16)
    for part_of in range(2):
        at = pl.ds(part_of * half, half)
        y_sum.wait(2 * part_of)
        base[at, :] = base[at, :] + yp[part_of].astype(F32)
    last[1].start()
    for part_of in range(2):
        at = pl.ds(part_of * half, half)
        sown[at, :] = sbuf[0, at, :].astype(F32) + grad_sum.total(part_of)
    sg = sown[...]
    value = res[...]
    q = sg * g2
    inv = lax.rsqrt(jnp.mean(value * value, axis=-1, keepdims=True) + EPS)
    pull = jnp.mean(q * value, axis=-1, keepdims=True)
    rgrad[...] = cots[0].astype(F32) + (inv * q - value * (inv * inv * inv * pull))
    g2g[...] = jnp.sum(sg * value * inv, axis=0, keepdims=True)
    last[3].start()
    last[4].start()
    for zz in range(nz):
        out.arrived(core_copy(2, zz))
        fc[2, zz] = (fc[2, zz].astype(F32) + f[2, feed_half(zz, me.core), :].astype(F32)).astype(BF16)
    for zz in range(nz):
        out.arrived(core_copy(0, zz))
        fc[0, zz] = (fc[0, zz].astype(F32) + f[0, feed_half(zz, me.core), :].astype(F32)).astype(BF16)
    last[2].start()
    for copy in saved + last:
        copy.wait()
    out.finish()


def forward(nz, gain1, gain2, bias1, bias2, starts, taps, dlogit, x, rg, ig, cot, lw, bw, ow, fgate, fup, fdown):
    tokens, model = x.shape
    heads, width = rg.shape[0], rg.shape[1]
    lru = heads * width
    cols = fgate.shape[1]
    k = nz - 1
    hbm = pl.BlockSpec(memory_space=pl.ANY)
    by_head = (heads, tokens, width)
    saved = [
        ((model, lru), BF16), ((model, lru), BF16), ((lru, model), BF16), ((HALO + tokens, model), BF16),
        ((heads, HALO + tokens, width), F32), (by_head, F32), (by_head, BF16), (by_head, BF16), (by_head, BF16),
        (by_head, F32), ((tokens, lru), BF16), ((3, tokens, model), BF16), ((3, nz, cols // (2 * nz), model), BF16),
        ((tokens, model), F32), ((tokens, model), F32),
    ]
    kept = [((1, lru), F32), ((tokens, LANE), F32), ((8, lru), F32), ((1, model), F32), ((16, lru), F32)]
    sems = []
    for shape in ((5, k, 2), (3, 2 * k, 5), (2, 2 * k), (6,), (k,), (k,), (1,), (4,), (6,), (3, nz), (3,)):
        sems += [DMA(shape)] * 2
    return pl.pallas_call(
        functools.partial(forward_kernel, nz, heads),
        out_shape=tuple(jax.ShapeDtypeStruct(*a) for a in saved + kept),
        in_specs=[hbm] * 17,
        out_specs=[hbm] * (len(saved) + len(kept)),
        scratch_shapes=[VMEM(v.shape, v.dtype) for v in (gain1, gain2, bias1, bias2, starts, taps, dlogit)]
        + [VMEM(*a) for a in kept]
        + [
            VMEM((tokens, model), BF16), VMEM((heads, width, width), BF16), VMEM((heads, width, width), BF16),
            VMEM((tokens, model), F32), VMEM((tokens, model), F32), VMEM((model, lru), BF16), VMEM((model, lru), BF16), VMEM((lru, model), BF16), VMEM((3, cols, model), BF16),
            VMEM((4, tokens, model), BF16), VMEM((2, model, 256), BF16), VMEM((2, 256, model), BF16),
            VMEM((HALO + tokens, model), BF16), VMEM((heads, HALO + tokens, width), F32), VMEM(by_head, F32),
            VMEM(by_head, BF16), VMEM(by_head, BF16), VMEM(by_head, BF16), VMEM(by_head, F32), VMEM((tokens, lru), BF16),
            VMEM(by_head, F32), VMEM((nz, 8, lru), F32), VMEM((8, nz * tokens), F32), VMEM((HALO, model), BF16),
            VMEM((tokens, model), F32), VMEM((4 * tokens, model), BF16), VMEM((4 * tokens, cols), BF16),
            VMEM((4 * tokens, cols), BF16), VMEM((4 * tokens, cols), BF16), VMEM((3, tokens, model), BF16),
            VMEM((4, tokens, model), BF16), VMEM((6, tokens // 2, model), BF16), VMEM((tokens, model), F32), VMEM((3, nz, cols // (2 * nz), model), BF16),
            VMEM((4 * tokens, cols), F32), VMEM((4 * tokens, cols), F32),
            VMEM((2, tokens // 2, model), BF16),
            DMA((18,)), DMA((len(saved) + len(kept),)),
        ] + sems,
        compiler_params=pltpu.CompilerParams(collective_id=0, has_side_effects=True, vmem_limit_bytes=62 * 2**20),
        name="forward_and_feed",
    )(gain1, gain2, bias1, bias2, starts, taps, dlogit, x, rg, ig, cot, lw, bw, ow, fgate, fup, fdown)


def backward_kernel(nz, heads, i_sin, i_mk, i_vec, i_vecs, i_g2g,
                    i_rg, i_ig, i_rgrad, i_x, i_wl, i_wb, i_wo, i_fb, i_lin, i_br, i_cv, i_rl, i_il, i_st, i_pr, i_base, i_y, i_ffg,
                    wa, fa, ga, o_bout, o_igrad, o_osm, o_osmz,
                    sin, mk, vec, vecs, g2g, osm, osmz, rg, ig, rgrad, bout, igrad, x, wl, wb, wo, fb, lin, br, cv, rl, il, st, pr, yk,
                    rgb, turned, fl, rlg, ilg, bg, lgr, ends, hal,
                    g, wc, wp, wz, fin, fc, fz, ffin, gt, gc, gp, gz, gfin, sm, smz, yp, inc,
                    lsem, osem, wcs, wcr, wps, wpr, wzs, wzr, was, war, fzs, fzr, fas, far,
                    gcs, gcr, gps, gpr, gzs, gzr, gys, gyr, gas, gar, yps, ypr, s1s, s1r, s2s, s2r,
                    es, er, hs, hr):
    me = Place(nz)
    out = Sends()
    core, other, chip, z = me.core, 1 - me.core, me.chip, me.z
    tokens, model = x.shape
    lru = wl.shape[1]
    width = lru // heads
    own = lru // nz
    block = model // 8
    half_rows = block // 2
    part = fc.shape[2]
    k = nz - 1

    loads = dict(
        rgrad=(i_rgrad, rgrad), g2g=(i_g2g, g2g), vec=(i_vec, vec), mk=(i_mk, mk), sin=(i_sin, sin), vecs=(i_vecs, vecs),
        fc=(i_ffg, fc), pr=(i_pr, pr), wo=(i_wo, wo), br=(i_br, br), st=(i_st, st),
        rl=(i_rl, rl), fb=(i_fb, fb), wb=(i_wb, wb), cv=(i_cv, cv), il=(i_il, il), lin=(i_lin, lin), wl=(i_wl, wl),
        y0=(i_y.at[1, 0:tokens // 2], yk.at[0]), y1=(i_y.at[0, tokens // 2:tokens], yk.at[1]),
        x=(i_x, x), base=(i_base, bout), rg=(i_rg, rg), ig=(i_ig, ig),
    )
    loads = {name: pltpu.make_async_copy(a, b, lsem.at[i]) for i, (name, (a, b)) in enumerate(loads.items())}
    for copy in loads.values():
        copy.start()

    def need(*names):
        for name in names:
            loads[name].wait()

    greet([me.along(d) for d in range(1, nz)] + [me.plane(r) for r in (1, 2, 3)] + [me.sibling()])


    def lanes(h):
        return head_lanes(h, width)

    def chain(i, right, from_me):
        def make():
            dest = nz - 1 - i if right else i
            peer = (me.t, z + (1 if right else -1) if from_me else z)
            at = (int(right), i)
            return remote(fc.at[:, dest], fz.at[at], fzs.at[at], fzr.at[at], peer)
        return make

    def chain_begin(i, right):
        out.go(chain(i, right, True), z == 0 if right else z == nz - 1)

    def chain_step(slot):
        for right in (True, False):
            i = slot - (z - 1 if right else nz - 2 - z)
            dest = nz - 1 - i if right else i
            here = jnp.logical_and(i >= 0, dest >= z if right else dest <= z)
            here = jnp.logical_and(here, z >= 1 if right else z <= nz - 2)
            onward = jnp.logical_and(here, dest != z)
            out.arrived(chain(i, right, False), here)

            @pl.when(here)
            def _(right=right, dest=dest, i=i):
                for m in range(3):
                    fc[m, dest] = (fc[m, dest].astype(F32) + fz[int(right), i, m].astype(F32)).astype(BF16)

            out.go(chain(i, right, True), onward)

    def feed_place(c, kk, half):
        at = pl.multiple_of((2 * c + kk) * part, part)
        if half is None:
            return fa.at[:, pl.ds(at, part)]
        return fa.at[:, pl.ds(pl.multiple_of(at + half * (part // 2), part // 2), part // 2)]

    feed_gather = PlaneGather(me, out, feed_place, fas, far, (), None, first=lambda: ffin)
    feed_own = pltpu.make_async_copy(ffin, feed_place(chip, core, None), osem.at[3])

    def feed_total():
        ffin[...] = fc[:, z]
        feed_gather.begin()
        feed_own.start()

    def y_half(r, half):
        return i_y.at[r - 1, pl.ds(half * (tokens // 2), tokens // 2)]

    y_sum = PlaneSum(me, out, lambda r, half: yk.at[half], lambda i: yp.at[{1: 0, 3: 1, 4: 2, 5: 3}[i]], yps, ypr, (), source=y_half)
    made = [pltpu.make_async_copy(a, b, osem.at[5 + i]) for i, (a, b) in enumerate(((bout, o_bout), (igrad, o_igrad), (osm, o_osm), (osmz, o_osmz)))]

    slot_of = {2: 0, 1: 1, 0: 0}

    def core_of(m):
        at = pl.ds(pl.multiple_of(other * (model // 2), model // 2), model // 2)
        return lambda: remote(g.at[slot_of[m], at], wc.at[m], wcs.at[m], wcr.at[m], me.sibling())

    core_copies = [core_of(m) for m in range(3)]

    def block_of(m, r, half=None):
        start = me.chip_of(r) * block
        if half is None:
            return wc.at[m, pl.ds(pl.multiple_of(start, block), block)]
        return wc.at[m, pl.ds(pl.multiple_of(start + half * half_rows, half_rows), half_rows)]

    sums = [
        PlaneSum(me, out, lambda r, half, m=m: block_of(m, r, half), lambda i, m=m: wp.at[m, i], wps, wpr, (m,))
        for m in range(3)
    ]

    def core_sum(m):
        out.arrived(core_copies[m])

        def add(c, _):
            at = rows(c, block)
            mine = pl.ds(pl.multiple_of(core * (model // 2) + c * block, block), block)
            wc[m, at, :] = (wc[m, at, :].astype(F32) + g[slot_of[m], mine, :].astype(F32)).astype(BF16)
            return 0

        lax.fori_loop(0, 4, add, 0)
        sums[m].begin()

    def z_copy(m, d):
        return lambda: remote(
            wc.at[m, rows(chip, block), rows(me.along(d)[1], own)], wz.at[m, d - 1], wzs.at[m, d - 1], wzr.at[m, d - 1], me.along(d)
        )

    def plane_total(m):
        for half in range(2):
            at = pl.ds(pl.multiple_of(chip * block + half * half_rows, half_rows), half_rows)
            wc[m, at, :] = (wc[m, at, :].astype(F32) + sums[m].total(half)).astype(BF16)
        for d in range(1, nz):
            out.go(z_copy(m, d))

    def weight_place(m):
        def place(c, kk, half):
            start = (4 * kk + c) * block
            if half is None:
                return wa.at[m, pl.ds(pl.multiple_of(start, block), block)]
            return wa.at[m, pl.ds(pl.multiple_of(start + half * half_rows, half_rows), half_rows)]
        return place

    own_copies = [pltpu.make_async_copy(fin.at[m], weight_place(m)(chip, core, None), osem.at[m]) for m in range(3)]
    gathers = [
        PlaneGather(
            me, out, weight_place(m), was, war, (m,), None, first=lambda m=m: fin.at[m],
            joined=lambda kk, m=m: wa.at[m, rows(kk, 4 * block)], ready=own_copies[m].wait,
        )
        for m in range(3)
    ]

    def z_total(m):
        for d in range(1, nz):
            out.arrived(z_copy(m, d))
        total = wc[m, rows(chip, block), rows(z, own)].astype(F32)
        for d in range(k):
            total = total + wz[m, d].astype(F32)
        fin[m] = total.astype(BF16)
        gathers[m].begin()
        own_copies[m].start()

    gate_half = gt.shape[0] // 2
    gate_block = gt.shape[0] // 8
    gate_part = gate_block // nz

    def gate_core():
        at = pl.ds(pl.multiple_of(other * gate_half, gate_half), gate_half)
        return remote(gt.at[at], gc, gcs.at[0], gcr.at[0], me.sibling())

    def gate_rows(r, half):
        return gc.at[pl.ds(pl.multiple_of(me.chip_of(r) * gate_block + half * (gate_block // 2), gate_block // 2), gate_block // 2)]

    gate_sum = PlaneSum(me, out, gate_rows, lambda i: gp.at[i], gps, gpr, ())

    def gate_core_sum():
        out.arrived(gate_core)
        mine = pl.ds(pl.multiple_of(core * gate_half, gate_half), gate_half)
        gc[...] = (gc[...].astype(F32) + gt[mine, :].astype(F32)).astype(BF16)
        gate_sum.begin()

    def gate_cut(i):
        return pl.ds(pl.multiple_of(chip * gate_block + i * gate_part, gate_part), gate_part)

    def gate_along(d):
        return lambda: remote(gc.at[gate_cut(me.along(d)[1])], gz.at[d - 1], gzs.at[d - 1], gzr.at[d - 1], me.along(d))

    def gate_back(d, origin):
        return lambda: remote(
            gfin.at[rows(origin(), gate_part)], gfin.at[rows(origin(), gate_part)], gys.at[d - 1], gyr.at[d - 1], me.along(d)
        )

    def gate_total():
        for half in range(2):
            at = pl.ds(pl.multiple_of(chip * gate_block + half * (gate_block // 2), gate_block // 2), gate_block // 2)
            gc[at, :] = (gc[at, :].astype(F32) + gate_sum.total(half)).astype(BF16)
        for d in range(1, nz):
            out.go(gate_along(d))

    def gate_z_total():
        for d in range(1, nz):
            out.arrived(gate_along(d))
        total = gc[gate_cut(z), :].astype(F32)
        for d in range(k):
            total = total + gz[d].astype(F32)
        gfin[rows(z, gate_part), :] = total.astype(BF16)
        for d in range(1, nz):
            out.go(gate_back(d, lambda: z))

    def gate_place(c, kk, half):
        start = (4 * kk + c) * gate_block
        if half is None:
            return ga.at[pl.ds(pl.multiple_of(start, gate_block), gate_block)]
        return ga.at[pl.ds(pl.multiple_of(start + half * (gate_block // 2), gate_block // 2), gate_block // 2)]

    gate_own = pltpu.make_async_copy(gfin, gate_place(chip, core, None), osem.at[4])
    gate_gather = PlaneGather(
        me, out, gate_place, gas, gar, (), None, first=lambda: gfin, joined=lambda kk: ga.at[rows(kk, 4 * gate_block)],
        ready=gate_own.wait,
    )

    def gate_spread():
        for d in range(1, nz):
            out.arrived(gate_back(d, lambda: me.z_from(d)))
        gate_gather.begin()
        gate_own.start()

    def small_copy(i):
        peer = (me.sibling(), me.plane(1), me.plane(2))[i]
        return lambda: remote(sm.at[2 * i], sm.at[2 * i + 1], s1s.at[i], s1r.at[i], peer)

    def small_step(i):
        out.arrived(small_copy(i))
        sm[2 * i + 2] = sm[2 * i] + sm[2 * i + 1]
        if i < 2:
            out.go(small_copy(i + 1))
        else:
            smz[z] = sm[6]
            for d in range(1, nz):
                out.go(small_along(d, lambda: z))

    def small_along(d, origin):
        return lambda: remote(sm.at[6], smz.at[origin()], s2s.at[d - 1], s2r.at[d - 1], me.along(d))


    small = sm.at[0]
    row = lax.broadcasted_iota(jnp.int32, (8, width), 0)

    def branch_back(h, _):
        pg = dot(rgb[...], wo[lanes(h), :], NT)
        act, slope = gelu_both(br[h])
        bg[:, lanes(h)] = (pg * st[h] * slope).astype(BF16)
        fl[h, 0:tokens] = pg * act
        return 0

    def scan_head(h, _):
        rate = softplus(-vec[4:5, lanes(h)]) * -DECAY_SCALE

        def tile(j, carried):
            later, factor = carried
            i = tokens // 16 - 1 - j
            at = rows(i, 16)
            keep = 1.0 - mk[at, 0:1]
            a = keep * jnp.exp(sigmoid(rl[h, at, :].astype(F32)) * rate)
            sgrad = fl[h, at, :]
            b = a * sgrad
            for t in (1, 0):
                cum, run = tile_scan(a[8 * t:8 * t + 8], b[8 * t:8 * t + 8], row, True)
                run = run + cum * later
                cum = cum * factor
                here = pl.ds(pl.multiple_of(i * 16 + 8 * t, 8), 8)
                last = row == 7
                fl[h, here, :] = sgrad[8 * t:8 * t + 8] + jnp.where(last, later, pltpu.roll(run, 7, 0))
                br[h, here, :] = jnp.where(last, factor, pltpu.roll(cum, 7, 0))
                later, factor = run[0:1], cum[0:1]
            return later, factor

        later, factor = lax.fori_loop(
            0, tokens // 16, tile, (jnp.zeros((1, width), F32), jnp.ones((1, width), F32)), unroll=4
        )
        ends[0, 0:1, lanes(h)] = later
        ends[0, 1:2, lanes(h)] = factor
        return 0

    def end_copy(d):
        return lambda: remote(ends.at[0], ends.at[d], es.at[d - 1], er.at[d - 1], me.along(nz - d))

    def wgrad(slot, right):
        def body(h, _):
            g[slot, :, lanes(h)] = dot(turned[...], right[:, lanes(h)], NN).astype(BF16)
            return 0

        lax.fori_loop(0, heads, body, 0)

    def terms(h, _):
        raw = vec[4:5, lanes(h)]
        soft = softplus(-raw)
        later = inc[:, lanes(h)]

        def tile(i, carried):
            before, decays, rates, inputs = carried
            at = rows(i, 16)
            start = mk[at, 0:1]
            keep = 1.0 - start
            flow = fl[h, at, :] + br[h, at, :] * later
            state = st[h, at, :]
            first = lax.broadcasted_iota(jnp.int32, (16, width), 0) == 0
            earlier = jnp.where(first, before, pltpu.roll(state, 1, 0))
            sig = sigmoid(rl[h, at, :].astype(F32))
            gate = sigmoid(il[h, at, :].astype(F32))
            decay = jnp.exp(sig * (soft * -DECAY_SCALE))
            root = jnp.sqrt(1.0 - decay * decay)
            level = start + keep * root
            conv = cv[h, at, :].astype(F32)
            to_scale = flow * conv
            to_decay = keep * (flow * earlier - to_scale * gate * (decay / root))
            to_power = to_decay * decay * sig
            rate_grad = (to_power * (1.0 - sig) * (soft * -DECAY_SCALE)).astype(BF16)
            input_grad = (to_scale * level * gate * (1.0 - gate)).astype(BF16)
            rlg[h, at, :] = rate_grad
            ilg[h, at, :] = input_grad
            fl[h, at, :] = flow * level * gate
            rates = rates + rate_grad.astype(F32)
            inputs = inputs + input_grad.astype(F32)
            return state[15:16], decays + to_power, rates, inputs

        zero = jnp.zeros((16, width), F32)
        _, decays, rates, inputs = lax.fori_loop(0, tokens // 16, tile, (sin[:, lanes(h)], zero, zero, zero), unroll=4)
        small[4:5, lanes(h)] = jnp.sum(decays, axis=0, keepdims=True) * (DECAY_SCALE * sigmoid(-raw))
        small[5:6, lanes(h)] = jnp.sum(rates, axis=0, keepdims=True)
        small[6:7, lanes(h)] = jnp.sum(inputs, axis=0, keepdims=True)
        rate_out, input_out = rlg[h], ilg[h]
        gt[rows(h, width), :] = dot(cv[h], rate_out, TN).astype(BF16)
        gt[rows(heads + h, width), :] = dot(cv[h], input_out, TN).astype(BF16)
        path = (dot(rate_out, rg[h], NT) + dot(input_out, ig[h], NT)).astype(BF16)
        fl[h, 0:tokens] = fl[h, 0:tokens] + path.astype(F32)
        hal[0, h] = fl[h, 0:8]
        return 0

    def halo():
        return remote(hal.at[0], hal.at[1], hs.at[0], hr.at[0], me.along(nz - 1))

    def first_back(left, right):
        def body(j, _):
            at = rows(j, 256)
            igrad[:, at] += dot(left[...], right[at, :], NT)
            return 0

        lax.fori_loop(0, model // 256, body, 0)

    def filter_back(h, _):
        taps = vec[0:4, lanes(h)]
        fl[h, tokens:tokens + 8] = hal[1, h]
        value = taps[0:1] * fl[h, 0:tokens]
        small[0:1, lanes(h)] = jnp.sum(fl[h, 0:tokens] * lin[h, HALO:], axis=0, keepdims=True)
        for t in range(1, 4):
            value = value + taps[t:t + 1] * (fl[h, t:t + tokens] * mk[:, 3 + t:4 + t])
            small[t:t + 1, lanes(h)] = jnp.sum(
                fl[h, 0:tokens] * (lin[h, HALO - t:HALO - t + tokens] * mk[:, t:t + 1]), axis=0, keepdims=True
            )
        lgr[:, lanes(h)] = value.astype(BF16)
        return 0

    y_sum.put(1)
    y_sum.put(3)
    need("g2g", "vec", "mk", "sin", "vecs", "fc")
    chain_begin(0, False)
    for i in range(k):
        chain_begin(i, True)
    small[...] = jnp.zeros(small.shape, F32)
    for i in range(8):
        small[i:i + 1, lru:lru + LANE] = g2g[:, i * LANE:(i + 1) * LANE]
    need("rgrad")
    rgb[...] = rgrad[...].astype(BF16)
    need("pr")
    turned[...] = rgb[...].T
    wgrad(0, pr)
    out.go(core_copies[2])
    need("wo", "br", "st")
    lax.fori_loop(0, heads, branch_back, 0, unroll=3)
    core_sum(2)
    need("rl")
    lax.fori_loop(0, heads // 2, scan_head, 0)
    need("y0", "y1")
    y_sum.relay()
    lax.fori_loop(heads // 2, heads, scan_head, 0)
    for d in range(1, nz):
        out.go(end_copy(d), z >= d)
    chain_begin(1, False)
    need("fb")
    turned[...] = fb[HALO:, :].T
    wgrad(1, bg)
    out.go(core_copies[1])
    chain_step(0)
    for d in range(1, nz):
        out.arrived(end_copy(d), z + d < nz)
    incoming = jnp.zeros((1, lru), F32)
    for d in range(nz - 1, 0, -1):
        end = ends[d, 0:1, :] + ends[d, 1:2, :] * incoming
        incoming = jnp.where(d + z < nz, end, incoming)
    inc[...] = incoming
    core_sum(1)
    sums[2].relay()
    need("cv", "il", "rg", "ig")
    lax.fori_loop(0, heads // 3, terms, 0)
    chain_begin(2, False)
    lax.fori_loop(heads // 3, heads, terms, 0)
    chain_step(1)
    out.go(gate_core)
    sums[1].relay()
    gate_core_sum()
    need("wb")
    igrad[...] = jnp.zeros(igrad.shape, F32)
    first_back(bg, wb)
    gate_sum.relay()
    out.go(halo)
    chain_step(2)
    feed_total()
    need("base")
    for half in range(2):
        at = pl.ds(half * (tokens // 2), tokens // 2)
        y_sum.wait(4 + half)
        bout[at, :] = bout[at, :] + yp[2 + half].astype(F32)
    made[0].start()
    plane_total(2)
    need("lin")
    out.arrived(halo)
    lax.fori_loop(0, heads, filter_back, 0)
    out.sent(core_copies[2])
    wgrad(0, lgr)
    out.go(core_copies[0])
    core_sum(0)
    gate_total()
    need("wl")
    first_back(lgr, wl)
    need("x")
    value = x[...].astype(F32)
    fgrad = igrad[...]
    q = fgrad * vecs[0:1, 0:model]
    inv = lax.rsqrt(jnp.mean(value * value, axis=-1, keepdims=True) + EPS)
    pull = jnp.mean(q * value, axis=-1, keepdims=True)
    small[7:8, 0:model] = jnp.sum(fgrad * value * inv, axis=0, keepdims=True)
    igrad[...] = rgrad[...] + (inv * q - value * (inv * inv * inv * pull))
    made[1].start()
    out.go(small_copy(0))
    gate_z_total()
    sums[0].relay()
    small_step(0)
    feed_gather.relay()
    plane_total(1)
    small_step(1)
    plane_total(0)
    gate_spread()
    z_total(1)
    z_total(2)
    small_step(2)
    gate_gather.relay()
    z_total(0)
    gathers[2].relay()
    feed_gather.far()
    gathers[1].relay()
    gate_gather.far()
    gathers[0].relay()
    gathers[2].far()
    for d in range(1, nz):
        out.arrived(small_along(d, lambda: me.z_from(d)))
    total = smz[0]
    for i in range(1, nz):
        total = total + smz[i]
    osm[...] = total
    osmz[...] = osm[:, rows(z, own)]
    made[2].start()
    made[3].start()
    gathers[1].far()
    gathers[0].far()
    for gathered in [feed_gather, gathers[2], gathers[1], gate_gather, gathers[0]]:
        gathered.end()
    for copy in [feed_own] + made:
        copy.wait()
    out.finish()


def backward(nz, sin, mk, vec, vecs, g2g, rg, ig, rgrad, x, wl, wb, wo, fb, lin, br, cv, rl, il, st, pr, base, y, ffg):
    tokens, model = x.shape
    heads, width = rg.shape[0], rg.shape[1]
    lru = heads * width
    own = lru // nz
    part = ffg.shape[2]
    k = nz - 1
    block = model // 8
    gate_rows = 2 * lru
    gate_block = gate_rows // 8
    hbm = pl.BlockSpec(memory_space=pl.ANY)
    by_head = (heads, tokens, width)
    half = tokens // 2
    sems = []
    for shape in (
        (3,), (3, 6), (3, k), (3, 8), (2, k), (8,),
        (1,), (6,), (k,), (k,), (8,), (6,), (3,), (k,), (k,), (1,),
    ):
        sems += [DMA(shape)] * 2
    return pl.pallas_call(
        functools.partial(backward_kernel, nz, heads),
        out_shape=(
            jax.ShapeDtypeStruct((3, model, own), BF16),
            jax.ShapeDtypeStruct((3, 8 * part, model), BF16),
            jax.ShapeDtypeStruct((gate_rows, width), BF16),
            jax.ShapeDtypeStruct((tokens, model), F32),
            jax.ShapeDtypeStruct((tokens, model), F32),
            jax.ShapeDtypeStruct((8, lru + LANE), F32),
            jax.ShapeDtypeStruct((8, own), F32),
        ),
        in_specs=[hbm] * 23,
        out_specs=[hbm] * 7,
        scratch_shapes=[
            VMEM(sin.shape, F32), VMEM(mk.shape, F32), VMEM(vec.shape, F32), VMEM(vecs.shape, F32), VMEM(g2g.shape, F32),
            VMEM((8, lru + LANE), F32), VMEM((8, own), F32),
            VMEM((heads, width, width), BF16), VMEM((heads, width, width), BF16), VMEM((tokens, model), F32),
            VMEM((tokens, model), F32), VMEM((tokens, model), F32),
            VMEM((tokens, model), BF16), VMEM((model, lru), BF16), VMEM((model, lru), BF16), VMEM((lru, model), BF16),
            VMEM((HALO + tokens, model), BF16), VMEM((heads, HALO + tokens, width), F32), VMEM(by_head, F32),
            VMEM(by_head, BF16), VMEM(by_head, BF16), VMEM(by_head, BF16), VMEM(by_head, F32), VMEM((tokens, lru), BF16),
            VMEM((2, half, model), BF16),
            VMEM((tokens, model), BF16), VMEM((model, tokens), BF16), VMEM((heads, tokens + 8, width), F32),
            VMEM(by_head, BF16), VMEM(by_head, BF16), VMEM((tokens, lru), BF16), VMEM((tokens, lru), BF16),
            VMEM((nz, 8, lru), F32), VMEM((2, heads, 8, width), F32),
            VMEM((2, model, lru), BF16), VMEM((3, model // 2, lru), BF16), VMEM((3, 6, block // 2, lru), BF16),
            VMEM((3, k, block, own), BF16), VMEM((3, block, own), BF16),
            VMEM((3, nz, part, model), BF16), VMEM((2, k, 3, part, model), BF16), VMEM((3, part, model), BF16),
            VMEM((gate_rows, width), BF16), VMEM((gate_rows // 2, width), BF16), VMEM((6, gate_block // 2, width), BF16),
            VMEM((k, gate_block // nz, width), BF16), VMEM((gate_block, width), BF16),
            VMEM((7, 8, lru + LANE), F32), VMEM((nz, 8, lru + LANE), F32), VMEM((4, half, model), BF16), VMEM((1, lru), F32),
            DMA((25,)), DMA((9,)),
        ] + sems,
        compiler_params=pltpu.CompilerParams(collective_id=1, has_side_effects=True, vmem_limit_bytes=62 * 2**20),
        name="backward_and_sums",
    )(sin, mk, vec, vecs, g2g, rg, ig, rgrad, x, wl, wb, wo, fb, lin, br, cv, rl, il, st, pr, base, y, ffg)


def results_kernel(wa, fa, fd, ga, gb, bout, igrad, osm, osmz,
                   o_out, o_in, o_g1, o_branch, o_lru, o_taps, o_rate, o_input, o_rb, o_ib, o_decay, o_ow, o_g2, o_gate, o_up, o_down):
    model = bout.shape[1]

    @pl.when(pl.program_id(0) == 0)
    def _():
        o_taps[...] = osmz[0:4, :]
        o_decay[...] = osmz[4, :]
        lru = o_rb.shape[0]
        o_rb[...] = osm[5, 0:lru]
        o_ib[...] = osm[6, 0:lru]
        o_g1[...] = osm[7, 0:model]
        for i in range(8):
            o_g2[i * LANE:(i + 1) * LANE] = osm[i, lru:lru + LANE]

    o_out[...] = bout[...]
    o_in[...] = igrad[...]
    o_lru[...] = wa[0].astype(F32)
    o_branch[...] = wa[1].astype(F32)
    o_ow[...] = wa[2].T.astype(F32)
    o_rate[...] = ga[...].astype(F32)
    o_input[...] = gb[...].astype(F32)
    o_gate[...] = fa[0].T.astype(F32)
    o_up[...] = fa[1].T.astype(F32)
    o_down[...] = fd[0].astype(F32)


def results(wa, fa, ga, bout, igrad, osm, osmz):
    steps = 2
    model, own = wa.shape[1:]
    cols = fa.shape[1]
    gate_rows, width = ga.shape[0] // 2, ga.shape[1]
    lru = osm.shape[1] - LANE
    tokens = bout.shape[0]

    def whole(shape):
        return pl.BlockSpec(shape, lambda i: (0,) * len(shape))

    def down(count, lanes):
        return pl.BlockSpec((count // steps, lanes), lambda i: (i, 0))

    outs = [
        ((tokens, model), down(tokens, model)), ((tokens, model), down(tokens, model)), ((model,), whole((model,))),
        ((model, own), down(model, own)), ((model, own), down(model, own)), ((4, own), whole((4, own))),
        ((gate_rows, width), down(gate_rows, width)), ((gate_rows, width), down(gate_rows, width)),
        ((lru,), whole((lru,))), ((lru,), whole((lru,))), ((own,), whole((own,))),
        ((own, model), pl.BlockSpec((own, model // steps), lambda i: (0, i))), ((model,), whole((model,))),
        ((model, cols), down(model, cols)), ((model, cols), down(model, cols)), ((cols, model), down(cols, model)),
    ]
    return pl.pallas_call(
        results_kernel,
        grid=(steps,),
        out_shape=tuple(jax.ShapeDtypeStruct(shape, F32) for shape, _ in outs),
        in_specs=[
            pl.BlockSpec((3, model // steps, own), lambda i: (0, i, 0)),
            pl.BlockSpec((2, cols, model // steps), lambda i: (0, 0, i)),
            pl.BlockSpec((1, cols // steps, model), lambda i: (2, i, 0)),
            down(gate_rows, width),
            pl.BlockSpec((gate_rows // steps, width), lambda i: (i + steps, 0)),
            down(tokens, model), down(tokens, model), whole(osm.shape), whole(osmz.shape),
        ],
        out_specs=tuple(spec for _, spec in outs),
        compiler_params=pltpu.CompilerParams(vmem_limit_bytes=62 * 2**20),
        name="results",
    )(wa, fa, fa, ga, ga, bout, igrad, osm, osmz)


def local(
    nz,
    groups,
    block_input,
    doc_starts,
    first_gain,
    branch_weight,
    lru_weight,
    filter_taps,
    rate_gate,
    input_gate,
    rate_bias,
    input_bias,
    decay_logit,
    out_weight,
    second_gain,
    feed_gate,
    feed_up,
    feed_down,
    cotangent,
):
    model = block_input.shape[1]
    heads, width = rate_gate.shape[:2]
    lru = heads * width

    (wl, wb, wo, fb, lin, br, cv, rl, il, st, pr, y, ffg, base, rgrad, sin, mk, vec, g2g, vecs) = forward(
        nz, first_gain, second_gain, rate_bias, input_bias, doc_starts, filter_taps, decay_logit, block_input, rate_gate,
        input_gate, cotangent, lru_weight, branch_weight, out_weight,
        feed_gate, feed_up, feed_down,
    )
    sums = backward(
        nz, sin, mk, vec, vecs, g2g, rate_gate, input_gate, rgrad, block_input, wl, wb, wo, fb, lin, br, cv, rl, il, st, pr,
        base, y, ffg,
    )
    made = results(*sums)
    block_output, input_grad, *summed = made
    if groups > 1:
        same = [[8 * g + b for g in range(groups)] for b in range(8)]
        summed = lax.psum(tuple(summed), "tp", axis_index_groups=same)
    g1, branch, lru_grad, taps, rate, inputs, rb, ib, decay, ow, g2, gate, up, down = summed
    rate, inputs = rate.reshape(heads, width, width), inputs.reshape(heads, width, width)
    return (
        block_output, input_grad, g1, branch, lru_grad, taps, rate, inputs, rb, ib, decay, ow, g2,
        gate, up, down,
    )


def solution(mesh):
    by_rows = P(("tp", "dp"), None)
    by_cols = P(None, "dp")
    split = P("dp", None)
    return jax.shard_map(
        functools.partial(local, mesh.shape["dp"], mesh.shape["tp"] // 8),
        mesh=mesh,
        in_specs=(
            by_rows, P("tp"), P(), by_cols, by_cols, by_cols, P(), P(), P(), P(), P("dp"), split, P(), by_cols, by_cols,
            split, by_rows,
        ),
        out_specs=(
            by_rows, by_rows, P(), by_cols, by_cols, by_cols, P(), P(), P(), P(), P("dp"), split, P(), by_cols, by_cols,
            split,
        ),
        check_vma=False,
    )
```
